768 devices in a mesh: tile: 48 (over x, z), rep: 16 (over y, core).
Axes of the slice: x: 4, y: 8, z: 12, core: 2. Of those that a mesh axis runs over, the one named last changes fastest.
Arguments:
- amplitudes: bfloat16 [144, 960, 960], P('tile', None, 'rep'), may hold values from -6 to 6, as said below
- occ_energy: float32 [12], replicated, may hold values from -3 to -0.5
- vir_energy: float32 [960], replicated, may hold values from 0.5 to 4
- occ_irrep: int32 [12], replicated, may hold values from 0 to 7, as said below
- vir_irrep: int32 [960], replicated, may hold values from 0 to 7, as said below
- factors: bfloat16 [12, 960, 2048], P(None, 'rep'), as said below
Outputs:
- updated: float32 [12, 960, 12, 960], P(None, 'tile', None, 'rep')
The draws below stay inside these ranges and needn't reach their ends.
Inputs may be any that keep to these rules, and one draw needn't show every extreme that they name: `occ_irrep`: sorted: the occupied orbitals come in contiguous blocks of one irrep each, and every irrep occurs. `vir_irrep`: sorted: the virtual orbitals come in 8 contiguous blocks, one for each irrep. `amplitudes`: zero wherever occ_irrep[i] xor occ_irrep[j] xor vir_irrep[a] xor vir_irrep[b] is not 0. The auxiliary functions come in 8 contiguous blocks of one irrep each; factors[k, c, P] is zero unless occ_irrep[k] xor vir_irrep[c] equals the irrep of P.
All inputs are finite; a program needn't handle non-finite values.
Results may differ from the reference program's by a relative error of at most 0.0015.
Values may be sent and summed in bfloat16 or wider, within the bound.
A program may use at most 32 MiB of HBM per device.

```python
import jax
import jax.numpy as jnp

SO = 12
V = 960
NAUX = 2048


def block_labels(key, count):
    base = count // 8
    spread = base * 7 // 15
    first_key = jax.random.fold_in(key, 1)
    second_key = jax.random.fold_in(key, 2)
    offsets = jax.random.randint(first_key, (4,), -spread, spread + 1)
    block_sizes = jnp.stack([base + offsets, base - offsets], axis=1).reshape(8)
    block_sizes = jax.random.permutation(second_key, block_sizes)
    block_ends = jnp.cumsum(block_sizes)
    positions = jnp.arange(count, dtype=jnp.int32)
    return jnp.sum((positions[:, None] >= block_ends[None, :]).astype(jnp.int32), axis=1).astype(jnp.int32)


def orbital_labels(key):
    occ_key = jax.random.fold_in(key, 11)
    extra = jax.random.randint(occ_key, (SO - 8,), 0, 8)
    occ_labels = jnp.sort(jnp.concatenate([jnp.arange(8, dtype=jnp.int32), extra.astype(jnp.int32)]))
    vir_labels = block_labels(jax.random.fold_in(key, 12), V)
    aux_labels = block_labels(jax.random.fold_in(key, 13), NAUX)
    return (occ_labels, vir_labels, aux_labels)


def draw_occ_irrep(key, part):
    return orbital_labels(key)[0]


def draw_vir_irrep(key, part):
    return orbital_labels(key)[1]


def draw_amplitudes(key, part):
    occ_labels, vir_labels, aux_labels = orbital_labels(key)
    key = jax.random.fold_in(key, 21)
    values = jnp.clip(jax.random.normal(key, (SO * SO, V, V), jnp.float32), -6.0, 6.0)
    pair_labels = jnp.bitwise_xor(occ_labels[:, None], occ_labels[None, :]).reshape(SO * SO)
    allowed = jnp.bitwise_xor(jnp.bitwise_xor(pair_labels[:, None, None], vir_labels[None, :, None]), vir_labels[None, None, :]) == 0
    return jnp.where(allowed, values, jnp.float32(0.0)).astype(jnp.bfloat16)


def draw_factors(key, part):
    occ_labels, vir_labels, aux_labels = orbital_labels(key)
    key = jax.random.fold_in(key, 22)
    scale = (SO * V // 8) ** (-0.5)
    values = jnp.clip(jax.random.normal(key, (SO, V, NAUX), jnp.float32), -6.0, 6.0) * scale
    allowed = jnp.bitwise_xor(jnp.bitwise_xor(occ_labels[:, None, None], vir_labels[None, :, None]), aux_labels[None, None, :]) == 0
    return jnp.where(allowed, values, jnp.float32(0.0)).astype(jnp.bfloat16)


def setup_inputs(seed: int = 0) -> dict:
    arg_keys = jax.random.split(jax.random.key(seed), 7)
    amplitudes = draw_amplitudes(jax.random.fold_in(arg_keys[6], 71), 0)
    occ_energy = jnp.clip(jax.random.uniform(arg_keys[1], (SO,), jnp.float32, -3.0, -0.5), -3.0, -0.5)
    vir_energy = jnp.clip(jax.random.uniform(arg_keys[2], (V,), jnp.float32, 0.5, 4.0), 0.5, 4.0)
    occ_irrep = draw_occ_irrep(jax.random.fold_in(arg_keys[6], 71), 0)
    vir_irrep = draw_vir_irrep(jax.random.fold_in(arg_keys[6], 71), 0)
    factors = draw_factors(jax.random.fold_in(arg_keys[6], 71), 0)
    return dict(amplitudes=amplitudes, occ_energy=occ_energy, vir_energy=vir_energy, occ_irrep=occ_irrep, vir_irrep=vir_irrep, factors=factors)


def reference(amplitudes, occ_energy, vir_energy, occ_irrep, vir_irrep, factors):
    relaid = amplitudes.reshape(SO, SO, V, V).transpose(0, 2, 1, 3)
    matrix = relaid.reshape(SO * V, SO * V)
    factor_rows = factors.reshape(SO * V, NAUX)
    inter = jnp.dot(matrix, factor_rows, preferred_element_type=jnp.float32).astype(jnp.bfloat16)
    cycle = jnp.einsum("mq,nq->mn", inter, factor_rows, preferred_element_type=jnp.float32).reshape(SO, V, SO, V)
    denom = occ_energy[:, None, None, None] - vir_energy[None, :, None, None] + occ_energy[None, None, :, None] - vir_energy[None, None, None, :]
    symmetry = jnp.bitwise_xor(jnp.bitwise_xor(occ_irrep[:, None, None, None], vir_irrep[None, :, None, None]), jnp.bitwise_xor(occ_irrep[None, None, :, None], vir_irrep[None, None, None, :]))
    return jnp.where(symmetry == 0, relaid.astype(jnp.float32) + cycle / denom, jnp.float32(0.0))
```

```python
import functools

import jax
import jax.numpy as jnp
from jax import lax
from jax.experimental import pallas as pl
from jax.experimental.pallas import tpu as pltpu
from jax.sharding import PartitionSpec as P

X, Z, R = 4, 12, 16
OCC = 12
SLAB = 20
WIDTH = 60
PAIRS = 3
GROUPS = 4
FOLD = SLAB * Z
NAUX = 2048
WINDOW = 384
COLS = GROUPS * 256
ROWS = 64
MAIN = 16
REM = SLAB - MAIN
F32, BF16, I32 = jnp.float32, jnp.bfloat16, jnp.int32


def dense_path(amplitudes, occ_energy, vir_energy, occ_irrep, vir_irrep, factors):
    tile_count = lax.axis_size("tile")
    occ_count = occ_energy.shape[0]
    vir_count = vir_energy.shape[0]
    first_width = vir_count // tile_count
    second_width = amplitudes.shape[2]
    relaid = lax.all_to_all(amplitudes, "tile", split_axis=1, concat_axis=0, tiled=True)
    relaid = relaid.reshape(occ_count, occ_count, first_width, second_width).transpose(0, 2, 1, 3)
    matrix = relaid.reshape(occ_count * first_width, occ_count * second_width)
    factor_rows = factors.reshape(occ_count * second_width, factors.shape[2])
    partial_value = jnp.dot(matrix, factor_rows, preferred_element_type=jnp.float32)
    inter = lax.psum(partial_value.astype(jnp.bfloat16), "rep")
    cycle = jnp.einsum("mq,nq->mn", inter, factor_rows, preferred_element_type=jnp.float32)
    cycle = cycle.reshape(occ_count, first_width, occ_count, second_width)
    tile_start = lax.axis_index("tile") * first_width
    rep_start = lax.axis_index("rep") * second_width
    vir_first = lax.dynamic_slice_in_dim(vir_energy, tile_start, first_width)
    vir_second = lax.dynamic_slice_in_dim(vir_energy, rep_start, second_width)
    irrep_first = lax.dynamic_slice_in_dim(vir_irrep, tile_start, first_width)
    irrep_second = lax.dynamic_slice_in_dim(vir_irrep, rep_start, second_width)
    denom = (
        occ_energy[:, None, None, None]
        - vir_first[None, :, None, None]
        + occ_energy[None, None, :, None]
        - vir_second[None, None, None, :]
    )
    symmetry = jnp.bitwise_xor(
        jnp.bitwise_xor(occ_irrep[:, None, None, None], irrep_first[None, :, None, None]),
        jnp.bitwise_xor(occ_irrep[None, None, :, None], irrep_second[None, None, None, :]),
    )
    return jnp.where(symmetry == 0, relaid.astype(jnp.float32) + cycle / denom, jnp.float32(0.0))


def lane_iota(rows):
    return lax.broadcasted_iota(I32, (rows, 128), 1)


def exchange_kernel(
    amp_hbm, fac_hbm, vir_irrep, vir_energy, occ_irrep, occ_energy,
    m_out, inter_out, ff_out, row_lab, row_en, col_lab, col_occ, col_vir, flag_out,
    amp_v, fac_v, pkf, pk, gbuf, part, rsbuf, inter_s, flag_s,
    load_sem, zsend, zrecv, xsend, xrecv, rsend, rrecv, gsend, grecv,
):
    t = lax.axis_index("tile")
    r = lax.axis_index("rep")
    x = t // Z
    z = t % Z

    loads = [pltpu.make_async_copy(amp_hbm.at[j], amp_v.at[j], load_sem.at[j]) for j in range(PAIRS)]
    loads.append(pltpu.make_async_copy(fac_hbm, fac_v, load_sem.at[PAIRS]))
    for copy in loads:
        copy.start()

    barrier = pltpu.get_barrier_semaphore()

    @pl.loop(1, Z)
    def _(d):
        pl.semaphore_signal(barrier, inc=1, device_id=(x * Z + (z + d) % Z, r))

    @pl.loop(1, X)
    def _(d):
        pl.semaphore_signal(barrier, inc=1, device_id=(((x + d) % X) * Z + z, r))

    @pl.loop(1, R)
    def _(d):
        pl.semaphore_signal(barrier, inc=1, device_id=(t, (r + d) % R))

    pkf[...] = jnp.zeros_like(pkf)
    row = lax.broadcasted_iota(I32, (FOLD, 1), 0)
    rem_row = row - MAIN * Z
    target = jnp.where(
        row < MAIN * Z,
        SLAB * (row >> 4) + (row & 15),
        SLAB * (rem_row >> 2) + MAIN + (rem_row & 3),
    )
    lane = lax.broadcasted_iota(I32, (1, X * FOLD), 1)
    folded_lane = lane
    for n in range(1, X):
        folded_lane = folded_lane - jnp.where(lane >= n * FOLD, FOLD, 0)
    pick = jnp.where(target == folded_lane, 1.0, 0.0).astype(BF16)
    for j in range(PAIRS):
        loads[j].wait()
        folded = lax.dot_general(pick, amp_v[j], (((1,), (1,)), ((), ())), preferred_element_type=F32)
        pkf[:, 64 * j : 64 * j + WIDTH] = folded
    for n in range(Z):
        pk[n, :, 0:128] = pkf[MAIN * n : MAIN * (n + 1), 0:128].astype(BF16)
        base = MAIN * Z + REM * n
        rem_rows = [pkf[base : base + REM, 128 * (j // 2) : 128 * (j // 2) + 128] for j in range(PAIRS)]
        rem_rows = [rem_rows[0], pltpu.roll(rem_rows[1], 64, 1), rem_rows[2]]
        rem = jnp.concatenate(rem_rows + [jnp.zeros((MAIN - PAIRS * REM, 128), F32)], axis=0)
        rem = jnp.where(lane_iota(MAIN) < 64, rem, 0.0)
        right = pkf[MAIN * n : MAIN * (n + 1), 128:256] + pltpu.roll(rem, 64, 1)
        pk[n, :, 128:256] = right.astype(BF16)

    pl.semaphore_wait(barrier, Z - 1 + X - 1 + R - 1)

    def z_send(d):
        to = (z + d) % Z
        pltpu.make_async_remote_copy(
            src_ref=pk.at[to], dst_ref=gbuf.at[t], send_sem=zsend, recv_sem=zrecv.at[z],
            device_id=(x * Z + to, r),
        ).start()

    def x_send(slot, d):
        pltpu.make_async_remote_copy(
            src_ref=gbuf.at[slot], dst_ref=gbuf.at[slot], send_sem=xsend, recv_sem=xrecv.at[x],
            device_id=(((x + d) % X) * Z + z, r),
        ).start()

    gbuf[t] = pk[z]

    @pl.loop(0, Z - 1)
    def _(n):
        near = Z // 2 - (n + 1) // 2
        z_send(jnp.where(n % 2 == 0, near, Z - near))

    for d in range(1, X):
        x_send(t, d)

    vlane = lax.broadcasted_iota(I32, (24, X * FOLD), 1)
    vsub = lax.broadcasted_iota(I32, (24, X * FOLD), 0)
    mine = vlane == SLAB * t + vsub
    va_lab = jnp.sum(jnp.where(mine, vir_irrep[...].astype(F32), 0.0), axis=1, keepdims=True).astype(I32)
    va_en = jnp.sum(jnp.where(mine, vir_energy[...], 0.0), axis=1, keepdims=True)
    for i in range(OCC):
        n, i3 = i // PAIRS, i % PAIRS
        lab = jnp.broadcast_to(jnp.bitwise_xor(va_lab, occ_irrep[i]), (24, 128))
        en = jnp.broadcast_to(occ_energy[i] - va_en, (24, 128))
        row_lab[n, MAIN * i3 : MAIN * (i3 + 1), :] = lab[:MAIN]
        row_lab[n, MAIN * PAIRS + REM * i3 : MAIN * PAIRS + REM * (i3 + 1), :] = lab[MAIN:SLAB]
        row_en[n, MAIN * i3 : MAIN * (i3 + 1), :] = en[:MAIN]
        row_en[n, MAIN * PAIRS + REM * i3 : MAIN * PAIRS + REM * (i3 + 1), :] = en[MAIN:SLAB]
    for n in range(X):
        row_lab[n, ROWS - REM : ROWS, :] = jnp.full((REM, 128), -1, I32)
        row_en[n, ROWS - REM : ROWS, :] = jnp.zeros((REM, 128), F32)

    pad = jnp.zeros((8, 1024 - X * FOLD), F32)
    shift = (1024 - WIDTH * r) % 1024
    lane8 = lane_iota(8)
    half = lane8 & 63

    def columns(values):
        whole = jnp.concatenate([jnp.broadcast_to(values, (8, X * FOLD)), pad], axis=1)
        mine = jnp.where(lane8 < WIDTH, pltpu.roll(whole, shift, 1)[:, :128], 0.0)
        return mine + pltpu.roll(mine, 64, 1)

    vb_lab = columns(vir_irrep[...].astype(F32)).astype(I32)
    vb_en = columns(vir_energy[...])
    for g in range(GROUPS):
        for h in range(2):
            first = PAIRS * g + 2 * h
            second = min(first + 1, PAIRS * g + 2)
            cols = slice(256 * g + 128 * h, 256 * g + 128 * h + 128)
            lab = jnp.bitwise_xor(vb_lab, jnp.where(lane8 < 64, occ_irrep[first], occ_irrep[second]))
            valid = (half < WIDTH) & ((lane8 < 64) | (h == 0))
            col_lab[:, cols] = jnp.where(valid, lab, -2)
            col_occ[:, cols] = jnp.where(lane8 < 64, occ_energy[first], occ_energy[second])
            col_vir[:, cols] = vb_en

    @pl.loop(0, Z - 1)
    def _(n):
        near = n // 2 + 1
        slot = x * Z + (z + jnp.where(n % 2 == 0, near, Z - near)) % Z
        pltpu.make_async_copy(gbuf.at[slot], gbuf.at[slot], zrecv.at[slot - x * Z]).wait()
        for d in range(1, X):
            x_send(slot, d)

    loads[PAIRS].wait()
    zero4 = jnp.zeros((64 - WIDTH, WINDOW), F32)
    for g in range(GROUPS):
        ff_out[256 * g + 192 : 256 * (g + 1), :] = jnp.zeros((64, WINDOW), BF16)
    for k in range(OCC):
        base = 256 * (k // PAIRS) + 64 * (k % PAIRS)
        total = fac_v[k, :, 0:WINDOW].astype(F32)
        for n in range(1, NAUX // WINDOW):
            total = total + fac_v[k, :, WINDOW * n : WINDOW * (n + 1)].astype(F32)
        last = NAUX // WINDOW * WINDOW
        tail = fac_v[k, :, last:NAUX].astype(F32)
        total = total + jnp.concatenate([tail, jnp.zeros((WIDTH, WINDOW - NAUX + last), F32)], axis=1)
        ff_out[base : base + 64, :] = jnp.concatenate([total, zero4], axis=0).astype(BF16)

    vlane8 = lax.broadcasted_iota(I32, (8, X * FOLD), 1)
    vsub8 = lax.broadcasted_iota(I32, (8, X * FOLD), 0)
    first_lab = jnp.sum(
        jnp.where(vlane8 == WIDTH * r + vsub8, vir_irrep[...].astype(F32), 0.0), axis=1, keepdims=True
    ).astype(I32)
    seen = jnp.zeros((8, NAUX), I32)
    for k in range(OCC):
        bit = jnp.left_shift(jnp.int32(1), jnp.bitwise_xor(first_lab, occ_irrep[k]))
        seen = jnp.bitwise_or(seen, jnp.where(fac_v[k, 0:16, :].astype(F32)[0:8] != 0.0, bit, 0))
    for n in (4, 2, 1):
        seen = jnp.bitwise_or(seen, pltpu.roll(seen, n, 0))
    seen = seen[0:1]
    bad = jnp.zeros((1, 1), F32)
    covered = jnp.zeros((1, 1), F32)
    for h in range(8):
        aux_size = jnp.sum(jnp.where(seen == (1 << h), 1.0, 0.0), axis=1, keepdims=True)
        vir_size = jnp.sum(jnp.where(vir_irrep[...] == h, 1.0, 0.0), axis=1, keepdims=True)
        covered = covered + aux_size
        bad = bad + jnp.where(aux_size > WINDOW, 1.0, 0.0) + jnp.where(vir_size > FOLD, 1.0, 0.0)
    bad = bad + jnp.where(covered != NAUX, 1.0, 0.0)
    flag_s[...] = jnp.broadcast_to(jnp.where(bad > 0.0, 1.0, 0.0), (8, 128))

    @pl.loop(0, X)
    def _(d):
        xs = (x + d) % X

        @pl.when(d > 0)
        def _():
            block = gbuf.at[pl.ds(xs * Z, Z)]
            pltpu.make_async_copy(block, block, xrecv.at[xs]).wait()

        for g in range(GROUPS):
            blocks = [gbuf[xs * Z + GROUPS * i3 + g].astype(F32) for i3 in range(PAIRS)]
            cols = slice(256 * g, 256 * (g + 1))
            clab = col_lab[0:1, cols]
            for i3 in range(PAIRS):
                rows = slice(MAIN * i3, MAIN * (i3 + 1))
                rlab = jnp.concatenate([row_lab[xs, rows, :]] * 2, axis=1)
                m_out[xs, rows, cols] = jnp.where(rlab == clab, blocks[i3], 0.0).astype(BF16)
            pieces = []
            for j in range(PAIRS):
                rem = [b[REM * j : REM * (j + 1), 128:256] for b in blocks]
                pieces.append(jnp.concatenate(rem + [jnp.zeros((REM, 128), F32)], axis=0))
            low = lane_iota(MAIN) < 64
            left = jnp.where(low, pltpu.roll(pieces[0], 64, 1), pieces[1])
            right = jnp.where(low, pltpu.roll(pieces[2], 64, 1), 0.0)
            rows = slice(MAIN * PAIRS, ROWS)
            rlab = jnp.concatenate([row_lab[xs, rows, :]] * 2, axis=1)
            whole = jnp.concatenate([left, right], axis=1)
            m_out[xs, rows, cols] = jnp.where(rlab == clab, whole, 0.0).astype(BF16)
        res = jnp.dot(m_out[xs], ff_out[...], preferred_element_type=F32)
        sub = lax.broadcasted_iota(I32, (ROWS, WINDOW), 0)
        res = jnp.where(sub < ROWS - REM, res, flag_s[0:1, 0:1]).astype(BF16)
        for c in range(4):
            e = 4 * xs + c
            part[e] = res[MAIN * c : MAIN * (c + 1)]

            @pl.when(e != r)
            def _():
                pltpu.make_async_remote_copy(
                    src_ref=part.at[e], dst_ref=rsbuf.at[r], send_sem=rsend, recv_sem=rrecv,
                    device_id=(t, e),
                ).start()

    rsbuf[r] = part[r]
    rest = rsbuf.at[pl.ds(0, R - 1)]
    pltpu.make_async_copy(rest, rest, rrecv).wait()
    total = rsbuf[0].astype(F32)
    for n in range(1, R):
        total = total + rsbuf[n].astype(F32)
    inter_s[r] = total.astype(BF16)

    @pl.loop(1, R)
    def _(d):
        pltpu.make_async_remote_copy(
            src_ref=inter_s.at[r], dst_ref=inter_s.at[r], send_sem=gsend, recv_sem=grecv,
            device_id=(t, (r + d) % R),
        ).start()

    rest = inter_s.at[pl.ds(0, R - 1)]
    pltpu.make_async_copy(rest, rest, grecv).wait()
    inter_out[...] = inter_s[...]
    flag_out[...] = inter_s[3].astype(F32)[8:16, 0:128]

    sent = pk.at[pl.ds(0, Z - 1)]
    pltpu.make_async_copy(sent, sent, zsend).wait()
    sent = gbuf.at[pl.ds(0, Z * (X - 1))]
    pltpu.make_async_copy(sent, sent, xsend).wait()
    sent = part.at[pl.ds(0, R - 1)]
    pltpu.make_async_copy(sent, sent, rsend).wait()
    sent = inter_s.at[pl.ds(0, R - 1)]
    pltpu.make_async_copy(sent, sent, gsend).wait()


def exchange(amplitudes, occ_energy, vir_energy, occ_irrep, vir_irrep, factors):
    vmem = pl.BlockSpec(memory_space=pltpu.VMEM)
    smem = pl.BlockSpec(memory_space=pltpu.SMEM)
    hbm = pl.BlockSpec(memory_space=pl.ANY)
    shapes = [
        ((X, ROWS, COLS), BF16),
        ((R, MAIN, WINDOW), BF16),
        ((COLS, WINDOW), BF16),
        ((X, ROWS, 128), I32),
        ((X, ROWS, 128), F32),
        ((8, COLS), I32),
        ((8, COLS), F32),
        ((8, COLS), F32),
        ((8, 128), F32),
    ]
    dma = pltpu.SemaphoreType.DMA
    return pl.pallas_call(
        exchange_kernel,
        out_shape=[jax.ShapeDtypeStruct(*s) for s in shapes],
        in_specs=[hbm, hbm, vmem, vmem, smem, smem],
        out_specs=[vmem] * len(shapes),
        scratch_shapes=[
            pltpu.VMEM((PAIRS, WIDTH, X * FOLD), BF16),
            pltpu.VMEM((OCC, WIDTH, NAUX), BF16),
            pltpu.VMEM((FOLD, 256), F32),
            pltpu.VMEM((Z, MAIN, 256), BF16),
            pltpu.VMEM((X * Z, MAIN, 256), BF16),
            pltpu.VMEM((R, MAIN, WINDOW), BF16),
            pltpu.VMEM((R, MAIN, WINDOW), BF16),
            pltpu.VMEM((R, MAIN, WINDOW), BF16),
            pltpu.VMEM((8, 128), F32),
            dma((PAIRS + 1,)), dma, dma((Z,)), dma, dma((X,)), dma, dma, dma, dma,
        ],
        compiler_params=pltpu.CompilerParams(
            collective_id=0, has_side_effects=True, vmem_limit_bytes=32 * 1024 * 1024
        ),
        name="exchange",
    )(
        amplitudes.transpose(0, 2, 1), factors, vir_irrep.reshape(1, -1), vir_energy.reshape(1, -1),
        occ_irrep, occ_energy,
    )


def finish_kernel(m_ref, inter_ref, ff_ref, row_lab, row_en, col_lab, col_occ, col_vir, out, res):
    for n in range(X):
        inter = jnp.concatenate([inter_ref[4 * n + c] for c in range(4)], axis=0)
        cycle = lax.dot_general(inter, ff_ref[...], (((1,), (1,)), ((), ())), preferred_element_type=F32)
        for g in range(GROUPS):
            cols = slice(256 * g, 256 * (g + 1))
            rlab = jnp.concatenate([row_lab[n]] * 2, axis=1)
            ren = jnp.concatenate([row_en[n]] * 2, axis=1)
            denom = ren + col_occ[0:1, cols] - col_vir[0:1, cols]
            value = m_ref[n, :, cols].astype(F32) + cycle[:, cols] / denom
            res[:, cols] = jnp.where(rlab == col_lab[0:1, cols], value, 0.0)
        for i3 in range(PAIRS):
            i = PAIRS * n + i3
            for j in range(OCC):
                base = 256 * (j // PAIRS) + 64 * (j % PAIRS)
                out[i, j, 0:MAIN, :] = res[MAIN * i3 : MAIN * (i3 + 1), base : base + WIDTH]
                rem = MAIN * PAIRS + REM * i3
                out[i, j, MAIN:SLAB, :] = res[rem : rem + REM, base : base + WIDTH]


def finish(*operands):
    vmem = pl.BlockSpec(memory_space=pltpu.VMEM)
    out = pl.pallas_call(
        finish_kernel,
        out_shape=jax.ShapeDtypeStruct((OCC, OCC, SLAB, WIDTH), F32),
        in_specs=[vmem] * 8,
        out_specs=vmem,
        scratch_shapes=[pltpu.VMEM((ROWS, COLS), F32)],
        compiler_params=pltpu.CompilerParams(vmem_limit_bytes=32 * 1024 * 1024),
        name="finish",
    )(*operands)
    return out.transpose(0, 2, 1, 3)


def per_device(*arguments):
    *operands, flag = exchange(*arguments)
    return lax.cond(flag[7, 0] == 0.0, lambda: finish(*operands), lambda: dense_path(*arguments))


def solution(mesh):
    return jax.shard_map(
        per_device,
        mesh=mesh,
        in_specs=(P("tile", None, "rep"), P(), P(), P(), P(), P(None, "rep", None)),
        out_specs=P(None, "tile", None, "rep"),
        check_vma=False,
    )
```

```python
import functools

import jax
import jax.numpy as jnp
from jax import lax
from jax.experimental import pallas as pl
from jax.experimental.pallas import tpu as pltpu
from jax.sharding import PartitionSpec as P

X, Z, R = 4, 12, 16
OCC = 12
SLAB = 20
WIDTH = 60
PAIRS = 3
GROUPS = 4
FOLD = SLAB * Z
NAUX = 2048
WINDOW = 384
COLS = GROUPS * 256
ROWS = 64
MAIN = 16
REM = SLAB - MAIN
F32, BF16, I32 = jnp.float32, jnp.bfloat16, jnp.int32


def dense_path(amplitudes, occ_energy, vir_energy, occ_irrep, vir_irrep, factors):
    tile_count = lax.axis_size("tile")
    occ_count = occ_energy.shape[0]
    vir_count = vir_energy.shape[0]
    first_width = vir_count // tile_count
    second_width = amplitudes.shape[2]
    relaid = lax.all_to_all(amplitudes, "tile", split_axis=1, concat_axis=0, tiled=True)
    relaid = relaid.reshape(occ_count, occ_count, first_width, second_width).transpose(0, 2, 1, 3)
    matrix = relaid.reshape(occ_count * first_width, occ_count * second_width)
    factor_rows = factors.reshape(occ_count * second_width, factors.shape[2])
    partial_value = jnp.dot(matrix, factor_rows, preferred_element_type=jnp.float32)
    inter = lax.psum(partial_value.astype(jnp.bfloat16), "rep")
    cycle = jnp.einsum("mq,nq->mn", inter, factor_rows, preferred_element_type=jnp.float32)
    cycle = cycle.reshape(occ_count, first_width, occ_count, second_width)
    tile_start = lax.axis_index("tile") * first_width
    rep_start = lax.axis_index("rep") * second_width
    vir_first = lax.dynamic_slice_in_dim(vir_energy, tile_start, first_width)
    vir_second = lax.dynamic_slice_in_dim(vir_energy, rep_start, second_width)
    irrep_first = lax.dynamic_slice_in_dim(vir_irrep, tile_start, first_width)
    irrep_second = lax.dynamic_slice_in_dim(vir_irrep, rep_start, second_width)
    denom = (
        occ_energy[:, None, None, None]
        - vir_first[None, :, None, None]
        + occ_energy[None, None, :, None]
        - vir_second[None, None, None, :]
    )
    symmetry = jnp.bitwise_xor(
        jnp.bitwise_xor(occ_irrep[:, None, None, None], irrep_first[None, :, None, None]),
        jnp.bitwise_xor(occ_irrep[None, None, :, None], irrep_second[None, None, None, :]),
    )
    return jnp.where(symmetry == 0, relaid.astype(jnp.float32) + cycle / denom, jnp.float32(0.0))


def lane_iota(rows):
    return lax.broadcasted_iota(I32, (rows, 128), 1)


def assemble(dst, blocks, rows, bcol):
    low = lane_iota(MAIN) < 64
    for g in range(GROUPS):
        cols = slice(256 * g, 256 * (g + 1))
        kept = [
            jnp.where(rows[i3] == bcol[g], blocks[GROUPS * i3 + g].astype(F32), 0.0) for i3 in range(PAIRS)
        ]
        for i3 in range(PAIRS):
            dst[MAIN * i3 : MAIN * (i3 + 1), cols] = kept[i3].astype(BF16)
        pieces = []
        for j in range(PAIRS):
            rem = [v[REM * j : REM * (j + 1), 128:256] for v in kept]
            pieces.append(jnp.concatenate(rem + [jnp.zeros((REM, 128), F32)], axis=0))
        left = jnp.where(low, pltpu.roll(pieces[0], 64, 1), pieces[1])
        right = jnp.where(low, pltpu.roll(pieces[2], 64, 1), 0.0)
        dst[MAIN * PAIRS : ROWS, cols] = jnp.concatenate([left, right], axis=1).astype(BF16)


def block_rows(lab, occ):
    main = jnp.broadcast_to(jnp.bitwise_xor(lab[:MAIN], occ), (MAIN, 128))
    rem = jnp.bitwise_xor(lab[MAIN:SLAB], occ)
    rem = jnp.concatenate([rem] * PAIRS + [jnp.full((MAIN - PAIRS * REM, 1), -1, I32)], axis=0)
    right = jnp.where(lane_iota(MAIN) < 64, main, jnp.broadcast_to(rem, (MAIN, 128)))
    return jnp.concatenate([main, right], axis=1)


def exchange_kernel(
    amp_hbm, fac_hbm, vir_irrep, vir_energy, occ_irrep, occ_energy,
    m_out, inter_out, ff_out, row_lab, row_en, col_lab, col_occ, col_vir, flag_out,
    amp_v, fac_v, pkf, pk, gbuf, bcol, brow, ms, part, cbuf, send, rsbuf, inter_s, flag_s,
    load_sem, zsend, zrecv, xsend, xrecv, csend, crecv, rsend, rrecv, gsend, grecv, fsend, frecv,
):
    t = lax.axis_index("tile")
    r = lax.axis_index("rep")
    x = t // Z
    z = t % Z
    y = r // 2
    core = r % 2
    sibling = (t, 2 * y + 1 - core)

    loads = [pltpu.make_async_copy(amp_hbm.at[j], amp_v.at[j], load_sem.at[j]) for j in range(PAIRS)]
    loads.append(pltpu.make_async_copy(fac_hbm, fac_v, load_sem.at[PAIRS]))
    for copy in loads:
        copy.start()

    barrier = pltpu.get_barrier_semaphore()

    def z_peer(n):
        near = Z // 2 - (n + 1) // 2
        return (z + jnp.where(n % 2 == 0, near, Z - near)) % Z

    @pl.loop(0, Z - 1)
    def _(n):
        pl.semaphore_signal(barrier, inc=1, device_id=(x * Z + z_peer(n), r))

    def reducer(d, h):
        return 2 * (2 * ((x + d) % X) + h) + core

    origin = (y // 2 - x + X) % X
    mine_h = y % 2
    chunk = 4 * origin + 2 * core + mine_h

    @pl.loop(0, X)
    def _(d):
        @pl.loop(0, R // 2)
        def _(n):
            @pl.when((d != x) | (n != y))
            def _():
                pl.semaphore_signal(barrier, inc=1, device_id=(d * Z + z, 2 * n + core))

    pl.semaphore_signal(barrier, inc=1, device_id=sibling)

    pkf[...] = jnp.zeros_like(pkf)
    row = lax.broadcasted_iota(I32, (FOLD, 1), 0)
    rem_row = row - MAIN * Z
    target = jnp.where(
        row < MAIN * Z,
        SLAB * (row >> 4) + (row & 15),
        SLAB * (rem_row >> 2) + MAIN + (rem_row & 3),
    )
    lane = lax.broadcasted_iota(I32, (1, X * FOLD), 1)
    folded_lane = lane
    for n in range(1, X):
        folded_lane = folded_lane - jnp.where(lane >= n * FOLD, FOLD, 0)
    pick = jnp.where(target == folded_lane, 1.0, 0.0).astype(BF16)
    for j in range(PAIRS):
        loads[j].wait()
        folded = lax.dot_general(pick, amp_v[j], (((1,), (1,)), ((), ())), preferred_element_type=F32)
        pkf[:, 64 * j : 64 * j + WIDTH] = folded
    for n in range(Z):
        pk[n, :, 0:128] = pkf[MAIN * n : MAIN * (n + 1), 0:128].astype(BF16)
        base = MAIN * Z + REM * n
        rem_rows = [pkf[base : base + REM, 128 * (j // 2) : 128 * (j // 2) + 128] for j in range(PAIRS)]
        rem_rows = [rem_rows[0], pltpu.roll(rem_rows[1], 64, 1), rem_rows[2]]
        rem = jnp.concatenate(rem_rows + [jnp.zeros((MAIN - PAIRS * REM, 128), F32)], axis=0)
        rem = jnp.where(lane_iota(MAIN) < 64, rem, 0.0)
        right = pkf[MAIN * n : MAIN * (n + 1), 128:256] + pltpu.roll(rem, 64, 1)
        pk[n, :, 128:256] = right.astype(BF16)

    pl.semaphore_wait(barrier, Z - 1 + X * (R // 2) - 1 + 1)

    @pl.loop(0, Z - 1)
    def _(n):
        to = z_peer(n)
        pltpu.make_async_remote_copy(
            src_ref=pk.at[to], dst_ref=gbuf.at[x, z], send_sem=zsend, recv_sem=zrecv,
            device_id=(x * Z + to, r),
        ).start()

    gbuf[x, z] = pk[z]

    vlane = lax.broadcasted_iota(I32, (24, X * FOLD), 1)
    vsub = lax.broadcasted_iota(I32, (24, X * FOLD), 0)
    virs = vir_irrep[...].astype(F32)

    def slab_values(tile, values):
        return jnp.sum(jnp.where(vlane == SLAB * tile + vsub, values, 0.0), axis=1, keepdims=True)

    for n in range(X):
        lab = slab_values(n * Z + z, virs).astype(I32)
        for i3 in range(PAIRS):
            brow[n, i3] = block_rows(lab, occ_irrep[PAIRS * x + i3])
    va_lab = slab_values(t, virs).astype(I32)
    va_en = slab_values(t, vir_energy[...])
    for i in range(OCC):
        n, i3 = i // PAIRS, i % PAIRS
        brow[X + n, i3] = block_rows(va_lab, occ_irrep[i])
        lab = jnp.broadcast_to(jnp.bitwise_xor(va_lab, occ_irrep[i]), (24, 128))
        en = jnp.broadcast_to(occ_energy[i] - va_en, (24, 128))
        row_lab[n, MAIN * i3 : MAIN * (i3 + 1), :] = lab[:MAIN]
        row_lab[n, MAIN * PAIRS + REM * i3 : MAIN * PAIRS + REM * (i3 + 1), :] = lab[MAIN:SLAB]
        row_en[n, MAIN * i3 : MAIN * (i3 + 1), :] = en[:MAIN]
        row_en[n, MAIN * PAIRS + REM * i3 : MAIN * PAIRS + REM * (i3 + 1), :] = en[MAIN:SLAB]
    for n in range(X):
        row_lab[n, ROWS - REM : ROWS, :] = jnp.full((REM, 128), -1, I32)
        row_en[n, ROWS - REM : ROWS, :] = jnp.zeros((REM, 128), F32)

    pad = jnp.zeros((8, 1024 - X * FOLD), F32)
    shift = (1024 - WIDTH * r) % 1024
    lane8 = lane_iota(8)
    half = lane8 & 63

    def columns(values):
        whole = jnp.concatenate([jnp.broadcast_to(values, (8, X * FOLD)), pad], axis=1)
        mine = jnp.where(lane8 < WIDTH, pltpu.roll(whole, shift, 1)[:, :128], 0.0)
        return mine + pltpu.roll(mine, 64, 1)

    vb_lab = columns(virs).astype(I32)
    vb_en = columns(vir_energy[...])
    sub16 = lax.broadcasted_iota(I32, (MAIN, 128), 0)
    vb_lab16 = jnp.concatenate([vb_lab, vb_lab], axis=0)
    for g in range(GROUPS):
        for h in range(2):
            first = PAIRS * g + 2 * h
            second = min(first + 1, PAIRS * g + 2)
            cols = slice(256 * g + 128 * h, 256 * g + 128 * h + 128)
            lab = jnp.bitwise_xor(vb_lab, jnp.where(lane8 < 64, occ_irrep[first], occ_irrep[second]))
            lab = jnp.where(half < WIDTH, lab, -2)
            col_lab[:, cols] = jnp.where((lane8 < 64) | (h == 0), lab, -2)
            col_occ[:, cols] = jnp.where(lane8 < 64, occ_energy[first], occ_energy[second])
            col_vir[:, cols] = vb_en
            lab = jnp.concatenate([lab, lab], axis=0)
            if h == 1:
                occ = [occ_irrep[PAIRS * g + j] for j in range(PAIRS)]
                occ = jnp.where(sub16 < REM, occ[0], jnp.where(sub16 < 2 * REM, occ[1], occ[2]))
                rem = jnp.where((lane_iota(MAIN) & 63) < WIDTH, jnp.bitwise_xor(vb_lab16, occ), -2)
                lab = jnp.where(lane_iota(MAIN) < 64, lab, rem)
            bcol[g, :, 128 * h : 128 * h + 128] = lab

    loads[PAIRS].wait()
    zero4 = jnp.zeros((64 - WIDTH, WINDOW), F32)
    for g in range(GROUPS):
        ff_out[256 * g + 192 : 256 * (g + 1), :] = jnp.zeros((64, WINDOW), BF16)
    for k in range(OCC):
        base = 256 * (k // PAIRS) + 64 * (k % PAIRS)
        total = fac_v[k, :, 0:WINDOW].astype(F32)
        for n in range(1, NAUX // WINDOW):
            total = total + fac_v[k, :, WINDOW * n : WINDOW * (n + 1)].astype(F32)
        last = NAUX // WINDOW * WINDOW
        tail = fac_v[k, :, last:NAUX].astype(F32)
        total = total + jnp.concatenate([tail, jnp.zeros((WIDTH, WINDOW - NAUX + last), F32)], axis=1)
        ff_out[base : base + 64, :] = jnp.concatenate([total, zero4], axis=0).astype(BF16)

    vlane8 = lax.broadcasted_iota(I32, (8, X * FOLD), 1)
    vsub8 = lax.broadcasted_iota(I32, (8, X * FOLD), 0)
    first_lab = jnp.sum(
        jnp.where(vlane8 == WIDTH * r + vsub8, virs, 0.0), axis=1, keepdims=True
    ).astype(I32)
    seen = jnp.zeros((8, NAUX), I32)
    for k in range(OCC):
        bit = jnp.left_shift(jnp.int32(1), jnp.bitwise_xor(first_lab, occ_irrep[k]))
        seen = jnp.bitwise_or(seen, jnp.where(fac_v[k, 0:16, :].astype(F32)[0:8] != 0.0, bit, 0))
    for n in (4, 2, 1):
        seen = jnp.bitwise_or(seen, pltpu.roll(seen, n, 0))
    seen = seen[0:1]
    bad = jnp.zeros((1, 1), F32)
    covered = jnp.zeros((1, 1), F32)
    for h in range(8):
        aux_size = jnp.sum(jnp.where(seen == (1 << h), 1.0, 0.0), axis=1, keepdims=True)
        vir_size = jnp.sum(jnp.where(vir_irrep[...] == h, 1.0, 0.0), axis=1, keepdims=True)
        covered = covered + aux_size
        bad = bad + jnp.where(aux_size > WINDOW, 1.0, 0.0) + jnp.where(vir_size > FOLD, 1.0, 0.0)
    bad = bad + jnp.where(covered != NAUX, 1.0, 0.0)
    flag_s[...] = jnp.broadcast_to(jnp.where(bad > 0.0, 1.0, 0.0), (8, 128))

    peers = gbuf.at[x, pl.ds(0, Z - 1)]
    pltpu.make_async_copy(peers, peers, zrecv).wait()
    blocks = [gbuf[x, n] for n in range(Z)]
    cols = [bcol[g] for g in range(GROUPS)]
    for n in range(X):
        assemble(ms.at[pl.ds(ROWS * n, ROWS)], blocks, [brow[n, i3] for i3 in range(PAIRS)], cols)
    sub = lax.broadcasted_iota(I32, (ROWS, WINDOW), 0)
    for n in range(X):
        rows = slice(ROWS * n, ROWS * (n + 1))
        res = jnp.dot(ms[rows], ff_out[...], preferred_element_type=F32)
        res = jnp.where(sub < ROWS - REM, res, flag_s[0:1, 0:1]).astype(BF16)
        part[0, n] = res[: ROWS // 2]
        part[1, n] = res[ROWS // 2 :]

    swap = pltpu.make_async_remote_copy(
        src_ref=part.at[1 - core], dst_ref=cbuf, send_sem=csend, recv_sem=crecv, device_id=sibling
    )
    swap.start()
    swap.wait_recv()
    for n in range(X):
        total = (part[core, n].astype(F32) + cbuf[n].astype(F32)).astype(BF16)
        send[n, 0] = total[:MAIN]
        send[n, 1] = total[MAIN:]

    for n in range(X):
        for h in range(2):
            to = reducer(n, h)

            @pl.when((n != x) | (to != r))
            def _():
                pltpu.make_async_remote_copy(
                    src_ref=send.at[n, h], dst_ref=rsbuf.at[y], send_sem=rsend, recv_sem=rrecv,
                    device_id=(n * Z + z, to),
                ).start()

    for d in (1, 3, 2):
        pltpu.make_async_remote_copy(
            src_ref=gbuf.at[x], dst_ref=gbuf.at[x], send_sem=xsend, recv_sem=xrecv.at[x],
            device_id=(((x + d) % X) * Z + z, r),
        ).start()
    assemble(m_out.at[x], blocks, [brow[X + x, i3] for i3 in range(PAIRS)], cols)

    own = origin == x

    @pl.when(own)
    def _():
        rsbuf[y] = send[x, mine_h]
        rest = rsbuf.at[pl.ds(0, R // 2 - 1)]
        pltpu.make_async_copy(rest, rest, rrecv).wait()
        pltpu.make_async_copy(rest, rest, rsend).wait()

    @pl.when(jnp.logical_not(own))
    def _():
        pltpu.make_async_copy(rsbuf, rsbuf, rrecv).wait()
        pltpu.make_async_copy(rsbuf, rsbuf, rsend).wait()

    total = rsbuf[0].astype(F32)
    for n in range(1, R // 2):
        total = total + rsbuf[n].astype(F32)
    inter_s[chunk] = total.astype(BF16)

    @pl.loop(0, R // 2 - 1)
    def _(n):
        near = (R // 4) - (n + 1) // 2
        to = (y + jnp.where(n % 2 == 0, near, R // 2 - near)) % (R // 2)
        pltpu.make_async_remote_copy(
            src_ref=inter_s.at[chunk], dst_ref=inter_s.at[chunk], send_sem=gsend, recv_sem=grecv.at[y],
            device_id=(t, 2 * to + core),
        ).start()

    def hand_on(slot):
        pltpu.make_async_remote_copy(
            src_ref=inter_s.at[slot], dst_ref=inter_s.at[slot], send_sem=fsend, recv_sem=frecv,
            device_id=sibling,
        ).start()

    hand_on(chunk)

    for d in (1, 3, 2):
        xs = (x + d) % X
        pltpu.make_async_copy(gbuf.at[xs], gbuf.at[xs], xrecv.at[xs]).wait()
        assemble(
            m_out.at[xs], [gbuf[xs, n] for n in range(Z)], [brow[X + xs, i3] for i3 in range(PAIRS)], cols
        )

    @pl.loop(0, R // 2 - 1)
    def _(n):
        near = n // 2 + 1
        source = (y + jnp.where(n % 2 == 0, near, R // 2 - near)) % (R // 2)
        slot = 4 * ((source // 2 - x + X) % X) + 2 * core + source % 2
        pltpu.make_async_copy(inter_s.at[slot], inter_s.at[slot], grecv.at[source]).wait()
        hand_on(slot)

    others = inter_s.at[pl.ds(0, R // 2)]
    pltpu.make_async_copy(others, others, frecv).wait()
    inter_out[...] = inter_s[...]
    flag_out[...] = inter_s[3].astype(F32)[8:16, 0:128]

    sent = pk.at[pl.ds(0, Z - 1)]
    pltpu.make_async_copy(sent, sent, zsend).wait()
    sent = gbuf.at[pl.ds(0, X - 1)]
    pltpu.make_async_copy(sent, sent, xsend).wait()
    swap.wait_send()
    sent = inter_s.at[pl.ds(0, R // 2 - 1)]
    pltpu.make_async_copy(sent, sent, gsend).wait()
    pltpu.make_async_copy(others, others, fsend).wait()


def exchange(amplitudes, occ_energy, vir_energy, occ_irrep, vir_irrep, factors):
    vmem = pl.BlockSpec(memory_space=pltpu.VMEM)
    smem = pl.BlockSpec(memory_space=pltpu.SMEM)
    hbm = pl.BlockSpec(memory_space=pl.ANY)
    shapes = [
        ((X, ROWS, COLS), BF16),
        ((R, MAIN, WINDOW), BF16),
        ((COLS, WINDOW), BF16),
        ((X, ROWS, 128), I32),
        ((X, ROWS, 128), F32),
        ((8, COLS), I32),
        ((8, COLS), F32),
        ((8, COLS), F32),
        ((8, 128), F32),
    ]
    dma = pltpu.SemaphoreType.DMA
    return pl.pallas_call(
        exchange_kernel,
        out_shape=[jax.ShapeDtypeStruct(*s) for s in shapes],
        in_specs=[hbm, hbm, vmem, vmem, smem, smem],
        out_specs=[vmem] * len(shapes),
        scratch_shapes=[
            pltpu.VMEM((PAIRS, WIDTH, X * FOLD), BF16),
            pltpu.VMEM((OCC, WIDTH, NAUX), BF16),
            pltpu.VMEM((FOLD, 256), F32),
            pltpu.VMEM((Z, MAIN, 256), BF16),
            pltpu.VMEM((X, Z, MAIN, 256), BF16),
            pltpu.VMEM((GROUPS, MAIN, 256), I32),
            pltpu.VMEM((2 * X, PAIRS, MAIN, 256), I32),
            pltpu.VMEM((X * ROWS, COLS), BF16),
            pltpu.VMEM((2, X, ROWS // 2, WINDOW), BF16),
            pltpu.VMEM((X, ROWS // 2, WINDOW), BF16),
            pltpu.VMEM((X, 2, MAIN, WINDOW), BF16),
            pltpu.VMEM((R // 2, MAIN, WINDOW), BF16),
            pltpu.VMEM((R, MAIN, WINDOW), BF16),
            pltpu.VMEM((8, 128), F32),
            dma((PAIRS + 1,)), dma, dma, dma, dma((X,)), dma, dma, dma, dma, dma, dma((R // 2,)), dma, dma,
        ],
        compiler_params=pltpu.CompilerParams(
            collective_id=0, has_side_effects=True, vmem_limit_bytes=62 * 1024 * 1024
        ),
        name="exchange",
    )(
        amplitudes.transpose(0, 2, 1), factors, vir_irrep.reshape(1, -1), vir_energy.reshape(1, -1),
        occ_irrep, occ_energy,
    )


def finish_kernel(m_ref, inter_ref, ff_ref, row_lab, row_en, col_lab, col_occ, col_vir, out, res):
    for n in range(X):
        inter = jnp.concatenate([inter_ref[4 * n + c] for c in range(4)], axis=0)
        cycle = lax.dot_general(inter, ff_ref[...], (((1,), (1,)), ((), ())), preferred_element_type=F32)
        for g in range(GROUPS):
            cols = slice(256 * g, 256 * (g + 1))
            rlab = jnp.concatenate([row_lab[n]] * 2, axis=1)
            ren = jnp.concatenate([row_en[n]] * 2, axis=1)
            denom = ren + col_occ[0:1, cols] - col_vir[0:1, cols]
            value = m_ref[n, :, cols].astype(F32) + cycle[:, cols] / denom
            res[:, cols] = jnp.where(rlab == col_lab[0:1, cols], value, 0.0)
        for i3 in range(PAIRS):
            i = PAIRS * n + i3
            for j in range(OCC):
                base = 256 * (j // PAIRS) + 64 * (j % PAIRS)
                out[i, j, 0:MAIN, :] = res[MAIN * i3 : MAIN * (i3 + 1), base : base + WIDTH]
                rem = MAIN * PAIRS + REM * i3
                out[i, j, MAIN:SLAB, :] = res[rem : rem + REM, base : base + WIDTH]


def finish(*operands):
    vmem = pl.BlockSpec(memory_space=pltpu.VMEM)
    out = pl.pallas_call(
        finish_kernel,
        out_shape=jax.ShapeDtypeStruct((OCC, OCC, SLAB, WIDTH), F32),
        in_specs=[vmem] * 8,
        out_specs=vmem,
        scratch_shapes=[pltpu.VMEM((ROWS, COLS), F32)],
        compiler_params=pltpu.CompilerParams(vmem_limit_bytes=32 * 1024 * 1024),
        name="finish",
    )(*operands)
    return out.transpose(0, 2, 1, 3)


def per_device(*arguments):
    *operands, flag = exchange(*arguments)
    return lax.cond(flag[7, 0] == 0.0, lambda: finish(*operands), lambda: dense_path(*arguments))


def solution(mesh):
    return jax.shard_map(
        per_device,
        mesh=mesh,
        in_specs=(P("tile", None, "rep"), P(), P(), P(), P(), P(None, "rep", None)),
        out_specs=P(None, "tile", None, "rep"),
        check_vma=False,
    )
```

```python
import functools

import jax
import jax.numpy as jnp
from jax import lax
from jax.experimental import pallas as pl
from jax.experimental.pallas import tpu as pltpu
from jax.sharding import PartitionSpec as P

X, Z, R = 4, 12, 16
OCC = 12
SLAB = 20
WIDTH = 60
PAIRS = 3
GROUPS = 4
FOLD = SLAB * Z
NAUX = 2048
WINDOW = 384
COLS = GROUPS * 256
ROWS = 64
MAIN = 16
REM = SLAB - MAIN
F32, BF16, I32 = jnp.float32, jnp.bfloat16, jnp.int32


def sum_over_rep(partial_value):
    count = lax.axis_size("rep")
    blocks = partial_value.reshape(count, -1, partial_value.shape[1])
    blocks = lax.all_to_all(blocks, "rep", split_axis=0, concat_axis=0, tiled=True)
    total = jnp.sum(blocks.astype(jnp.float32), axis=0).astype(jnp.bfloat16)
    total = jnp.broadcast_to(total[None], blocks.shape)
    total = lax.all_to_all(total, "rep", split_axis=0, concat_axis=0, tiled=True)
    return total.reshape(partial_value.shape)


def dense_path(amplitudes, occ_energy, vir_energy, occ_irrep, vir_irrep, factors):
    tile_count = lax.axis_size("tile")
    occ_count = occ_energy.shape[0]
    vir_count = vir_energy.shape[0]
    first_width = vir_count // tile_count
    second_width = amplitudes.shape[2]
    relaid = lax.all_to_all(amplitudes, "tile", split_axis=1, concat_axis=0, tiled=True)
    relaid = relaid.reshape(occ_count, occ_count, first_width, second_width).transpose(0, 2, 1, 3)
    matrix = relaid.reshape(occ_count * first_width, occ_count * second_width)
    factor_rows = factors.reshape(occ_count * second_width, factors.shape[2])
    partial_value = jnp.dot(matrix, factor_rows, preferred_element_type=jnp.float32)
    inter = sum_over_rep(partial_value.astype(jnp.bfloat16))
    cycle = jnp.einsum("mq,nq->mn", inter, factor_rows, preferred_element_type=jnp.float32)
    cycle = cycle.reshape(occ_count, first_width, occ_count, second_width)
    tile_start = lax.axis_index("tile") * first_width
    rep_start = lax.axis_index("rep") * second_width
    vir_first = lax.dynamic_slice_in_dim(vir_energy, tile_start, first_width)
    vir_second = lax.dynamic_slice_in_dim(vir_energy, rep_start, second_width)
    irrep_first = lax.dynamic_slice_in_dim(vir_irrep, tile_start, first_width)
    irrep_second = lax.dynamic_slice_in_dim(vir_irrep, rep_start, second_width)
    denom = (
        occ_energy[:, None, None, None]
        - vir_first[None, :, None, None]
        + occ_energy[None, None, :, None]
        - vir_second[None, None, None, :]
    )
    symmetry = jnp.bitwise_xor(
        jnp.bitwise_xor(occ_irrep[:, None, None, None], irrep_first[None, :, None, None]),
        jnp.bitwise_xor(occ_irrep[None, None, :, None], irrep_second[None, None, None, :]),
    )
    return jnp.where(symmetry == 0, relaid.astype(jnp.float32) + cycle / denom, jnp.float32(0.0))


def lane_iota(rows):
    return lax.broadcasted_iota(I32, (rows, 128), 1)


def assemble(dst, blocks, rows, bcol):
    low = lane_iota(MAIN) < 64
    for g in range(GROUPS):
        cols = slice(256 * g, 256 * (g + 1))
        kept = [
            jnp.where(rows[i3] == bcol[g], blocks[GROUPS * i3 + g].astype(F32), 0.0) for i3 in range(PAIRS)
        ]
        for i3 in range(PAIRS):
            dst[MAIN * i3 : MAIN * (i3 + 1), cols] = kept[i3].astype(BF16)
        pieces = []
        for j in range(PAIRS):
            rem = [v[REM * j : REM * (j + 1), 128:256] for v in kept]
            pieces.append(jnp.concatenate(rem + [jnp.zeros((REM, 128), F32)], axis=0))
        left = jnp.where(low, pltpu.roll(pieces[0], 64, 1), pieces[1])
        right = jnp.where(low, pltpu.roll(pieces[2], 64, 1), 0.0)
        dst[MAIN * PAIRS : ROWS, cols] = jnp.concatenate([left, right], axis=1).astype(BF16)


def block_rows(lab, occ):
    main = jnp.broadcast_to(jnp.bitwise_xor(lab[:MAIN], occ), (MAIN, 128))
    rem = jnp.bitwise_xor(lab[MAIN:SLAB], occ)
    rem = jnp.concatenate([rem] * PAIRS + [jnp.full((MAIN - PAIRS * REM, 1), -1, I32)], axis=0)
    right = jnp.where(lane_iota(MAIN) < 64, main, jnp.broadcast_to(rem, (MAIN, 128)))
    return jnp.concatenate([main, right], axis=1)


def exchange_kernel(
    amp_hbm, fac_hbm, vir_irrep, vir_energy, occ_irrep, occ_energy,
    m_out, inter_out, ff_out, row_lab, row_en, col_lab, col_occ, col_vir, flag_out,
    amp_v, fac_v, pkf, pk, gbuf, bcol, brow, ms, part, cbuf, send, rsbuf, inter_s, flag_s,
    load_sem, zsend, zrecv, xsend, xrecv, csend, crecv, rsend, rrecv, gsend, grecv, fsend, frecv,
):
    t = lax.axis_index("tile")
    r = lax.axis_index("rep")
    x = t // Z
    z = t % Z
    y = r // 2
    core = r % 2
    sibling = (t, 2 * y + 1 - core)

    loads = [pltpu.make_async_copy(amp_hbm.at[j], amp_v.at[j], load_sem.at[j]) for j in range(PAIRS)]
    loads.append(pltpu.make_async_copy(fac_hbm, fac_v, load_sem.at[PAIRS]))
    for copy in loads:
        copy.start()

    barrier = pltpu.get_barrier_semaphore()

    def z_peer(n):
        near = Z // 2 - (n + 1) // 2
        return (z + jnp.where(n % 2 == 0, near, Z - near)) % Z

    @pl.loop(0, Z - 1)
    def _(n):
        pl.semaphore_signal(barrier, inc=1, device_id=(x * Z + z_peer(n), r))

    def reducer(d, h):
        return 2 * (2 * ((x + d) % X) + h) + core

    origin = (y // 2 - x + X) % X
    mine_h = y % 2
    chunk = 4 * origin + 2 * core + mine_h

    @pl.loop(0, X)
    def _(d):
        @pl.loop(0, R // 2)
        def _(n):
            @pl.when((d != x) | (n != y))
            def _():
                pl.semaphore_signal(barrier, inc=1, device_id=(d * Z + z, 2 * n + core))

    pl.semaphore_signal(barrier, inc=1, device_id=sibling)

    pkf[...] = jnp.zeros_like(pkf)
    row = lax.broadcasted_iota(I32, (FOLD, 1), 0)
    rem_row = row - MAIN * Z
    target = jnp.where(
        row < MAIN * Z,
        SLAB * (row >> 4) + (row & 15),
        SLAB * (rem_row >> 2) + MAIN + (rem_row & 3),
    )
    lane = lax.broadcasted_iota(I32, (1, X * FOLD), 1)
    folded_lane = lane
    for n in range(1, X):
        folded_lane = folded_lane - jnp.where(lane >= n * FOLD, FOLD, 0)
    pick = jnp.where(target == folded_lane, 1.0, 0.0).astype(BF16)
    for j in range(PAIRS):
        loads[j].wait()
        folded = lax.dot_general(pick, amp_v[j], (((1,), (1,)), ((), ())), preferred_element_type=F32)
        pkf[:, 64 * j : 64 * j + WIDTH] = folded
    for n in range(Z):
        pk[n, :, 0:128] = pkf[MAIN * n : MAIN * (n + 1), 0:128].astype(BF16)
        base = MAIN * Z + REM * n
        rem_rows = [pkf[base : base + REM, 128 * (j // 2) : 128 * (j // 2) + 128] for j in range(PAIRS)]
        rem_rows = [rem_rows[0], pltpu.roll(rem_rows[1], 64, 1), rem_rows[2]]
        rem = jnp.concatenate(rem_rows + [jnp.zeros((MAIN - PAIRS * REM, 128), F32)], axis=0)
        rem = jnp.where(lane_iota(MAIN) < 64, rem, 0.0)
        right = pkf[MAIN * n : MAIN * (n + 1), 128:256] + pltpu.roll(rem, 64, 1)
        pk[n, :, 128:256] = right.astype(BF16)

    pl.semaphore_wait(barrier, Z - 1 + X * (R // 2) - 1 + 1)

    @pl.loop(0, Z - 1)
    def _(n):
        to = z_peer(n)
        pltpu.make_async_remote_copy(
            src_ref=pk.at[to], dst_ref=gbuf.at[x, z], send_sem=zsend, recv_sem=zrecv,
            device_id=(x * Z + to, r),
        ).start()

    gbuf[x, z] = pk[z]

    vlane = lax.broadcasted_iota(I32, (24, X * FOLD), 1)
    vsub = lax.broadcasted_iota(I32, (24, X * FOLD), 0)
    virs = vir_irrep[...].astype(F32)

    def slab_values(tile, values):
        return jnp.sum(jnp.where(vlane == SLAB * tile + vsub, values, 0.0), axis=1, keepdims=True)

    for n in range(X):
        lab = slab_values(n * Z + z, virs).astype(I32)
        for i3 in range(PAIRS):
            brow[n, i3] = block_rows(lab, occ_irrep[PAIRS * x + i3])
    va_lab = slab_values(t, virs).astype(I32)
    va_en = slab_values(t, vir_energy[...])
    for i in range(OCC):
        n, i3 = i // PAIRS, i % PAIRS
        brow[X + n, i3] = block_rows(va_lab, occ_irrep[i])
        lab = jnp.broadcast_to(jnp.bitwise_xor(va_lab, occ_irrep[i]), (24, 128))
        en = jnp.broadcast_to(occ_energy[i] - va_en, (24, 128))
        row_lab[n, MAIN * i3 : MAIN * (i3 + 1), :] = lab[:MAIN]
        row_lab[n, MAIN * PAIRS + REM * i3 : MAIN * PAIRS + REM * (i3 + 1), :] = lab[MAIN:SLAB]
        row_en[n, MAIN * i3 : MAIN * (i3 + 1), :] = en[:MAIN]
        row_en[n, MAIN * PAIRS + REM * i3 : MAIN * PAIRS + REM * (i3 + 1), :] = en[MAIN:SLAB]
    for n in range(X):
        row_lab[n, ROWS - REM : ROWS, :] = jnp.full((REM, 128), -1, I32)
        row_en[n, ROWS - REM : ROWS, :] = jnp.zeros((REM, 128), F32)

    pad = jnp.zeros((8, 1024 - X * FOLD), F32)
    shift = (1024 - WIDTH * r) % 1024
    lane8 = lane_iota(8)
    half = lane8 & 63

    def columns(values):
        whole = jnp.concatenate([jnp.broadcast_to(values, (8, X * FOLD)), pad], axis=1)
        mine = jnp.where(lane8 < WIDTH, pltpu.roll(whole, shift, 1)[:, :128], 0.0)
        return mine + pltpu.roll(mine, 64, 1)

    vb_lab = columns(virs).astype(I32)
    vb_en = columns(vir_energy[...])
    sub16 = lax.broadcasted_iota(I32, (MAIN, 128), 0)
    vb_lab16 = jnp.concatenate([vb_lab, vb_lab], axis=0)
    for g in range(GROUPS):
        for h in range(2):
            first = PAIRS * g + 2 * h
            second = min(first + 1, PAIRS * g + 2)
            cols = slice(256 * g + 128 * h, 256 * g + 128 * h + 128)
            lab = jnp.bitwise_xor(vb_lab, jnp.where(lane8 < 64, occ_irrep[first], occ_irrep[second]))
            lab = jnp.where(half < WIDTH, lab, -2)
            col_lab[:, cols] = jnp.where((lane8 < 64) | (h == 0), lab, -2)
            col_occ[:, cols] = jnp.where(lane8 < 64, occ_energy[first], occ_energy[second])
            col_vir[:, cols] = vb_en
            lab = jnp.concatenate([lab, lab], axis=0)
            if h == 1:
                occ = [occ_irrep[PAIRS * g + j] for j in range(PAIRS)]
                occ = jnp.where(sub16 < REM, occ[0], jnp.where(sub16 < 2 * REM, occ[1], occ[2]))
                rem = jnp.where((lane_iota(MAIN) & 63) < WIDTH, jnp.bitwise_xor(vb_lab16, occ), -2)
                lab = jnp.where(lane_iota(MAIN) < 64, lab, rem)
            bcol[g, :, 128 * h : 128 * h + 128] = lab

    loads[PAIRS].wait()
    zero4 = jnp.zeros((64 - WIDTH, WINDOW), F32)
    for g in range(GROUPS):
        ff_out[256 * g + 192 : 256 * (g + 1), :] = jnp.zeros((64, WINDOW), BF16)
    for k in range(OCC):
        base = 256 * (k // PAIRS) + 64 * (k % PAIRS)
        total = fac_v[k, :, 0:WINDOW].astype(F32)
        for n in range(1, NAUX // WINDOW):
            total = total + fac_v[k, :, WINDOW * n : WINDOW * (n + 1)].astype(F32)
        last = NAUX // WINDOW * WINDOW
        tail = fac_v[k, :, last:NAUX].astype(F32)
        total = total + jnp.concatenate([tail, jnp.zeros((WIDTH, WINDOW - NAUX + last), F32)], axis=1)
        ff_out[base : base + 64, :] = jnp.concatenate([total, zero4], axis=0).astype(BF16)

    vlane8 = lax.broadcasted_iota(I32, (8, X * FOLD), 1)
    vsub8 = lax.broadcasted_iota(I32, (8, X * FOLD), 0)
    first_lab = jnp.sum(
        jnp.where(vlane8 == WIDTH * r + vsub8, virs, 0.0), axis=1, keepdims=True
    ).astype(I32)
    seen = jnp.zeros((8, NAUX), I32)
    for k in range(OCC):
        bit = jnp.left_shift(jnp.int32(1), jnp.bitwise_xor(first_lab, occ_irrep[k]))
        seen = jnp.bitwise_or(seen, jnp.where(fac_v[k, 0:16, :].astype(F32)[0:8] != 0.0, bit, 0))
    for n in (4, 2, 1):
        seen = jnp.bitwise_or(seen, pltpu.roll(seen, n, 0))
    seen = seen[0:1]
    bad = jnp.zeros((1, 1), F32)
    covered = jnp.zeros((1, 1), F32)
    for h in range(8):
        aux_size = jnp.sum(jnp.where(seen == (1 << h), 1.0, 0.0), axis=1, keepdims=True)
        vir_size = jnp.sum(jnp.where(vir_irrep[...] == h, 1.0, 0.0), axis=1, keepdims=True)
        covered = covered + aux_size
        bad = bad + jnp.where(aux_size > WINDOW, 1.0, 0.0) + jnp.where(vir_size > FOLD, 1.0, 0.0)
    bad = bad + jnp.where(covered != NAUX, 1.0, 0.0)
    flag_s[...] = jnp.broadcast_to(jnp.where(bad > 0.0, 1.0, 0.0), (8, 128))

    peers = gbuf.at[x, pl.ds(0, Z - 1)]
    pltpu.make_async_copy(peers, peers, zrecv).wait()
    blocks = [gbuf[x, n] for n in range(Z)]
    cols = [bcol[g] for g in range(GROUPS)]
    for n in range(X):
        assemble(ms.at[pl.ds(ROWS * n, ROWS)], blocks, [brow[n, i3] for i3 in range(PAIRS)], cols)
    sub = lax.broadcasted_iota(I32, (ROWS, WINDOW), 0)
    for n in range(X):
        rows = slice(ROWS * n, ROWS * (n + 1))
        res = jnp.dot(ms[rows], ff_out[...], preferred_element_type=F32)
        res = jnp.where(sub < ROWS - REM, res, flag_s[0:1, 0:1]).astype(BF16)
        part[0, n] = res[: ROWS // 2]
        part[1, n] = res[ROWS // 2 :]

    swap = pltpu.make_async_remote_copy(
        src_ref=part.at[1 - core], dst_ref=cbuf, send_sem=csend, recv_sem=crecv, device_id=sibling
    )
    swap.start()
    swap.wait_recv()
    for n in range(X):
        total = (part[core, n].astype(F32) + cbuf[n].astype(F32)).astype(BF16)
        send[n, 0] = total[:MAIN]
        send[n, 1] = total[MAIN:]

    for n in range(X):
        for h in range(2):
            to = reducer(n, h)

            @pl.when((n != x) | (to != r))
            def _():
                pltpu.make_async_remote_copy(
                    src_ref=send.at[n, h], dst_ref=rsbuf.at[y], send_sem=rsend, recv_sem=rrecv,
                    device_id=(n * Z + z, to),
                ).start()

    for d in (1, 3, 2):
        pltpu.make_async_remote_copy(
            src_ref=gbuf.at[x], dst_ref=gbuf.at[x], send_sem=xsend, recv_sem=xrecv.at[x],
            device_id=(((x + d) % X) * Z + z, r),
        ).start()
    assemble(m_out.at[x], blocks, [brow[X + x, i3] for i3 in range(PAIRS)], cols)

    own = origin == x

    @pl.when(own)
    def _():
        rsbuf[y] = send[x, mine_h]
        rest = rsbuf.at[pl.ds(0, R // 2 - 1)]
        pltpu.make_async_copy(rest, rest, rrecv).wait()
        pltpu.make_async_copy(rest, rest, rsend).wait()

    @pl.when(jnp.logical_not(own))
    def _():
        pltpu.make_async_copy(rsbuf, rsbuf, rrecv).wait()
        pltpu.make_async_copy(rsbuf, rsbuf, rsend).wait()

    total = rsbuf[0].astype(F32)
    for n in range(1, R // 2):
        total = total + rsbuf[n].astype(F32)
    inter_s[chunk] = total.astype(BF16)

    @pl.loop(0, R // 2 - 1)
    def _(n):
        near = (R // 4) - (n + 1) // 2
        to = (y + jnp.where(n % 2 == 0, near, R // 2 - near)) % (R // 2)
        pltpu.make_async_remote_copy(
            src_ref=inter_s.at[chunk], dst_ref=inter_s.at[chunk], send_sem=gsend, recv_sem=grecv.at[y],
            device_id=(t, 2 * to + core),
        ).start()

    def hand_on(slot):
        pltpu.make_async_remote_copy(
            src_ref=inter_s.at[slot], dst_ref=inter_s.at[slot], send_sem=fsend, recv_sem=frecv,
            device_id=sibling,
        ).start()

    hand_on(chunk)

    for d in (1, 3, 2):
        xs = (x + d) % X
        pltpu.make_async_copy(gbuf.at[xs], gbuf.at[xs], xrecv.at[xs]).wait()
        assemble(
            m_out.at[xs], [gbuf[xs, n] for n in range(Z)], [brow[X + xs, i3] for i3 in range(PAIRS)], cols
        )

    @pl.loop(0, R // 2 - 1)
    def _(n):
        near = n // 2 + 1
        source = (y + jnp.where(n % 2 == 0, near, R // 2 - near)) % (R // 2)
        slot = 4 * ((source // 2 - x + X) % X) + 2 * core + source % 2
        pltpu.make_async_copy(inter_s.at[slot], inter_s.at[slot], grecv.at[source]).wait()
        hand_on(slot)

    others = inter_s.at[pl.ds(0, R // 2)]
    pltpu.make_async_copy(others, others, frecv).wait()
    inter_out[...] = inter_s[...]
    flag_out[...] = inter_s[3].astype(F32)[8:16, 0:128]

    sent = pk.at[pl.ds(0, Z - 1)]
    pltpu.make_async_copy(sent, sent, zsend).wait()
    sent = gbuf.at[pl.ds(0, X - 1)]
    pltpu.make_async_copy(sent, sent, xsend).wait()
    swap.wait_send()
    sent = inter_s.at[pl.ds(0, R // 2 - 1)]
    pltpu.make_async_copy(sent, sent, gsend).wait()
    pltpu.make_async_copy(others, others, fsend).wait()


def exchange(amplitudes, occ_energy, vir_energy, occ_irrep, vir_irrep, factors):
    vmem = pl.BlockSpec(memory_space=pltpu.VMEM)
    smem = pl.BlockSpec(memory_space=pltpu.SMEM)
    hbm = pl.BlockSpec(memory_space=pl.ANY)
    shapes = [
        ((X, ROWS, COLS), BF16),
        ((R, MAIN, WINDOW), BF16),
        ((COLS, WINDOW), BF16),
        ((X, ROWS, 128), I32),
        ((X, ROWS, 128), F32),
        ((8, COLS), I32),
        ((8, COLS), F32),
        ((8, COLS), F32),
        ((8, 128), F32),
    ]
    dma = pltpu.SemaphoreType.DMA
    return pl.pallas_call(
        exchange_kernel,
        out_shape=[jax.ShapeDtypeStruct(*s) for s in shapes],
        in_specs=[hbm, hbm, vmem, vmem, smem, smem],
        out_specs=[vmem] * len(shapes),
        scratch_shapes=[
            pltpu.VMEM((PAIRS, WIDTH, X * FOLD), BF16),
            pltpu.VMEM((OCC, WIDTH, NAUX), BF16),
            pltpu.VMEM((FOLD, 256), F32),
            pltpu.VMEM((Z, MAIN, 256), BF16),
            pltpu.VMEM((X, Z, MAIN, 256), BF16),
            pltpu.VMEM((GROUPS, MAIN, 256), I32),
            pltpu.VMEM((2 * X, PAIRS, MAIN, 256), I32),
            pltpu.VMEM((X * ROWS, COLS), BF16),
            pltpu.VMEM((2, X, ROWS // 2, WINDOW), BF16),
            pltpu.VMEM((X, ROWS // 2, WINDOW), BF16),
            pltpu.VMEM((X, 2, MAIN, WINDOW), BF16),
            pltpu.VMEM((R // 2, MAIN, WINDOW), BF16),
            pltpu.VMEM((R, MAIN, WINDOW), BF16),
            pltpu.VMEM((8, 128), F32),
            dma((PAIRS + 1,)), dma, dma, dma, dma((X,)), dma, dma, dma, dma, dma, dma((R // 2,)), dma, dma,
        ],
        compiler_params=pltpu.CompilerParams(
            collective_id=0, has_side_effects=True, vmem_limit_bytes=62 * 1024 * 1024
        ),
        name="exchange",
    )(
        amplitudes.transpose(0, 2, 1), factors, vir_irrep.reshape(1, -1), vir_energy.reshape(1, -1),
        occ_irrep, occ_energy,
    )


def finish_kernel(m_ref, inter_ref, ff_ref, row_lab, row_en, col_lab, col_occ, col_vir, out, res):
    for n in range(X):
        inter = jnp.concatenate([inter_ref[4 * n + c] for c in range(4)], axis=0)
        cycle = lax.dot_general(inter, ff_ref[...], (((1,), (1,)), ((), ())), preferred_element_type=F32)
        for g in range(GROUPS):
            cols = slice(256 * g, 256 * (g + 1))
            rlab = jnp.concatenate([row_lab[n]] * 2, axis=1)
            ren = jnp.concatenate([row_en[n]] * 2, axis=1)
            denom = ren + col_occ[0:1, cols] - col_vir[0:1, cols]
            value = m_ref[n, :, cols].astype(F32) + cycle[:, cols] / denom
            res[:, cols] = jnp.where(rlab == col_lab[0:1, cols], value, 0.0)
        for i3 in range(PAIRS):
            i = PAIRS * n + i3
            for j in range(OCC):
                base = 256 * (j // PAIRS) + 64 * (j % PAIRS)
                out[i, j, 0:MAIN, :] = res[MAIN * i3 : MAIN * (i3 + 1), base : base + WIDTH]
                rem = MAIN * PAIRS + REM * i3
                out[i, j, MAIN:SLAB, :] = res[rem : rem + REM, base : base + WIDTH]


def finish(*operands):
    vmem = pl.BlockSpec(memory_space=pltpu.VMEM)
    out = pl.pallas_call(
        finish_kernel,
        out_shape=jax.ShapeDtypeStruct((OCC, OCC, SLAB, WIDTH), F32),
        in_specs=[vmem] * 8,
        out_specs=vmem,
        scratch_shapes=[pltpu.VMEM((ROWS, COLS), F32)],
        compiler_params=pltpu.CompilerParams(vmem_limit_bytes=32 * 1024 * 1024),
        name="finish",
    )(*operands)
    return out.transpose(0, 2, 1, 3)


def per_device(*arguments):
    *operands, flag = exchange(*arguments)
    return lax.cond(flag[7, 0] == 0.0, lambda: finish(*operands), lambda: dense_path(*arguments))


def solution(mesh):
    return jax.shard_map(
        per_device,
        mesh=mesh,
        in_specs=(P("tile", None, "rep"), P(), P(), P(), P(), P(None, "rep", None)),
        out_specs=P(None, "tile", None, "rep"),
        check_vma=False,
    )
```

```python
import functools

import jax
import jax.numpy as jnp
from jax import lax
from jax.experimental import pallas as pl
from jax.experimental.pallas import tpu as pltpu
from jax.sharding import PartitionSpec as P

X, Z, R = 4, 12, 16
OCC = 12
SLAB = 20
WIDTH = 60
PAIRS = 3
GROUPS = 4
FOLD = SLAB * Z
NAUX = 2048
WINDOW = 384
COLS = GROUPS * 256
ROWS = 64
MAIN = 16
REM = SLAB - MAIN
F32, BF16, I32 = jnp.float32, jnp.bfloat16, jnp.int32


def sum_over_rep(partial_value):
    count = lax.axis_size("rep")
    blocks = partial_value.reshape(count, -1, partial_value.shape[1])
    blocks = lax.all_to_all(blocks, "rep", split_axis=0, concat_axis=0, tiled=True)
    total = jnp.sum(blocks.astype(jnp.float32), axis=0).astype(jnp.bfloat16)
    total = jnp.broadcast_to(total[None], blocks.shape)
    total = lax.all_to_all(total, "rep", split_axis=0, concat_axis=0, tiled=True)
    return total.reshape(partial_value.shape)


def dense_path(amplitudes, occ_energy, vir_energy, occ_irrep, vir_irrep, factors):
    tile_count = lax.axis_size("tile")
    occ_count = occ_energy.shape[0]
    vir_count = vir_energy.shape[0]
    first_width = vir_count // tile_count
    second_width = amplitudes.shape[2]
    relaid = lax.all_to_all(amplitudes, "tile", split_axis=1, concat_axis=0, tiled=True)
    relaid = relaid.reshape(occ_count, occ_count, first_width, second_width).transpose(0, 2, 1, 3)
    matrix = relaid.reshape(occ_count * first_width, occ_count * second_width)
    factor_rows = factors.reshape(occ_count * second_width, factors.shape[2])
    partial_value = jnp.dot(matrix, factor_rows, preferred_element_type=jnp.float32)
    inter = sum_over_rep(partial_value.astype(jnp.bfloat16))
    cycle = jnp.einsum("mq,nq->mn", inter, factor_rows, preferred_element_type=jnp.float32)
    cycle = cycle.reshape(occ_count, first_width, occ_count, second_width)
    tile_start = lax.axis_index("tile") * first_width
    rep_start = lax.axis_index("rep") * second_width
    vir_first = lax.dynamic_slice_in_dim(vir_energy, tile_start, first_width)
    vir_second = lax.dynamic_slice_in_dim(vir_energy, rep_start, second_width)
    irrep_first = lax.dynamic_slice_in_dim(vir_irrep, tile_start, first_width)
    irrep_second = lax.dynamic_slice_in_dim(vir_irrep, rep_start, second_width)
    denom = (
        occ_energy[:, None, None, None]
        - vir_first[None, :, None, None]
        + occ_energy[None, None, :, None]
        - vir_second[None, None, None, :]
    )
    symmetry = jnp.bitwise_xor(
        jnp.bitwise_xor(occ_irrep[:, None, None, None], irrep_first[None, :, None, None]),
        jnp.bitwise_xor(occ_irrep[None, None, :, None], irrep_second[None, None, None, :]),
    )
    return jnp.where(symmetry == 0, relaid.astype(jnp.float32) + cycle / denom, jnp.float32(0.0))


def lane_iota(rows):
    return lax.broadcasted_iota(I32, (rows, 128), 1)


def assemble(dst, blocks, rows, bcol):
    low = lane_iota(MAIN) < 64
    for g in range(GROUPS):
        cols = slice(256 * g, 256 * (g + 1))
        kept = [
            jnp.where(rows[i3] == bcol[g], blocks[GROUPS * i3 + g].astype(F32), 0.0) for i3 in range(PAIRS)
        ]
        for i3 in range(PAIRS):
            dst[MAIN * i3 : MAIN * (i3 + 1), cols] = kept[i3].astype(BF16)
        pieces = []
        for j in range(PAIRS):
            rem = [v[REM * j : REM * (j + 1), 128:256] for v in kept]
            pieces.append(jnp.concatenate(rem + [jnp.zeros((REM, 128), F32)], axis=0))
        left = jnp.where(low, pltpu.roll(pieces[0], 64, 1), pieces[1])
        right = jnp.where(low, pltpu.roll(pieces[2], 64, 1), 0.0)
        dst[MAIN * PAIRS : ROWS, cols] = jnp.concatenate([left, right], axis=1).astype(BF16)


def block_rows(lab, occ):
    main = jnp.broadcast_to(jnp.bitwise_xor(lab[:MAIN], occ), (MAIN, 128))
    rem = jnp.bitwise_xor(lab[MAIN:SLAB], occ)
    rem = jnp.concatenate([rem] * PAIRS + [jnp.full((MAIN - PAIRS * REM, 1), -1, I32)], axis=0)
    right = jnp.where(lane_iota(MAIN) < 64, main, jnp.broadcast_to(rem, (MAIN, 128)))
    return jnp.concatenate([main, right], axis=1)


def exchange_kernel(
    amp_hbm, fac_hbm, vir_irrep_hbm, vir_energy_hbm, occ_irrep_hbm, occ_energy_hbm,
    m_hbm, inter_hbm, ff_hbm, rows_hbm, cols_hbm, flag_out,
    amp_v, fac_v, vir_irrep, vir_energy, occ_irrep, occ_energy, m_out, ff_out, rows_out, cols_out,
    pkf, pk, gbuf, bcol, brow, ms, part, cbuf, send, rsbuf, inter_s, flag_s,
    load_sem, out_sem, zsend, zrecv, xsend, xrecv, csend, crecv, rsend, rrecv, gsend, grecv, fsend, frecv,
):
    t = lax.axis_index("tile")
    r = lax.axis_index("rep")
    x = t // Z
    z = t % Z
    y = r // 2
    core = r % 2
    sibling = (t, 2 * y + 1 - core)

    loads = [pltpu.make_async_copy(amp_hbm.at[j], amp_v.at[j], load_sem.at[j]) for j in range(PAIRS)]
    loads.append(pltpu.make_async_copy(fac_hbm, fac_v, load_sem.at[PAIRS]))
    small = [
        (vir_irrep_hbm, vir_irrep), (vir_energy_hbm, vir_energy),
        (occ_irrep_hbm, occ_irrep), (occ_energy_hbm, occ_energy),
    ]
    small = [pltpu.make_async_copy(a, b, load_sem.at[PAIRS + 1 + n]) for n, (a, b) in enumerate(small)]
    saves = [(ff_out, ff_hbm), (rows_out, rows_hbm), (cols_out, cols_hbm), (m_out, m_hbm), (inter_s, inter_hbm)]
    saves = [pltpu.make_async_copy(a, b, out_sem.at[n]) for n, (a, b) in enumerate(saves)]
    barrier = pltpu.get_barrier_semaphore()

    def z_peer(n):
        near = Z // 2 - (n + 1) // 2
        return (z + jnp.where(n % 2 == 0, near, Z - near)) % Z

    @pl.loop(0, Z - 1)
    def _(n):
        pl.semaphore_signal(barrier, inc=1, device_id=(x * Z + z_peer(n), r))

    for copy in loads[:PAIRS] + small + loads[PAIRS:]:
        copy.start()

    def reducer(d, h):
        return 2 * (2 * ((x + d) % X) + h) + core

    origin = (y // 2 - x + X) % X
    mine_h = y % 2
    chunk = 4 * origin + 2 * core + mine_h

    @pl.loop(0, X)
    def _(d):
        @pl.loop(0, R // 2)
        def _(n):
            @pl.when((d != x) | (n != y))
            def _():
                pl.semaphore_signal(barrier, inc=1, device_id=(d * Z + z, 2 * n + core))

    pl.semaphore_signal(barrier, inc=1, device_id=sibling)

    pkf[...] = jnp.zeros_like(pkf)
    row = lax.broadcasted_iota(I32, (FOLD, 1), 0)
    rem_row = row - MAIN * Z
    target = jnp.where(
        row < MAIN * Z,
        SLAB * (row >> 4) + (row & 15),
        SLAB * (rem_row >> 2) + MAIN + (rem_row & 3),
    )
    lane = lax.broadcasted_iota(I32, (1, X * FOLD), 1)
    folded_lane = lane
    for n in range(1, X):
        folded_lane = folded_lane - jnp.where(lane >= n * FOLD, FOLD, 0)
    pick = jnp.where(target == folded_lane, 1.0, 0.0).astype(BF16)
    for j in range(PAIRS):
        loads[j].wait()
        folded = lax.dot_general(pick, amp_v[j], (((1,), (1,)), ((), ())), preferred_element_type=F32)
        pkf[:, 64 * j : 64 * j + WIDTH] = folded
    for n in range(Z):
        pk[n, :, 0:128] = pkf[MAIN * n : MAIN * (n + 1), 0:128].astype(BF16)
        base = MAIN * Z + REM * n
        rem_rows = [pkf[base : base + REM, 128 * (j // 2) : 128 * (j // 2) + 128] for j in range(PAIRS)]
        rem_rows = [rem_rows[0], pltpu.roll(rem_rows[1], 64, 1), rem_rows[2]]
        rem = jnp.concatenate(rem_rows + [jnp.zeros((MAIN - PAIRS * REM, 128), F32)], axis=0)
        rem = jnp.where(lane_iota(MAIN) < 64, rem, 0.0)
        right = pkf[MAIN * n : MAIN * (n + 1), 128:256] + pltpu.roll(rem, 64, 1)
        pk[n, :, 128:256] = right.astype(BF16)

    pl.semaphore_wait(barrier, Z - 1 + X * (R // 2) - 1 + 1)

    @pl.loop(0, Z - 1)
    def _(n):
        to = z_peer(n)
        pltpu.make_async_remote_copy(
            src_ref=pk.at[to], dst_ref=gbuf.at[x, z], send_sem=zsend, recv_sem=zrecv,
            device_id=(x * Z + to, r),
        ).start()

    gbuf[x, z] = pk[z]

    for copy in small:
        copy.wait()
    vlane = lax.broadcasted_iota(I32, (24, X * FOLD), 1)
    vsub = lax.broadcasted_iota(I32, (24, X * FOLD), 0)
    virs = vir_irrep[...].astype(F32)

    def slab_values(tile, values):
        return jnp.sum(jnp.where(vlane == SLAB * tile + vsub, values, 0.0), axis=1, keepdims=True)

    for n in range(X):
        lab = slab_values(n * Z + z, virs).astype(I32)
        for i3 in range(PAIRS):
            brow[n, i3] = block_rows(lab, occ_irrep[PAIRS * x + i3])
    va_lab = slab_values(t, virs).astype(I32)
    va_en = slab_values(t, vir_energy[...])
    for i in range(OCC):
        n, i3 = i // PAIRS, i % PAIRS
        brow[X + n, i3] = block_rows(va_lab, occ_irrep[i])
        lab = jnp.broadcast_to(jnp.bitwise_xor(va_lab, occ_irrep[i]).astype(F32), (24, 128))
        en = jnp.broadcast_to(occ_energy[i] - va_en, (24, 128))
        rows_out[0, n, MAIN * i3 : MAIN * (i3 + 1), :] = lab[:MAIN]
        rows_out[0, n, MAIN * PAIRS + REM * i3 : MAIN * PAIRS + REM * (i3 + 1), :] = lab[MAIN:SLAB]
        rows_out[1, n, MAIN * i3 : MAIN * (i3 + 1), :] = en[:MAIN]
        rows_out[1, n, MAIN * PAIRS + REM * i3 : MAIN * PAIRS + REM * (i3 + 1), :] = en[MAIN:SLAB]
    for n in range(X):
        rows_out[0, n, ROWS - REM : ROWS, :] = jnp.full((REM, 128), -1.0, F32)
        rows_out[1, n, ROWS - REM : ROWS, :] = jnp.zeros((REM, 128), F32)

    pad = jnp.zeros((8, 1024 - X * FOLD), F32)
    shift = (1024 - WIDTH * r) % 1024
    lane8 = lane_iota(8)
    half = lane8 & 63

    def columns(values):
        whole = jnp.concatenate([jnp.broadcast_to(values, (8, X * FOLD)), pad], axis=1)
        mine = jnp.where(lane8 < WIDTH, pltpu.roll(whole, shift, 1)[:, :128], 0.0)
        return mine + pltpu.roll(mine, 64, 1)

    vb_lab = columns(virs).astype(I32)
    vb_en = columns(vir_energy[...])
    sub16 = lax.broadcasted_iota(I32, (MAIN, 128), 0)
    vb_lab16 = jnp.concatenate([vb_lab, vb_lab], axis=0)
    for g in range(GROUPS):
        for h in range(2):
            first = PAIRS * g + 2 * h
            second = min(first + 1, PAIRS * g + 2)
            cols = slice(256 * g + 128 * h, 256 * g + 128 * h + 128)
            lab = jnp.bitwise_xor(vb_lab, jnp.where(lane8 < 64, occ_irrep[first], occ_irrep[second]))
            lab = jnp.where(half < WIDTH, lab, -2)
            cols_out[0, :, cols] = jnp.where((lane8 < 64) | (h == 0), lab, -2).astype(F32)
            cols_out[1, :, cols] = jnp.where(lane8 < 64, occ_energy[first], occ_energy[second])
            cols_out[2, :, cols] = vb_en
            lab = jnp.concatenate([lab, lab], axis=0)
            if h == 1:
                occ = [occ_irrep[PAIRS * g + j] for j in range(PAIRS)]
                occ = jnp.where(sub16 < REM, occ[0], jnp.where(sub16 < 2 * REM, occ[1], occ[2]))
                rem = jnp.where((lane_iota(MAIN) & 63) < WIDTH, jnp.bitwise_xor(vb_lab16, occ), -2)
                lab = jnp.where(lane_iota(MAIN) < 64, lab, rem)
            bcol[g, :, 128 * h : 128 * h + 128] = lab

    saves[1].start()
    saves[2].start()

    loads[PAIRS].wait()
    zero4 = jnp.zeros((64 - WIDTH, WINDOW), F32)
    for g in range(GROUPS):
        ff_out[256 * g + 192 : 256 * (g + 1), :] = jnp.zeros((64, WINDOW), BF16)
    for k in range(OCC):
        base = 256 * (k // PAIRS) + 64 * (k % PAIRS)
        total = fac_v[k, :, 0:WINDOW].astype(F32)
        for n in range(1, NAUX // WINDOW):
            total = total + fac_v[k, :, WINDOW * n : WINDOW * (n + 1)].astype(F32)
        last = NAUX // WINDOW * WINDOW
        tail = fac_v[k, :, last:NAUX].astype(F32)
        total = total + jnp.concatenate([tail, jnp.zeros((WIDTH, WINDOW - NAUX + last), F32)], axis=1)
        ff_out[base : base + 64, :] = jnp.concatenate([total, zero4], axis=0).astype(BF16)

    saves[0].start()
    vlane8 = lax.broadcasted_iota(I32, (8, X * FOLD), 1)
    vsub8 = lax.broadcasted_iota(I32, (8, X * FOLD), 0)
    first_lab = jnp.sum(
        jnp.where(vlane8 == WIDTH * r + vsub8, virs, 0.0), axis=1, keepdims=True
    ).astype(I32)
    seen = jnp.zeros((8, NAUX), I32)
    for k in range(OCC):
        bit = jnp.left_shift(jnp.int32(1), jnp.bitwise_xor(first_lab, occ_irrep[k]))
        seen = jnp.bitwise_or(seen, jnp.where(fac_v[k, 0:16, :].astype(F32)[0:8] != 0.0, bit, 0))
    for n in (4, 2, 1):
        seen = jnp.bitwise_or(seen, pltpu.roll(seen, n, 0))
    seen = seen[0:1]
    bad = jnp.zeros((1, 1), F32)
    covered = jnp.zeros((1, 1), F32)
    for h in range(8):
        aux_size = jnp.sum(jnp.where(seen == (1 << h), 1.0, 0.0), axis=1, keepdims=True)
        vir_size = jnp.sum(jnp.where(vir_irrep[...] == h, 1.0, 0.0), axis=1, keepdims=True)
        covered = covered + aux_size
        bad = bad + jnp.where(aux_size > WINDOW, 1.0, 0.0) + jnp.where(vir_size > FOLD, 1.0, 0.0)
    bad = bad + jnp.where(covered != NAUX, 1.0, 0.0)
    flag_s[...] = jnp.broadcast_to(jnp.where(bad > 0.0, 1.0, 0.0), (8, 128))

    peers = gbuf.at[x, pl.ds(0, Z - 1)]
    pltpu.make_async_copy(peers, peers, zrecv).wait()
    blocks = [gbuf[x, n] for n in range(Z)]
    cols = [bcol[g] for g in range(GROUPS)]
    for n in range(X):
        assemble(ms.at[pl.ds(ROWS * n, ROWS)], blocks, [brow[n, i3] for i3 in range(PAIRS)], cols)
    sub = lax.broadcasted_iota(I32, (ROWS, WINDOW), 0)
    for n in range(X):
        rows = slice(ROWS * n, ROWS * (n + 1))
        res = jnp.dot(ms[rows], ff_out[...], preferred_element_type=F32)
        res = jnp.where(sub < ROWS - REM, res, flag_s[0:1, 0:1]).astype(BF16)
        part[0, n] = res[: ROWS // 2]
        part[1, n] = res[ROWS // 2 :]

    swap = pltpu.make_async_remote_copy(
        src_ref=part.at[1 - core], dst_ref=cbuf, send_sem=csend, recv_sem=crecv, device_id=sibling
    )
    swap.start()
    swap.wait_recv()
    for n in range(X):
        total = (part[core, n].astype(F32) + cbuf[n].astype(F32)).astype(BF16)
        send[n, 0] = total[:MAIN]
        send[n, 1] = total[MAIN:]

    for n in range(X):
        for h in range(2):
            to = reducer(n, h)

            @pl.when((n != x) | (to != r))
            def _():
                pltpu.make_async_remote_copy(
                    src_ref=send.at[n, h], dst_ref=rsbuf.at[y], send_sem=rsend, recv_sem=rrecv,
                    device_id=(n * Z + z, to),
                ).start()

    for d in (1, 3, 2):
        pltpu.make_async_remote_copy(
            src_ref=gbuf.at[x], dst_ref=gbuf.at[x], send_sem=xsend, recv_sem=xrecv.at[x],
            device_id=(((x + d) % X) * Z + z, r),
        ).start()
    assemble(m_out.at[x], blocks, [brow[X + x, i3] for i3 in range(PAIRS)], cols)

    own = origin == x

    @pl.when(own)
    def _():
        rsbuf[y] = send[x, mine_h]
        rest = rsbuf.at[pl.ds(0, R // 2 - 1)]
        pltpu.make_async_copy(rest, rest, rrecv).wait()
        pltpu.make_async_copy(rest, rest, rsend).wait()

    @pl.when(jnp.logical_not(own))
    def _():
        pltpu.make_async_copy(rsbuf, rsbuf, rrecv).wait()
        pltpu.make_async_copy(rsbuf, rsbuf, rsend).wait()

    total = rsbuf[0].astype(F32)
    for n in range(1, R // 2):
        total = total + rsbuf[n].astype(F32)
    inter_s[chunk] = total.astype(BF16)

    @pl.loop(0, R // 2 - 1)
    def _(n):
        near = (R // 4) - (n + 1) // 2
        to = (y + jnp.where(n % 2 == 0, near, R // 2 - near)) % (R // 2)
        pltpu.make_async_remote_copy(
            src_ref=inter_s.at[chunk], dst_ref=inter_s.at[chunk], send_sem=gsend, recv_sem=grecv.at[y],
            device_id=(t, 2 * to + core),
        ).start()

    def hand_on(slot):
        pltpu.make_async_remote_copy(
            src_ref=inter_s.at[slot], dst_ref=inter_s.at[slot], send_sem=fsend, recv_sem=frecv,
            device_id=sibling,
        ).start()

    hand_on(chunk)

    for d in (1, 3, 2):
        xs = (x + d) % X
        pltpu.make_async_copy(gbuf.at[xs], gbuf.at[xs], xrecv.at[xs]).wait()
        assemble(
            m_out.at[xs], [gbuf[xs, n] for n in range(Z)], [brow[X + xs, i3] for i3 in range(PAIRS)], cols
        )

    saves[3].start()

    @pl.loop(0, R // 2 - 1)
    def _(n):
        near = n // 2 + 1
        source = (y + jnp.where(n % 2 == 0, near, R // 2 - near)) % (R // 2)
        slot = 4 * ((source // 2 - x + X) % X) + 2 * core + source % 2
        pltpu.make_async_copy(inter_s.at[slot], inter_s.at[slot], grecv.at[source]).wait()
        hand_on(slot)

    others = inter_s.at[pl.ds(0, R // 2)]
    pltpu.make_async_copy(others, others, frecv).wait()
    saves[4].start()
    flag_out[0] = jnp.max(inter_s[3].astype(F32)[15:16, 0:128])

    sent = pk.at[pl.ds(0, Z - 1)]
    pltpu.make_async_copy(sent, sent, zsend).wait()
    sent = gbuf.at[pl.ds(0, X - 1)]
    pltpu.make_async_copy(sent, sent, xsend).wait()
    swap.wait_send()
    sent = inter_s.at[pl.ds(0, R // 2 - 1)]
    pltpu.make_async_copy(sent, sent, gsend).wait()
    pltpu.make_async_copy(others, others, fsend).wait()
    for copy in saves:
        copy.wait()


def exchange(amplitudes, occ_energy, vir_energy, occ_irrep, vir_irrep, factors):
    hbm = pl.BlockSpec(memory_space=pl.ANY)
    smem = pl.BlockSpec(memory_space=pltpu.SMEM)
    shapes = [
        ((X, ROWS, COLS), BF16),
        ((R, MAIN, WINDOW), BF16),
        ((COLS, WINDOW), BF16),
        ((2, X, ROWS, 128), F32),
        ((3, 8, COLS), F32),
    ]
    dma = pltpu.SemaphoreType.DMA
    return pl.pallas_call(
        exchange_kernel,
        out_shape=[jax.ShapeDtypeStruct(*s) for s in shapes] + [jax.ShapeDtypeStruct((1,), F32)],
        in_specs=[hbm] * 6,
        out_specs=[hbm] * 5 + [smem],
        scratch_shapes=[
            pltpu.VMEM((PAIRS, WIDTH, X * FOLD), BF16),
            pltpu.VMEM((OCC, WIDTH, NAUX), BF16),
            pltpu.VMEM((1, X * FOLD), I32),
            pltpu.VMEM((1, X * FOLD), F32),
            pltpu.SMEM((OCC,), I32),
            pltpu.SMEM((OCC,), F32),
            pltpu.VMEM((X, ROWS, COLS), BF16),
            pltpu.VMEM((COLS, WINDOW), BF16),
            pltpu.VMEM((2, X, ROWS, 128), F32),
            pltpu.VMEM((3, 8, COLS), F32),
            pltpu.VMEM((FOLD, 256), F32),
            pltpu.VMEM((Z, MAIN, 256), BF16),
            pltpu.VMEM((X, Z, MAIN, 256), BF16),
            pltpu.VMEM((GROUPS, MAIN, 256), I32),
            pltpu.VMEM((2 * X, PAIRS, MAIN, 256), I32),
            pltpu.VMEM((X * ROWS, COLS), BF16),
            pltpu.VMEM((2, X, ROWS // 2, WINDOW), BF16),
            pltpu.VMEM((X, ROWS // 2, WINDOW), BF16),
            pltpu.VMEM((X, 2, MAIN, WINDOW), BF16),
            pltpu.VMEM((R // 2, MAIN, WINDOW), BF16),
            pltpu.VMEM((R, MAIN, WINDOW), BF16),
            pltpu.VMEM((8, 128), F32),
            dma((PAIRS + 5,)), dma((5,)), dma, dma, dma, dma((X,)), dma, dma, dma, dma, dma, dma((R // 2,)), dma, dma,
        ],
        compiler_params=pltpu.CompilerParams(
            collective_id=0, has_side_effects=True, vmem_limit_bytes=62 * 1024 * 1024
        ),
        name="exchange",
    )(
        amplitudes.transpose(0, 2, 1), factors, vir_irrep.reshape(1, -1), vir_energy.reshape(1, -1),
        occ_irrep, occ_energy,
    )


def finish_kernel(m_ref, inter_ref, ff_ref, rows_ref, cols_ref, out_hbm, out, res, sem):
    for n in range(X):
        inter = jnp.concatenate([inter_ref[4 * n + c] for c in range(4)], axis=0)
        cycle = lax.dot_general(inter, ff_ref[...], (((1,), (1,)), ((), ())), preferred_element_type=F32)
        rlab = jnp.concatenate([rows_ref[0, n]] * 2, axis=1)
        ren = jnp.concatenate([rows_ref[1, n]] * 2, axis=1)
        for g in range(GROUPS):
            cols = slice(256 * g, 256 * (g + 1))
            denom = ren + cols_ref[1, 0:1, cols] - cols_ref[2, 0:1, cols]
            value = m_ref[n, :, cols].astype(F32) + cycle[:, cols] / denom
            res[:, cols] = jnp.where(rlab == cols_ref[0, 0:1, cols], value, 0.0)
        for i3 in range(PAIRS):
            i = PAIRS * n + i3
            for j in range(OCC):
                base = 256 * (j // PAIRS) + 64 * (j % PAIRS)
                out[i, j, 0:MAIN, :] = res[MAIN * i3 : MAIN * (i3 + 1), base : base + WIDTH]
                rem = MAIN * PAIRS + REM * i3
                out[i, j, MAIN:SLAB, :] = res[rem : rem + REM, base : base + WIDTH]
        done = pl.ds(PAIRS * n, PAIRS)
        pltpu.make_async_copy(out.at[done], out_hbm.at[done], sem.at[n]).start()
    for n in range(X):
        done = pl.ds(PAIRS * n, PAIRS)
        pltpu.make_async_copy(out.at[done], out_hbm.at[done], sem.at[n]).wait()


def finish(*operands):
    vmem = pl.BlockSpec(memory_space=pltpu.VMEM)
    out = pl.pallas_call(
        finish_kernel,
        out_shape=jax.ShapeDtypeStruct((OCC, OCC, SLAB, WIDTH), F32),
        in_specs=[vmem] * 5,
        out_specs=pl.BlockSpec(memory_space=pltpu.HBM),
        scratch_shapes=[
            pltpu.VMEM((OCC, OCC, SLAB, WIDTH), F32),
            pltpu.VMEM((ROWS, COLS), F32),
            pltpu.SemaphoreType.DMA((X,)),
        ],
        compiler_params=pltpu.CompilerParams(vmem_limit_bytes=62 * 1024 * 1024),
        name="finish",
    )(*operands)
    return out.transpose(0, 2, 1, 3)


def per_device(*arguments):
    *operands, flag = exchange(*arguments)
    return lax.cond(flag[0] == 0.0, lambda: finish(*operands), lambda: dense_path(*arguments))


def solution(mesh):
    return jax.shard_map(
        per_device,
        mesh=mesh,
        in_specs=(P("tile", None, "rep"), P(), P(), P(), P(), P(None, "rep", None)),
        out_specs=P(None, "tile", None, "rep"),
        check_vma=False,
    )
```

```python
import functools

import jax
import jax.numpy as jnp
from jax import lax
from jax.experimental import pallas as pl
from jax.experimental.pallas import tpu as pltpu
from jax.sharding import PartitionSpec as P

X, Z, R = 4, 12, 16
OCC = 12
SLAB = 20
WIDTH = 60
PAIRS = 3
GROUPS = 4
FOLD = SLAB * Z
NAUX = 2048
WINDOW = 384
COLS = GROUPS * 256
ROWS = 64
MAIN = 16
REM = SLAB - MAIN
F32, BF16, I32 = jnp.float32, jnp.bfloat16, jnp.int32


def sum_over_rep(partial_value):
    count = lax.axis_size("rep")
    blocks = partial_value.reshape(count, -1, partial_value.shape[1])
    blocks = lax.all_to_all(blocks, "rep", split_axis=0, concat_axis=0, tiled=True)
    total = jnp.sum(blocks.astype(jnp.float32), axis=0).astype(jnp.bfloat16)
    total = jnp.broadcast_to(total[None], blocks.shape)
    total = lax.all_to_all(total, "rep", split_axis=0, concat_axis=0, tiled=True)
    return total.reshape(partial_value.shape)


def dense_path(amplitudes, occ_energy, vir_energy, occ_irrep, vir_irrep, factors):
    tile_count = lax.axis_size("tile")
    occ_count = occ_energy.shape[0]
    vir_count = vir_energy.shape[0]
    first_width = vir_count // tile_count
    second_width = amplitudes.shape[2]
    relaid = lax.all_to_all(amplitudes, "tile", split_axis=1, concat_axis=0, tiled=True)
    relaid = relaid.reshape(occ_count, occ_count, first_width, second_width).transpose(0, 2, 1, 3)
    matrix = relaid.reshape(occ_count * first_width, occ_count * second_width)
    factor_rows = factors.reshape(occ_count * second_width, factors.shape[2])
    partial_value = jnp.dot(matrix, factor_rows, preferred_element_type=jnp.float32)
    inter = sum_over_rep(partial_value.astype(jnp.bfloat16))
    cycle = jnp.einsum("mq,nq->mn", inter, factor_rows, preferred_element_type=jnp.float32)
    cycle = cycle.reshape(occ_count, first_width, occ_count, second_width)
    tile_start = lax.axis_index("tile") * first_width
    rep_start = lax.axis_index("rep") * second_width
    vir_first = lax.dynamic_slice_in_dim(vir_energy, tile_start, first_width)
    vir_second = lax.dynamic_slice_in_dim(vir_energy, rep_start, second_width)
    irrep_first = lax.dynamic_slice_in_dim(vir_irrep, tile_start, first_width)
    irrep_second = lax.dynamic_slice_in_dim(vir_irrep, rep_start, second_width)
    denom = (
        occ_energy[:, None, None, None]
        - vir_first[None, :, None, None]
        + occ_energy[None, None, :, None]
        - vir_second[None, None, None, :]
    )
    symmetry = jnp.bitwise_xor(
        jnp.bitwise_xor(occ_irrep[:, None, None, None], irrep_first[None, :, None, None]),
        jnp.bitwise_xor(occ_irrep[None, None, :, None], irrep_second[None, None, None, :]),
    )
    return jnp.where(symmetry == 0, relaid.astype(jnp.float32) + cycle / denom, jnp.float32(0.0))


def lane_iota(rows):
    return lax.broadcasted_iota(I32, (rows, 128), 1)


def assemble(dst, blocks, rows, bcol):
    low = lane_iota(MAIN) < 64
    for g in range(GROUPS):
        cols = slice(256 * g, 256 * (g + 1))
        kept = [
            jnp.where(rows[i3] == bcol[g], blocks[GROUPS * i3 + g].astype(F32), 0.0) for i3 in range(PAIRS)
        ]
        for i3 in range(PAIRS):
            dst[MAIN * i3 : MAIN * (i3 + 1), cols] = kept[i3].astype(BF16)
        pieces = []
        for j in range(PAIRS):
            rem = [v[REM * j : REM * (j + 1), 128:256] for v in kept]
            pieces.append(jnp.concatenate(rem + [jnp.zeros((REM, 128), F32)], axis=0))
        left = jnp.where(low, pltpu.roll(pieces[0], 64, 1), pieces[1])
        right = jnp.where(low, pltpu.roll(pieces[2], 64, 1), 0.0)
        dst[MAIN * PAIRS : ROWS, cols] = jnp.concatenate([left, right], axis=1).astype(BF16)


def block_rows(lab, occ):
    main = jnp.broadcast_to(jnp.bitwise_xor(lab[:MAIN], occ), (MAIN, 128))
    rem = jnp.bitwise_xor(lab[MAIN:SLAB], occ)
    rem = jnp.concatenate([rem] * PAIRS + [jnp.full((MAIN - PAIRS * REM, 1), -1, I32)], axis=0)
    right = jnp.where(lane_iota(MAIN) < 64, main, jnp.broadcast_to(rem, (MAIN, 128)))
    return jnp.concatenate([main, right], axis=1)


def exchange_kernel(
    amp_hbm, fac_hbm, vir_irrep_hbm, vir_energy_hbm, occ_irrep_hbm, occ_energy_hbm,
    m_out, inter_out, ff_out, rows_out, cols_out, flag_out,
    amp_v, fac_v, vir_irrep, vir_energy, occ_irrep, occ_energy, pkf, pk, gbuf, bcol, brow, ms, part, cbuf, send, rsbuf, inter_s, flag_s,
    load_sem, zsend, zrecv, xsend, xrecv, csend, crecv, rsend, rrecv, gsend, grecv, fsend, frecv,
):
    t = lax.axis_index("tile")
    r = lax.axis_index("rep")
    x = t // Z
    z = t % Z
    y = r // 2
    core = r % 2
    sibling = (t, 2 * y + 1 - core)

    loads = [pltpu.make_async_copy(amp_hbm.at[j], amp_v.at[j], load_sem.at[j]) for j in range(PAIRS)]
    loads.append(pltpu.make_async_copy(fac_hbm, fac_v, load_sem.at[PAIRS]))
    small = [
        (vir_irrep_hbm, vir_irrep), (vir_energy_hbm, vir_energy),
        (occ_irrep_hbm, occ_irrep), (occ_energy_hbm, occ_energy),
    ]
    small = [pltpu.make_async_copy(a, b, load_sem.at[PAIRS + 1 + n]) for n, (a, b) in enumerate(small)]
    barrier = pltpu.get_barrier_semaphore()

    def z_peer(n):
        near = Z // 2 - (n + 1) // 2
        return (z + jnp.where(n % 2 == 0, near, Z - near)) % Z

    @pl.loop(0, Z - 1)
    def _(n):
        pl.semaphore_signal(barrier, inc=1, device_id=(x * Z + z_peer(n), r))

    for copy in loads[:PAIRS] + small + loads[PAIRS:]:
        copy.start()

    def reducer(d, h):
        return 2 * (2 * ((x + d) % X) + h) + core

    origin = (y // 2 - x + X) % X
    mine_h = y % 2
    chunk = 4 * origin + 2 * core + mine_h

    @pl.loop(0, X)
    def _(d):
        @pl.loop(0, R // 2)
        def _(n):
            @pl.when((d != x) | (n != y))
            def _():
                pl.semaphore_signal(barrier, inc=1, device_id=(d * Z + z, 2 * n + core))

    pl.semaphore_signal(barrier, inc=1, device_id=sibling)

    pkf[...] = jnp.zeros_like(pkf)
    row = lax.broadcasted_iota(I32, (FOLD, 1), 0)
    rem_row = row - MAIN * Z
    target = jnp.where(
        row < MAIN * Z,
        SLAB * (row >> 4) + (row & 15),
        SLAB * (rem_row >> 2) + MAIN + (rem_row & 3),
    )
    lane = lax.broadcasted_iota(I32, (1, X * FOLD), 1)
    folded_lane = lane
    for n in range(1, X):
        folded_lane = folded_lane - jnp.where(lane >= n * FOLD, FOLD, 0)
    pick = jnp.where(target == folded_lane, 1.0, 0.0).astype(BF16)
    for j in range(PAIRS):
        loads[j].wait()
        folded = lax.dot_general(pick, amp_v[j], (((1,), (1,)), ((), ())), preferred_element_type=F32)
        pkf[:, 64 * j : 64 * j + WIDTH] = folded
    for n in range(Z):
        pk[n, :, 0:128] = pkf[MAIN * n : MAIN * (n + 1), 0:128].astype(BF16)
        base = MAIN * Z + REM * n
        rem_rows = [pkf[base : base + REM, 128 * (j // 2) : 128 * (j // 2) + 128] for j in range(PAIRS)]
        rem_rows = [rem_rows[0], pltpu.roll(rem_rows[1], 64, 1), rem_rows[2]]
        rem = jnp.concatenate(rem_rows + [jnp.zeros((MAIN - PAIRS * REM, 128), F32)], axis=0)
        rem = jnp.where(lane_iota(MAIN) < 64, rem, 0.0)
        right = pkf[MAIN * n : MAIN * (n + 1), 128:256] + pltpu.roll(rem, 64, 1)
        pk[n, :, 128:256] = right.astype(BF16)

    pl.semaphore_wait(barrier, Z - 1 + X * (R // 2) - 1 + 1)

    @pl.loop(0, Z - 1)
    def _(n):
        to = z_peer(n)
        pltpu.make_async_remote_copy(
            src_ref=pk.at[to], dst_ref=gbuf.at[x, z], send_sem=zsend, recv_sem=zrecv,
            device_id=(x * Z + to, r),
        ).start()

    gbuf[x, z] = pk[z]

    for copy in small:
        copy.wait()
    vlane = lax.broadcasted_iota(I32, (24, X * FOLD), 1)
    vsub = lax.broadcasted_iota(I32, (24, X * FOLD), 0)
    virs = vir_irrep[...].astype(F32)

    def slab_values(tile, values):
        return jnp.sum(jnp.where(vlane == SLAB * tile + vsub, values, 0.0), axis=1, keepdims=True)

    for n in range(X):
        lab = slab_values(n * Z + z, virs).astype(I32)
        for i3 in range(PAIRS):
            brow[n, i3] = block_rows(lab, occ_irrep[PAIRS * x + i3])
    va_lab = slab_values(t, virs).astype(I32)
    va_en = slab_values(t, vir_energy[...])
    for i in range(OCC):
        n, i3 = i // PAIRS, i % PAIRS
        brow[X + n, i3] = block_rows(va_lab, occ_irrep[i])
        lab = jnp.broadcast_to(jnp.bitwise_xor(va_lab, occ_irrep[i]).astype(F32), (24, 128))
        en = jnp.broadcast_to(occ_energy[i] - va_en, (24, 128))
        rows_out[0, n, MAIN * i3 : MAIN * (i3 + 1), :] = lab[:MAIN]
        rows_out[0, n, MAIN * PAIRS + REM * i3 : MAIN * PAIRS + REM * (i3 + 1), :] = lab[MAIN:SLAB]
        rows_out[1, n, MAIN * i3 : MAIN * (i3 + 1), :] = en[:MAIN]
        rows_out[1, n, MAIN * PAIRS + REM * i3 : MAIN * PAIRS + REM * (i3 + 1), :] = en[MAIN:SLAB]
    for n in range(X):
        rows_out[0, n, ROWS - REM : ROWS, :] = jnp.full((REM, 128), -1.0, F32)
        rows_out[1, n, ROWS - REM : ROWS, :] = jnp.zeros((REM, 128), F32)

    pad = jnp.zeros((8, 1024 - X * FOLD), F32)
    shift = (1024 - WIDTH * r) % 1024
    lane8 = lane_iota(8)
    half = lane8 & 63

    def columns(values):
        whole = jnp.concatenate([jnp.broadcast_to(values, (8, X * FOLD)), pad], axis=1)
        mine = jnp.where(lane8 < WIDTH, pltpu.roll(whole, shift, 1)[:, :128], 0.0)
        return mine + pltpu.roll(mine, 64, 1)

    vb_lab = columns(virs).astype(I32)
    vb_en = columns(vir_energy[...])
    sub16 = lax.broadcasted_iota(I32, (MAIN, 128), 0)
    vb_lab16 = jnp.concatenate([vb_lab, vb_lab], axis=0)
    for g in range(GROUPS):
        for h in range(2):
            first = PAIRS * g + 2 * h
            second = min(first + 1, PAIRS * g + 2)
            cols = slice(256 * g + 128 * h, 256 * g + 128 * h + 128)
            lab = jnp.bitwise_xor(vb_lab, jnp.where(lane8 < 64, occ_irrep[first], occ_irrep[second]))
            lab = jnp.where(half < WIDTH, lab, -2)
            cols_out[0, :, cols] = jnp.where((lane8 < 64) | (h == 0), lab, -2).astype(F32)
            cols_out[1, :, cols] = jnp.where(lane8 < 64, occ_energy[first], occ_energy[second])
            cols_out[2, :, cols] = vb_en
            lab = jnp.concatenate([lab, lab], axis=0)
            if h == 1:
                occ = [occ_irrep[PAIRS * g + j] for j in range(PAIRS)]
                occ = jnp.where(sub16 < REM, occ[0], jnp.where(sub16 < 2 * REM, occ[1], occ[2]))
                rem = jnp.where((lane_iota(MAIN) & 63) < WIDTH, jnp.bitwise_xor(vb_lab16, occ), -2)
                lab = jnp.where(lane_iota(MAIN) < 64, lab, rem)
            bcol[g, :, 128 * h : 128 * h + 128] = lab


    loads[PAIRS].wait()
    zero4 = jnp.zeros((64 - WIDTH, WINDOW), F32)
    for g in range(GROUPS):
        ff_out[256 * g + 192 : 256 * (g + 1), :] = jnp.zeros((64, WINDOW), BF16)
    for k in range(OCC):
        base = 256 * (k // PAIRS) + 64 * (k % PAIRS)
        total = fac_v[k, :, 0:WINDOW].astype(F32)
        for n in range(1, NAUX // WINDOW):
            total = total + fac_v[k, :, WINDOW * n : WINDOW * (n + 1)].astype(F32)
        last = NAUX // WINDOW * WINDOW
        tail = fac_v[k, :, last:NAUX].astype(F32)
        total = total + jnp.concatenate([tail, jnp.zeros((WIDTH, WINDOW - NAUX + last), F32)], axis=1)
        ff_out[base : base + 64, :] = jnp.concatenate([total, zero4], axis=0).astype(BF16)

    vlane8 = lax.broadcasted_iota(I32, (8, X * FOLD), 1)
    vsub8 = lax.broadcasted_iota(I32, (8, X * FOLD), 0)
    first_lab = jnp.sum(
        jnp.where(vlane8 == WIDTH * r + vsub8, virs, 0.0), axis=1, keepdims=True
    ).astype(I32)
    seen = jnp.zeros((8, NAUX), I32)
    for k in range(OCC):
        bit = jnp.left_shift(jnp.int32(1), jnp.bitwise_xor(first_lab, occ_irrep[k]))
        seen = jnp.bitwise_or(seen, jnp.where(fac_v[k, 0:16, :].astype(F32)[0:8] != 0.0, bit, 0))
    for n in (4, 2, 1):
        seen = jnp.bitwise_or(seen, pltpu.roll(seen, n, 0))
    seen = seen[0:1]
    bad = jnp.zeros((1, 1), F32)
    covered = jnp.zeros((1, 1), F32)
    for h in range(8):
        aux_size = jnp.sum(jnp.where(seen == (1 << h), 1.0, 0.0), axis=1, keepdims=True)
        vir_size = jnp.sum(jnp.where(vir_irrep[...] == h, 1.0, 0.0), axis=1, keepdims=True)
        covered = covered + aux_size
        bad = bad + jnp.where(aux_size > WINDOW, 1.0, 0.0) + jnp.where(vir_size > FOLD, 1.0, 0.0)
    bad = bad + jnp.where(covered != NAUX, 1.0, 0.0)
    flag_s[...] = jnp.broadcast_to(jnp.where(bad > 0.0, 1.0, 0.0), (8, 128))

    peers = gbuf.at[x, pl.ds(0, Z - 1)]
    pltpu.make_async_copy(peers, peers, zrecv).wait()
    blocks = [gbuf[x, n] for n in range(Z)]
    cols = [bcol[g] for g in range(GROUPS)]
    for n in range(X):
        assemble(ms.at[pl.ds(ROWS * n, ROWS)], blocks, [brow[n, i3] for i3 in range(PAIRS)], cols)
    sub = lax.broadcasted_iota(I32, (ROWS, WINDOW), 0)
    for n in range(X):
        rows = slice(ROWS * n, ROWS * (n + 1))
        res = jnp.dot(ms[rows], ff_out[...], preferred_element_type=F32)
        res = jnp.where(sub < ROWS - REM, res, flag_s[0:1, 0:1]).astype(BF16)
        part[0, n] = res[: ROWS // 2]
        part[1, n] = res[ROWS // 2 :]

    swap = pltpu.make_async_remote_copy(
        src_ref=part.at[1 - core], dst_ref=cbuf, send_sem=csend, recv_sem=crecv, device_id=sibling
    )
    swap.start()
    swap.wait_recv()
    for n in range(X):
        total = (part[core, n].astype(F32) + cbuf[n].astype(F32)).astype(BF16)
        send[n, 0] = total[:MAIN]
        send[n, 1] = total[MAIN:]

    for n in range(X):
        for h in range(2):
            to = reducer(n, h)

            @pl.when((n != x) | (to != r))
            def _():
                pltpu.make_async_remote_copy(
                    src_ref=send.at[n, h], dst_ref=rsbuf.at[y], send_sem=rsend, recv_sem=rrecv,
                    device_id=(n * Z + z, to),
                ).start()

    for d in (1, 3, 2):
        pltpu.make_async_remote_copy(
            src_ref=gbuf.at[x], dst_ref=gbuf.at[x], send_sem=xsend, recv_sem=xrecv.at[x],
            device_id=(((x + d) % X) * Z + z, r),
        ).start()
    assemble(m_out.at[x], blocks, [brow[X + x, i3] for i3 in range(PAIRS)], cols)

    own = origin == x

    @pl.when(own)
    def _():
        rsbuf[y] = send[x, mine_h]
        rest = rsbuf.at[pl.ds(0, R // 2 - 1)]
        pltpu.make_async_copy(rest, rest, rrecv).wait()
        pltpu.make_async_copy(rest, rest, rsend).wait()

    @pl.when(jnp.logical_not(own))
    def _():
        pltpu.make_async_copy(rsbuf, rsbuf, rrecv).wait()
        pltpu.make_async_copy(rsbuf, rsbuf, rsend).wait()

    total = rsbuf[0].astype(F32)
    for n in range(1, R // 2):
        total = total + rsbuf[n].astype(F32)
    inter_s[chunk] = total.astype(BF16)

    @pl.loop(0, R // 2 - 1)
    def _(n):
        near = (R // 4) - (n + 1) // 2
        to = (y + jnp.where(n % 2 == 0, near, R // 2 - near)) % (R // 2)
        pltpu.make_async_remote_copy(
            src_ref=inter_s.at[chunk], dst_ref=inter_s.at[chunk], send_sem=gsend, recv_sem=grecv.at[y],
            device_id=(t, 2 * to + core),
        ).start()

    def hand_on(slot):
        pltpu.make_async_remote_copy(
            src_ref=inter_s.at[slot], dst_ref=inter_s.at[slot], send_sem=fsend, recv_sem=frecv,
            device_id=sibling,
        ).start()

    hand_on(chunk)

    for d in (1, 3, 2):
        xs = (x + d) % X
        pltpu.make_async_copy(gbuf.at[xs], gbuf.at[xs], xrecv.at[xs]).wait()
        assemble(
            m_out.at[xs], [gbuf[xs, n] for n in range(Z)], [brow[X + xs, i3] for i3 in range(PAIRS)], cols
        )

    @pl.loop(0, R // 2 - 1)
    def _(n):
        near = n // 2 + 1
        source = (y + jnp.where(n % 2 == 0, near, R // 2 - near)) % (R // 2)
        slot = 4 * ((source // 2 - x + X) % X) + 2 * core + source % 2
        pltpu.make_async_copy(inter_s.at[slot], inter_s.at[slot], grecv.at[source]).wait()
        hand_on(slot)

    others = inter_s.at[pl.ds(0, R // 2)]
    pltpu.make_async_copy(others, others, frecv).wait()
    inter_out[...] = inter_s[...]
    flag_out[0] = jnp.max(inter_s[3].astype(F32)[15:16, 0:128])

    sent = pk.at[pl.ds(0, Z - 1)]
    pltpu.make_async_copy(sent, sent, zsend).wait()
    sent = gbuf.at[pl.ds(0, X - 1)]
    pltpu.make_async_copy(sent, sent, xsend).wait()
    swap.wait_send()
    sent = inter_s.at[pl.ds(0, R // 2 - 1)]
    pltpu.make_async_copy(sent, sent, gsend).wait()
    pltpu.make_async_copy(others, others, fsend).wait()


def exchange(amplitudes, occ_energy, vir_energy, occ_irrep, vir_irrep, factors):
    hbm = pl.BlockSpec(memory_space=pl.ANY)
    smem = pl.BlockSpec(memory_space=pltpu.SMEM)
    shapes = [
        ((X, ROWS, COLS), BF16),
        ((R, MAIN, WINDOW), BF16),
        ((COLS, WINDOW), BF16),
        ((2, X, ROWS, 128), F32),
        ((3, 8, COLS), F32),
    ]
    dma = pltpu.SemaphoreType.DMA
    return pl.pallas_call(
        exchange_kernel,
        out_shape=[pltpu.VMEM(*s) for s in shapes] + [jax.ShapeDtypeStruct((1,), F32)],
        in_specs=[hbm] * 6,
        out_specs=[pl.BlockSpec(memory_space=pltpu.VMEM)] * 5 + [smem],
        scratch_shapes=[
            pltpu.VMEM((PAIRS, WIDTH, X * FOLD), BF16),
            pltpu.VMEM((OCC, WIDTH, NAUX), BF16),
            pltpu.VMEM((1, X * FOLD), I32),
            pltpu.VMEM((1, X * FOLD), F32),
            pltpu.SMEM((OCC,), I32),
            pltpu.SMEM((OCC,), F32),
            pltpu.VMEM((FOLD, 256), F32),
            pltpu.VMEM((Z, MAIN, 256), BF16),
            pltpu.VMEM((X, Z, MAIN, 256), BF16),
            pltpu.VMEM((GROUPS, MAIN, 256), I32),
            pltpu.VMEM((2 * X, PAIRS, MAIN, 256), I32),
            pltpu.VMEM((X * ROWS, COLS), BF16),
            pltpu.VMEM((2, X, ROWS // 2, WINDOW), BF16),
            pltpu.VMEM((X, ROWS // 2, WINDOW), BF16),
            pltpu.VMEM((X, 2, MAIN, WINDOW), BF16),
            pltpu.VMEM((R // 2, MAIN, WINDOW), BF16),
            pltpu.VMEM((R, MAIN, WINDOW), BF16),
            pltpu.VMEM((8, 128), F32),
            dma((PAIRS + 5,)), dma, dma, dma, dma((X,)), dma, dma, dma, dma, dma, dma((R // 2,)), dma, dma,
        ],
        compiler_params=pltpu.CompilerParams(
            collective_id=0, has_side_effects=True, vmem_limit_bytes=24 * 1024 * 1024
        ),
        name="exchange",
    )(
        amplitudes.transpose(0, 2, 1), factors, vir_irrep.reshape(1, -1), vir_energy.reshape(1, -1),
        occ_irrep, occ_energy,
    )


def finish_kernel(m_ref, inter_ref, ff_ref, rows_ref, cols_ref, out_hbm, out, res, sem):
    for n in range(X):
        inter = jnp.concatenate([inter_ref[4 * n + c] for c in range(4)], axis=0)
        cycle = lax.dot_general(inter, ff_ref[...], (((1,), (1,)), ((), ())), preferred_element_type=F32)
        rlab = jnp.concatenate([rows_ref[0, n]] * 2, axis=1)
        ren = jnp.concatenate([rows_ref[1, n]] * 2, axis=1)
        for g in range(GROUPS):
            cols = slice(256 * g, 256 * (g + 1))
            denom = ren + cols_ref[1, 0:1, cols] - cols_ref[2, 0:1, cols]
            value = m_ref[n, :, cols].astype(F32) + cycle[:, cols] / denom
            res[:, cols] = jnp.where(rlab == cols_ref[0, 0:1, cols], value, 0.0)
        for i3 in range(PAIRS):
            i = PAIRS * n + i3
            for j in range(OCC):
                base = 256 * (j // PAIRS) + 64 * (j % PAIRS)
                out[i, j, 0:MAIN, :] = res[MAIN * i3 : MAIN * (i3 + 1), base : base + WIDTH]
                rem = MAIN * PAIRS + REM * i3
                out[i, j, MAIN:SLAB, :] = res[rem : rem + REM, base : base + WIDTH]
        done = pl.ds(PAIRS * n, PAIRS)
        pltpu.make_async_copy(out.at[done], out_hbm.at[done], sem.at[n]).start()
    for n in range(X):
        done = pl.ds(PAIRS * n, PAIRS)
        pltpu.make_async_copy(out.at[done], out_hbm.at[done], sem.at[n]).wait()


def finish(*operands):
    vmem = pl.BlockSpec(memory_space=pltpu.VMEM)
    out = pl.pallas_call(
        finish_kernel,
        out_shape=pltpu.HBM((OCC, OCC, SLAB, WIDTH), F32),
        in_specs=[vmem] * 5,
        out_specs=pl.BlockSpec(memory_space=pltpu.HBM),
        scratch_shapes=[
            pltpu.VMEM((OCC, OCC, SLAB, WIDTH), F32),
            pltpu.VMEM((ROWS, COLS), F32),
            pltpu.SemaphoreType.DMA((X,)),
        ],
        compiler_params=pltpu.CompilerParams(vmem_limit_bytes=24 * 1024 * 1024),
        name="finish",
    )(*operands)
    return out.transpose(0, 2, 1, 3)


def per_device(*arguments):
    *operands, flag = exchange(*arguments)
    return lax.cond(flag[0] == 0.0, lambda: finish(*operands), lambda: dense_path(*arguments))


def solution(mesh):
    return jax.shard_map(
        per_device,
        mesh=mesh,
        in_specs=(P("tile", None, "rep"), P(), P(), P(), P(), P(None, "rep", None)),
        out_specs=P(None, "tile", None, "rep"),
        check_vma=False,
    )
```

```python
import functools

import jax
import jax.numpy as jnp
from jax import lax
from jax.experimental import pallas as pl
from jax.experimental.pallas import tpu as pltpu
from jax.sharding import PartitionSpec as P

X, Z, R = 4, 12, 16
OCC = 12
SLAB = 20
WIDTH = 60
PAIRS = 3
GROUPS = 4
FOLD = SLAB * Z
NAUX = 2048
WINDOW = 384
COLS = GROUPS * 256
ROWS = 64
MAIN = 16
REM = SLAB - MAIN
F32, BF16, I32 = jnp.float32, jnp.bfloat16, jnp.int32


def sum_over_rep(partial_value):
    count = lax.axis_size("rep")
    blocks = partial_value.reshape(count, -1, partial_value.shape[1])
    blocks = lax.all_to_all(blocks, "rep", split_axis=0, concat_axis=0, tiled=True)
    total = jnp.sum(blocks.astype(jnp.float32), axis=0).astype(jnp.bfloat16)
    total = jnp.broadcast_to(total[None], blocks.shape)
    total = lax.all_to_all(total, "rep", split_axis=0, concat_axis=0, tiled=True)
    return total.reshape(partial_value.shape)


def dense_path(amplitudes, occ_energy, vir_energy, occ_irrep, vir_irrep, factors):
    tile_count = lax.axis_size("tile")
    occ_count = occ_energy.shape[0]
    vir_count = vir_energy.shape[0]
    first_width = vir_count // tile_count
    second_width = amplitudes.shape[2]
    relaid = lax.all_to_all(amplitudes, "tile", split_axis=1, concat_axis=0, tiled=True)
    relaid = relaid.reshape(occ_count, occ_count, first_width, second_width).transpose(0, 2, 1, 3)
    matrix = relaid.reshape(occ_count * first_width, occ_count * second_width)
    factor_rows = factors.reshape(occ_count * second_width, factors.shape[2])
    partial_value = jnp.dot(matrix, factor_rows, preferred_element_type=jnp.float32)
    inter = sum_over_rep(partial_value.astype(jnp.bfloat16))
    cycle = jnp.einsum("mq,nq->mn", inter, factor_rows, preferred_element_type=jnp.float32)
    cycle = cycle.reshape(occ_count, first_width, occ_count, second_width)
    tile_start = lax.axis_index("tile") * first_width
    rep_start = lax.axis_index("rep") * second_width
    vir_first = lax.dynamic_slice_in_dim(vir_energy, tile_start, first_width)
    vir_second = lax.dynamic_slice_in_dim(vir_energy, rep_start, second_width)
    irrep_first = lax.dynamic_slice_in_dim(vir_irrep, tile_start, first_width)
    irrep_second = lax.dynamic_slice_in_dim(vir_irrep, rep_start, second_width)
    denom = (
        occ_energy[:, None, None, None]
        - vir_first[None, :, None, None]
        + occ_energy[None, None, :, None]
        - vir_second[None, None, None, :]
    )
    symmetry = jnp.bitwise_xor(
        jnp.bitwise_xor(occ_irrep[:, None, None, None], irrep_first[None, :, None, None]),
        jnp.bitwise_xor(occ_irrep[None, None, :, None], irrep_second[None, None, None, :]),
    )
    return jnp.where(symmetry == 0, relaid.astype(jnp.float32) + cycle / denom, jnp.float32(0.0))


def lane_iota(rows):
    return lax.broadcasted_iota(I32, (rows, 128), 1)


def assemble(dst, blocks, rows, bcol):
    low = lane_iota(MAIN) < 64
    for g in range(GROUPS):
        cols = slice(256 * g, 256 * (g + 1))
        kept = [
            jnp.where(rows[i3] == bcol[g], blocks[GROUPS * i3 + g].astype(F32), 0.0) for i3 in range(PAIRS)
        ]
        for i3 in range(PAIRS):
            dst[MAIN * i3 : MAIN * (i3 + 1), cols] = kept[i3].astype(BF16)
        pieces = []
        for j in range(PAIRS):
            rem = [v[REM * j : REM * (j + 1), 128:256] for v in kept]
            pieces.append(jnp.concatenate(rem + [jnp.zeros((REM, 128), F32)], axis=0))
        left = jnp.where(low, pltpu.roll(pieces[0], 64, 1), pieces[1])
        right = jnp.where(low, pltpu.roll(pieces[2], 64, 1), 0.0)
        dst[MAIN * PAIRS : ROWS, cols] = jnp.concatenate([left, right], axis=1).astype(BF16)


def block_rows(lab, occ):
    main = jnp.broadcast_to(jnp.bitwise_xor(lab[:MAIN], occ), (MAIN, 128))
    rem = jnp.bitwise_xor(lab[MAIN:SLAB], occ)
    rem = jnp.concatenate([rem] * PAIRS + [jnp.full((MAIN - PAIRS * REM, 1), -1, I32)], axis=0)
    right = jnp.where(lane_iota(MAIN) < 64, main, jnp.broadcast_to(rem, (MAIN, 128)))
    return jnp.concatenate([main, right], axis=1)


def exchange_kernel(
    amp_hbm, fac_hbm, vir_irrep_hbm, vir_energy_hbm, occ_irrep_hbm, occ_energy_hbm,
    m_out, inter_out, ff_out, rows_out, cols_out, flag_out,
    amp_v, fac_v, vir_irrep, vir_energy, occ_irrep, occ_energy, pkf, pk, gbuf, bcol, brow, ms, part, cbuf, send, rsbuf, inter_s, flag_s,
    load_sem, zsend, zrecv, xsend, xrecv, csend, crecv, rsend, rrecv, gsend, grecv, fsend, frecv,
):
    t = lax.axis_index("tile")
    r = lax.axis_index("rep")
    x = t // Z
    z = t % Z
    y = r // 2
    core = r % 2
    sibling = (t, 2 * y + 1 - core)

    loads = [pltpu.make_async_copy(amp_hbm.at[j], amp_v.at[j], load_sem.at[j]) for j in range(PAIRS)]
    loads.append(pltpu.make_async_copy(fac_hbm, fac_v, load_sem.at[PAIRS]))
    small = [
        (vir_irrep_hbm, vir_irrep), (vir_energy_hbm, vir_energy),
        (occ_irrep_hbm, occ_irrep), (occ_energy_hbm, occ_energy),
    ]
    small = [pltpu.make_async_copy(a, b, load_sem.at[PAIRS + 1 + n]) for n, (a, b) in enumerate(small)]
    barrier = pltpu.get_barrier_semaphore()

    def z_peer(n):
        near = Z // 2 - (n + 1) // 2
        return (z + jnp.where(n % 2 == 0, near, Z - near)) % Z

    @pl.loop(0, Z - 1)
    def _(n):
        pl.semaphore_signal(barrier, inc=1, device_id=(x * Z + z_peer(n), r))

    for copy in loads[:PAIRS] + small + loads[PAIRS:]:
        copy.start()

    def reducer(d, h):
        return 2 * (2 * ((x + d) % X) + h) + core

    origin = (y // 2 - x + X) % X
    mine_h = y % 2
    chunk = 4 * origin + 2 * core + mine_h

    @pl.loop(0, X)
    def _(d):
        @pl.loop(0, R // 2)
        def _(n):
            @pl.when((d != x) | (n != y))
            def _():
                pl.semaphore_signal(barrier, inc=1, device_id=(d * Z + z, 2 * n + core))

    pl.semaphore_signal(barrier, inc=1, device_id=sibling)

    pkf[...] = jnp.zeros_like(pkf)
    row = lax.broadcasted_iota(I32, (FOLD, 1), 0)
    rem_row = row - MAIN * Z
    target = jnp.where(
        row < MAIN * Z,
        SLAB * (row >> 4) + (row & 15),
        SLAB * (rem_row >> 2) + MAIN + (rem_row & 3),
    )
    lane = lax.broadcasted_iota(I32, (1, X * FOLD), 1)
    folded_lane = lane
    for n in range(1, X):
        folded_lane = folded_lane - jnp.where(lane >= n * FOLD, FOLD, 0)
    pick = jnp.where(target == folded_lane, 1.0, 0.0).astype(BF16)
    for j in range(PAIRS):
        loads[j].wait()
        folded = lax.dot_general(pick, amp_v[j], (((1,), (1,)), ((), ())), preferred_element_type=F32)
        pkf[:, 64 * j : 64 * j + WIDTH] = folded
    for n in range(Z):
        pk[n, :, 0:128] = pkf[MAIN * n : MAIN * (n + 1), 0:128].astype(BF16)
        base = MAIN * Z + REM * n
        rem_rows = [pkf[base : base + REM, 128 * (j // 2) : 128 * (j // 2) + 128] for j in range(PAIRS)]
        rem_rows = [rem_rows[0], pltpu.roll(rem_rows[1], 64, 1), rem_rows[2]]
        rem = jnp.concatenate(rem_rows + [jnp.zeros((MAIN - PAIRS * REM, 128), F32)], axis=0)
        rem = jnp.where(lane_iota(MAIN) < 64, rem, 0.0)
        right = pkf[MAIN * n : MAIN * (n + 1), 128:256] + pltpu.roll(rem, 64, 1)
        pk[n, :, 128:256] = right.astype(BF16)

    pl.semaphore_wait(barrier, Z - 1 + X * (R // 2) - 1 + 1)

    @pl.loop(0, Z - 1)
    def _(n):
        to = z_peer(n)
        pltpu.make_async_remote_copy(
            src_ref=pk.at[to], dst_ref=gbuf.at[x, z], send_sem=zsend, recv_sem=zrecv,
            device_id=(x * Z + to, r),
        ).start()

    gbuf[x, z] = pk[z]

    for copy in small:
        copy.wait()
    vlane = lax.broadcasted_iota(I32, (24, X * FOLD), 1)
    vsub = lax.broadcasted_iota(I32, (24, X * FOLD), 0)
    virs = vir_irrep[...].astype(F32)

    def slab_values(tile, values):
        return jnp.sum(jnp.where(vlane == SLAB * tile + vsub, values, 0.0), axis=1, keepdims=True)

    for n in range(X):
        lab = slab_values(n * Z + z, virs).astype(I32)
        for i3 in range(PAIRS):
            brow[n, i3] = block_rows(lab, occ_irrep[PAIRS * x + i3])
    va_lab = slab_values(t, virs).astype(I32)
    va_en = slab_values(t, vir_energy[...])
    for i in range(OCC):
        n, i3 = i // PAIRS, i % PAIRS
        brow[X + n, i3] = block_rows(va_lab, occ_irrep[i])
        lab = jnp.broadcast_to(jnp.bitwise_xor(va_lab, occ_irrep[i]).astype(F32), (24, 128))
        en = jnp.broadcast_to(occ_energy[i] - va_en, (24, 128))
        rows_out[0, n, MAIN * i3 : MAIN * (i3 + 1), :] = lab[:MAIN]
        rows_out[0, n, MAIN * PAIRS + REM * i3 : MAIN * PAIRS + REM * (i3 + 1), :] = lab[MAIN:SLAB]
        rows_out[1, n, MAIN * i3 : MAIN * (i3 + 1), :] = en[:MAIN]
        rows_out[1, n, MAIN * PAIRS + REM * i3 : MAIN * PAIRS + REM * (i3 + 1), :] = en[MAIN:SLAB]
    for n in range(X):
        rows_out[0, n, ROWS - REM : ROWS, :] = jnp.full((REM, 128), -1.0, F32)
        rows_out[1, n, ROWS - REM : ROWS, :] = jnp.zeros((REM, 128), F32)

    pad = jnp.zeros((8, 1024 - X * FOLD), F32)
    shift = (1024 - WIDTH * r) % 1024
    lane8 = lane_iota(8)
    half = lane8 & 63

    def columns(values):
        whole = jnp.concatenate([jnp.broadcast_to(values, (8, X * FOLD)), pad], axis=1)
        mine = jnp.where(lane8 < WIDTH, pltpu.roll(whole, shift, 1)[:, :128], 0.0)
        return mine + pltpu.roll(mine, 64, 1)

    vb_lab = columns(virs).astype(I32)
    vb_en = columns(vir_energy[...])
    sub16 = lax.broadcasted_iota(I32, (MAIN, 128), 0)
    vb_lab16 = jnp.concatenate([vb_lab, vb_lab], axis=0)
    for g in range(GROUPS):
        for h in range(2):
            first = PAIRS * g + 2 * h
            second = min(first + 1, PAIRS * g + 2)
            cols = slice(256 * g + 128 * h, 256 * g + 128 * h + 128)
            lab = jnp.bitwise_xor(vb_lab, jnp.where(lane8 < 64, occ_irrep[first], occ_irrep[second]))
            lab = jnp.where(half < WIDTH, lab, -2)
            cols_out[0, :, cols] = jnp.where((lane8 < 64) | (h == 0), lab, -2).astype(F32)
            cols_out[1, :, cols] = jnp.where(lane8 < 64, occ_energy[first], occ_energy[second])
            cols_out[2, :, cols] = vb_en
            lab = jnp.concatenate([lab, lab], axis=0)
            if h == 1:
                occ = [occ_irrep[PAIRS * g + j] for j in range(PAIRS)]
                occ = jnp.where(sub16 < REM, occ[0], jnp.where(sub16 < 2 * REM, occ[1], occ[2]))
                rem = jnp.where((lane_iota(MAIN) & 63) < WIDTH, jnp.bitwise_xor(vb_lab16, occ), -2)
                lab = jnp.where(lane_iota(MAIN) < 64, lab, rem)
            bcol[g, :, 128 * h : 128 * h + 128] = lab


    loads[PAIRS].wait()
    zero4 = jnp.zeros((64 - WIDTH, WINDOW), F32)
    for g in range(GROUPS):
        ff_out[256 * g + 192 : 256 * (g + 1), :] = jnp.zeros((64, WINDOW), BF16)
    for k in range(OCC):
        base = 256 * (k // PAIRS) + 64 * (k % PAIRS)
        total = fac_v[k, :, 0:WINDOW].astype(F32)
        for n in range(1, NAUX // WINDOW):
            total = total + fac_v[k, :, WINDOW * n : WINDOW * (n + 1)].astype(F32)
        last = NAUX // WINDOW * WINDOW
        tail = fac_v[k, :, last:NAUX].astype(F32)
        total = total + jnp.concatenate([tail, jnp.zeros((WIDTH, WINDOW - NAUX + last), F32)], axis=1)
        ff_out[base : base + 64, :] = jnp.concatenate([total, zero4], axis=0).astype(BF16)

    vlane8 = lax.broadcasted_iota(I32, (8, X * FOLD), 1)
    vsub8 = lax.broadcasted_iota(I32, (8, X * FOLD), 0)
    first_lab = jnp.sum(
        jnp.where(vlane8 == WIDTH * r + vsub8, virs, 0.0), axis=1, keepdims=True
    ).astype(I32)
    seen = jnp.zeros((8, NAUX), I32)
    for k in range(OCC):
        bit = jnp.left_shift(jnp.int32(1), jnp.bitwise_xor(first_lab, occ_irrep[k]))
        seen = jnp.bitwise_or(seen, jnp.where(fac_v[k, 0:16, :].astype(F32)[0:8] != 0.0, bit, 0))
    for n in (4, 2, 1):
        seen = jnp.bitwise_or(seen, pltpu.roll(seen, n, 0))
    seen = seen[0:1]
    bad = jnp.zeros((1, 1), F32)
    covered = jnp.zeros((1, 1), F32)
    for h in range(8):
        aux_size = jnp.sum(jnp.where(seen == (1 << h), 1.0, 0.0), axis=1, keepdims=True)
        vir_size = jnp.sum(jnp.where(vir_irrep[...] == h, 1.0, 0.0), axis=1, keepdims=True)
        covered = covered + aux_size
        bad = bad + jnp.where(aux_size > WINDOW, 1.0, 0.0) + jnp.where(vir_size > FOLD, 1.0, 0.0)
    bad = bad + jnp.where(covered != NAUX, 1.0, 0.0)
    flag_s[...] = jnp.broadcast_to(jnp.where(bad > 0.0, 1.0, 0.0), (8, 128))

    peers = gbuf.at[x, pl.ds(0, Z - 1)]
    pltpu.make_async_copy(peers, peers, zrecv).wait()
    blocks = [gbuf[x, n] for n in range(Z)]
    cols = [bcol[g] for g in range(GROUPS)]
    for n in range(X):
        assemble(ms.at[pl.ds(ROWS * n, ROWS)], blocks, [brow[n, i3] for i3 in range(PAIRS)], cols)
    sub = lax.broadcasted_iota(I32, (ROWS, WINDOW), 0)
    sums = jnp.dot(ms[...], ff_out[...], preferred_element_type=F32)
    for n in range(X):
        res = sums[ROWS * n : ROWS * (n + 1)]
        res = jnp.where(sub < ROWS - REM, res, flag_s[0:1, 0:1]).astype(BF16)
        part[0, n] = res[: ROWS // 2]
        part[1, n] = res[ROWS // 2 :]

    swap = pltpu.make_async_remote_copy(
        src_ref=part.at[1 - core], dst_ref=cbuf, send_sem=csend, recv_sem=crecv, device_id=sibling
    )
    swap.start()
    swap.wait_recv()
    for n in range(X):
        total = (part[core, n].astype(F32) + cbuf[n].astype(F32)).astype(BF16)
        send[n, 0] = total[:MAIN]
        send[n, 1] = total[MAIN:]

    for n in range(X):
        for h in range(2):
            to = reducer(n, h)

            @pl.when((n != x) | (to != r))
            def _():
                pltpu.make_async_remote_copy(
                    src_ref=send.at[n, h], dst_ref=rsbuf.at[y], send_sem=rsend, recv_sem=rrecv,
                    device_id=(n * Z + z, to),
                ).start()

    for d in (1, 3, 2):
        pltpu.make_async_remote_copy(
            src_ref=gbuf.at[x], dst_ref=gbuf.at[x], send_sem=xsend, recv_sem=xrecv.at[x],
            device_id=(((x + d) % X) * Z + z, r),
        ).start()
    assemble(m_out.at[x], blocks, [brow[X + x, i3] for i3 in range(PAIRS)], cols)

    own = origin == x

    @pl.when(own)
    def _():
        rsbuf[y] = send[x, mine_h]
        rest = rsbuf.at[pl.ds(0, R // 2 - 1)]
        pltpu.make_async_copy(rest, rest, rrecv).wait()
        pltpu.make_async_copy(rest, rest, rsend).wait()

    @pl.when(jnp.logical_not(own))
    def _():
        pltpu.make_async_copy(rsbuf, rsbuf, rrecv).wait()
        pltpu.make_async_copy(rsbuf, rsbuf, rsend).wait()

    total = rsbuf[0].astype(F32)
    for n in range(1, R // 2):
        total = total + rsbuf[n].astype(F32)
    inter_s[chunk] = total.astype(BF16)

    @pl.loop(0, R // 2 - 1)
    def _(n):
        near = (R // 4) - (n + 1) // 2
        to = (y + jnp.where(n % 2 == 0, near, R // 2 - near)) % (R // 2)
        pltpu.make_async_remote_copy(
            src_ref=inter_s.at[chunk], dst_ref=inter_s.at[chunk], send_sem=gsend, recv_sem=grecv.at[y],
            device_id=(t, 2 * to + core),
        ).start()

    def hand_on(slot):
        pltpu.make_async_remote_copy(
            src_ref=inter_s.at[slot], dst_ref=inter_s.at[slot], send_sem=fsend, recv_sem=frecv,
            device_id=sibling,
        ).start()

    hand_on(chunk)

    for d in (1, 3, 2):
        xs = (x + d) % X
        pltpu.make_async_copy(gbuf.at[xs], gbuf.at[xs], xrecv.at[xs]).wait()
        assemble(
            m_out.at[xs], [gbuf[xs, n] for n in range(Z)], [brow[X + xs, i3] for i3 in range(PAIRS)], cols
        )

    @pl.loop(0, R // 2 - 1)
    def _(n):
        near = n // 2 + 1
        source = (y + jnp.where(n % 2 == 0, near, R // 2 - near)) % (R // 2)
        slot = 4 * ((source // 2 - x + X) % X) + 2 * core + source % 2
        pltpu.make_async_copy(inter_s.at[slot], inter_s.at[slot], grecv.at[source]).wait()
        hand_on(slot)

    others = inter_s.at[pl.ds(0, R // 2)]
    pltpu.make_async_copy(others, others, frecv).wait()
    inter_out[...] = inter_s[...]
    flag_out[0] = jnp.max(inter_s[3].astype(F32)[15:16, 0:128])

    sent = pk.at[pl.ds(0, Z - 1)]
    pltpu.make_async_copy(sent, sent, zsend).wait()
    sent = gbuf.at[pl.ds(0, X - 1)]
    pltpu.make_async_copy(sent, sent, xsend).wait()
    swap.wait_send()
    sent = inter_s.at[pl.ds(0, R // 2 - 1)]
    pltpu.make_async_copy(sent, sent, gsend).wait()
    pltpu.make_async_copy(others, others, fsend).wait()


def exchange(amplitudes, occ_energy, vir_energy, occ_irrep, vir_irrep, factors):
    hbm = pl.BlockSpec(memory_space=pl.ANY)
    smem = pl.BlockSpec(memory_space=pltpu.SMEM)
    shapes = [
        ((X, ROWS, COLS), BF16),
        ((R, MAIN, WINDOW), BF16),
        ((COLS, WINDOW), BF16),
        ((2, X, ROWS, 128), F32),
        ((3, 8, COLS), F32),
    ]
    dma = pltpu.SemaphoreType.DMA
    return pl.pallas_call(
        exchange_kernel,
        out_shape=[pltpu.VMEM(*s) for s in shapes] + [jax.ShapeDtypeStruct((1,), F32)],
        in_specs=[hbm] * 6,
        out_specs=[pl.BlockSpec(memory_space=pltpu.VMEM)] * 5 + [smem],
        scratch_shapes=[
            pltpu.VMEM((PAIRS, WIDTH, X * FOLD), BF16),
            pltpu.VMEM((OCC, WIDTH, NAUX), BF16),
            pltpu.VMEM((1, X * FOLD), I32),
            pltpu.VMEM((1, X * FOLD), F32),
            pltpu.SMEM((OCC,), I32),
            pltpu.SMEM((OCC,), F32),
            pltpu.VMEM((FOLD, 256), F32),
            pltpu.VMEM((Z, MAIN, 256), BF16),
            pltpu.VMEM((X, Z, MAIN, 256), BF16),
            pltpu.VMEM((GROUPS, MAIN, 256), I32),
            pltpu.VMEM((2 * X, PAIRS, MAIN, 256), I32),
            pltpu.VMEM((X * ROWS, COLS), BF16),
            pltpu.VMEM((2, X, ROWS // 2, WINDOW), BF16),
            pltpu.VMEM((X, ROWS // 2, WINDOW), BF16),
            pltpu.VMEM((X, 2, MAIN, WINDOW), BF16),
            pltpu.VMEM((R // 2, MAIN, WINDOW), BF16),
            pltpu.VMEM((R, MAIN, WINDOW), BF16),
            pltpu.VMEM((8, 128), F32),
            dma((PAIRS + 5,)), dma, dma, dma, dma((X,)), dma, dma, dma, dma, dma, dma((R // 2,)), dma, dma,
        ],
        compiler_params=pltpu.CompilerParams(
            collective_id=0, has_side_effects=True, vmem_limit_bytes=24 * 1024 * 1024
        ),
        name="exchange",
    )(
        amplitudes.transpose(0, 2, 1), factors, vir_irrep.reshape(1, -1), vir_energy.reshape(1, -1),
        occ_irrep, occ_energy,
    )


def finish_kernel(m_ref, inter_ref, ff_ref, rows_ref, cols_ref, out_hbm, out, res, sem):
    inter = inter_ref[...].reshape(X * ROWS, WINDOW)
    whole = lax.dot_general(inter, ff_ref[...], (((1,), (1,)), ((), ())), preferred_element_type=F32)
    for n in range(X):
        cycle = whole[ROWS * n : ROWS * (n + 1)]
        rlab = jnp.concatenate([rows_ref[0, n]] * 2, axis=1)
        ren = jnp.concatenate([rows_ref[1, n]] * 2, axis=1)
        for g in range(GROUPS):
            cols = slice(256 * g, 256 * (g + 1))
            denom = ren + cols_ref[1, 0:1, cols] - cols_ref[2, 0:1, cols]
            value = m_ref[n, :, cols].astype(F32) + cycle[:, cols] / denom
            res[:, cols] = jnp.where(rlab == cols_ref[0, 0:1, cols], value, 0.0)
        for i3 in range(PAIRS):
            i = PAIRS * n + i3
            for j in range(OCC):
                base = 256 * (j // PAIRS) + 64 * (j % PAIRS)
                out[i, j, 0:MAIN, :] = res[MAIN * i3 : MAIN * (i3 + 1), base : base + WIDTH]
                rem = MAIN * PAIRS + REM * i3
                out[i, j, MAIN:SLAB, :] = res[rem : rem + REM, base : base + WIDTH]
        done = pl.ds(PAIRS * n, PAIRS)
        pltpu.make_async_copy(out.at[done], out_hbm.at[done], sem.at[n]).start()
    for n in range(X):
        done = pl.ds(PAIRS * n, PAIRS)
        pltpu.make_async_copy(out.at[done], out_hbm.at[done], sem.at[n]).wait()


def finish(*operands):
    vmem = pl.BlockSpec(memory_space=pltpu.VMEM)
    out = pl.pallas_call(
        finish_kernel,
        out_shape=pltpu.HBM((OCC, OCC, SLAB, WIDTH), F32),
        in_specs=[vmem] * 5,
        out_specs=pl.BlockSpec(memory_space=pltpu.HBM),
        scratch_shapes=[
            pltpu.VMEM((OCC, OCC, SLAB, WIDTH), F32),
            pltpu.VMEM((ROWS, COLS), F32),
            pltpu.SemaphoreType.DMA((X,)),
        ],
        compiler_params=pltpu.CompilerParams(vmem_limit_bytes=24 * 1024 * 1024),
        name="finish",
    )(*operands)
    return out.transpose(0, 2, 1, 3)


def per_device(*arguments):
    *operands, flag = exchange(*arguments)
    return lax.cond(flag[0] == 0.0, lambda: finish(*operands), lambda: dense_path(*arguments))


def solution(mesh):
    return jax.shard_map(
        per_device,
        mesh=mesh,
        in_specs=(P("tile", None, "rep"), P(), P(), P(), P(), P(None, "rep", None)),
        out_specs=P(None, "tile", None, "rep"),
        check_vma=False,
    )
```

```python
import functools

import jax
import jax.numpy as jnp
from jax import lax
from jax.experimental import pallas as pl
from jax.experimental.pallas import tpu as pltpu
from jax.sharding import PartitionSpec as P

X, Z, R = 4, 12, 16
OCC = 12
SLAB = 20
WIDTH = 60
PAIRS = 3
GROUPS = 4
FOLD = SLAB * Z
NAUX = 2048
WINDOW = 384
COLS = GROUPS * 256
ROWS = 64
MAIN = 16
REM = SLAB - MAIN
F32, BF16, I32 = jnp.float32, jnp.bfloat16, jnp.int32


def sum_over_rep(partial_value):
    count = lax.axis_size("rep")
    blocks = partial_value.reshape(count, -1, partial_value.shape[1])
    blocks = lax.all_to_all(blocks, "rep", split_axis=0, concat_axis=0, tiled=True)
    total = jnp.sum(blocks.astype(jnp.float32), axis=0).astype(jnp.bfloat16)
    total = jnp.broadcast_to(total[None], blocks.shape)
    total = lax.all_to_all(total, "rep", split_axis=0, concat_axis=0, tiled=True)
    return total.reshape(partial_value.shape)


def dense_path(amplitudes, occ_energy, vir_energy, occ_irrep, vir_irrep, factors):
    tile_count = lax.axis_size("tile")
    occ_count = occ_energy.shape[0]
    vir_count = vir_energy.shape[0]
    first_width = vir_count // tile_count
    second_width = amplitudes.shape[2]
    relaid = lax.all_to_all(amplitudes, "tile", split_axis=1, concat_axis=0, tiled=True)
    relaid = relaid.reshape(occ_count, occ_count, first_width, second_width).transpose(0, 2, 1, 3)
    matrix = relaid.reshape(occ_count * first_width, occ_count * second_width)
    factor_rows = factors.reshape(occ_count * second_width, factors.shape[2])
    partial_value = jnp.dot(matrix, factor_rows, preferred_element_type=jnp.float32)
    inter = sum_over_rep(partial_value.astype(jnp.bfloat16))
    cycle = jnp.einsum("mq,nq->mn", inter, factor_rows, preferred_element_type=jnp.float32)
    cycle = cycle.reshape(occ_count, first_width, occ_count, second_width)
    tile_start = lax.axis_index("tile") * first_width
    rep_start = lax.axis_index("rep") * second_width
    vir_first = lax.dynamic_slice_in_dim(vir_energy, tile_start, first_width)
    vir_second = lax.dynamic_slice_in_dim(vir_energy, rep_start, second_width)
    irrep_first = lax.dynamic_slice_in_dim(vir_irrep, tile_start, first_width)
    irrep_second = lax.dynamic_slice_in_dim(vir_irrep, rep_start, second_width)
    denom = (
        occ_energy[:, None, None, None]
        - vir_first[None, :, None, None]
        + occ_energy[None, None, :, None]
        - vir_second[None, None, None, :]
    )
    symmetry = jnp.bitwise_xor(
        jnp.bitwise_xor(occ_irrep[:, None, None, None], irrep_first[None, :, None, None]),
        jnp.bitwise_xor(occ_irrep[None, None, :, None], irrep_second[None, None, None, :]),
    )
    return jnp.where(symmetry == 0, relaid.astype(jnp.float32) + cycle / denom, jnp.float32(0.0))


def lane_iota(rows):
    return lax.broadcasted_iota(I32, (rows, 128), 1)


def assemble(dst, blocks, rows, bcol):
    low = lane_iota(MAIN) < 64
    for g in range(GROUPS):
        cols = slice(256 * g, 256 * (g + 1))
        kept = [
            jnp.where(rows[i3] == bcol[g], blocks[GROUPS * i3 + g].astype(F32), 0.0) for i3 in range(PAIRS)
        ]
        for i3 in range(PAIRS):
            dst[MAIN * i3 : MAIN * (i3 + 1), cols] = kept[i3].astype(BF16)
        pieces = []
        for j in range(PAIRS):
            rem = [v[REM * j : REM * (j + 1), 128:256] for v in kept]
            pieces.append(jnp.concatenate(rem + [jnp.zeros((REM, 128), F32)], axis=0))
        left = jnp.where(low, pltpu.roll(pieces[0], 64, 1), pieces[1])
        right = jnp.where(low, pltpu.roll(pieces[2], 64, 1), 0.0)
        dst[MAIN * PAIRS : ROWS, cols] = jnp.concatenate([left, right], axis=1).astype(BF16)


def block_rows(lab, occ):
    main = jnp.broadcast_to(jnp.bitwise_xor(lab[:MAIN], occ), (MAIN, 128))
    rem = jnp.bitwise_xor(lab[MAIN:SLAB], occ)
    rem = jnp.concatenate([rem] * PAIRS + [jnp.full((MAIN - PAIRS * REM, 1), -1, I32)], axis=0)
    right = jnp.where(lane_iota(MAIN) < 64, main, jnp.broadcast_to(rem, (MAIN, 128)))
    return jnp.concatenate([main, right], axis=1)


def exchange_kernel(
    amp_hbm, fac_hbm, vir_irrep_hbm, vir_energy_hbm, occ_irrep_hbm, occ_energy_hbm,
    m_out, inter_out, ff_out, rows_out, cols_out, flag_out,
    amp_v, fac_v, vir_irrep, vir_energy, occ_irrep, occ_energy, pkf, pk, gbuf, bcol, brow, ms, part, cbuf, send, rsbuf, inter_s, flag_s,
    load_sem, zsend, zrecv, xsend, xrecv, csend, crecv, rsend, rrecv, gsend, grecv, fsend, frecv,
):
    t = lax.axis_index("tile")
    r = lax.axis_index("rep")
    x = t // Z
    z = t % Z
    y = r // 2
    core = r % 2
    sibling = (t, 2 * y + 1 - core)

    loads = [pltpu.make_async_copy(amp_hbm.at[j], amp_v.at[j], load_sem.at[j]) for j in range(PAIRS)]
    loads.append(pltpu.make_async_copy(fac_hbm, fac_v, load_sem.at[PAIRS]))
    small = [
        (vir_irrep_hbm, vir_irrep), (vir_energy_hbm, vir_energy),
        (occ_irrep_hbm, occ_irrep), (occ_energy_hbm, occ_energy),
    ]
    small = [pltpu.make_async_copy(a, b, load_sem.at[PAIRS + 1 + n]) for n, (a, b) in enumerate(small)]
    barrier = pltpu.get_barrier_semaphore()

    def z_peer(n):
        near = Z // 2 - (n + 1) // 2
        return (z + jnp.where(n % 2 == 0, near, Z - near)) % Z

    @pl.loop(0, Z - 1)
    def _(n):
        pl.semaphore_signal(barrier, inc=1, device_id=(x * Z + z_peer(n), r))

    for copy in loads[:PAIRS] + small + loads[PAIRS:]:
        copy.start()

    def reducer(d, h):
        return 2 * (2 * ((x + d) % X) + h) + core

    origin = (y // 2 - x + X) % X
    mine_h = y % 2
    chunk = 4 * origin + 2 * core + mine_h

    @pl.loop(0, X)
    def _(d):
        @pl.loop(0, R // 2)
        def _(n):
            @pl.when((d != x) | (n != y))
            def _():
                pl.semaphore_signal(barrier, inc=1, device_id=(d * Z + z, 2 * n + core))

    pl.semaphore_signal(barrier, inc=1, device_id=sibling)

    pkf[...] = jnp.zeros_like(pkf)
    row = lax.broadcasted_iota(I32, (FOLD, 1), 0)
    rem_row = row - MAIN * Z
    target = jnp.where(
        row < MAIN * Z,
        SLAB * (row >> 4) + (row & 15),
        SLAB * (rem_row >> 2) + MAIN + (rem_row & 3),
    )
    lane = lax.broadcasted_iota(I32, (1, X * FOLD), 1)
    folded_lane = lane
    for n in range(1, X):
        folded_lane = folded_lane - jnp.where(lane >= n * FOLD, FOLD, 0)
    pick = jnp.where(target == folded_lane, 1.0, 0.0).astype(BF16)
    for j in range(PAIRS):
        loads[j].wait()
        folded = lax.dot_general(pick, amp_v[j], (((1,), (1,)), ((), ())), preferred_element_type=F32)
        pkf[:, 64 * j : 64 * j + WIDTH] = folded
    for n in range(Z):
        pk[n, :, 0:128] = pkf[MAIN * n : MAIN * (n + 1), 0:128].astype(BF16)
        base = MAIN * Z + REM * n
        rem_rows = [pkf[base : base + REM, 128 * (j // 2) : 128 * (j // 2) + 128] for j in range(PAIRS)]
        rem_rows = [rem_rows[0], pltpu.roll(rem_rows[1], 64, 1), rem_rows[2]]
        rem = jnp.concatenate(rem_rows + [jnp.zeros((MAIN - PAIRS * REM, 128), F32)], axis=0)
        rem = jnp.where(lane_iota(MAIN) < 64, rem, 0.0)
        right = pkf[MAIN * n : MAIN * (n + 1), 128:256] + pltpu.roll(rem, 64, 1)
        pk[n, :, 128:256] = right.astype(BF16)

    pl.semaphore_wait(barrier, Z - 1 + X * (R // 2) - 1 + 1)

    @pl.loop(0, Z - 1)
    def _(n):
        to = z_peer(n)
        pltpu.make_async_remote_copy(
            src_ref=pk.at[to], dst_ref=gbuf.at[x, z], send_sem=zsend, recv_sem=zrecv,
            device_id=(x * Z + to, r),
        ).start()

    gbuf[x, z] = pk[z]

    for copy in small:
        copy.wait()
    vlane = lax.broadcasted_iota(I32, (24, X * FOLD), 1)
    vsub = lax.broadcasted_iota(I32, (24, X * FOLD), 0)
    virs = vir_irrep[...].astype(F32)

    def slab_values(tile, values):
        return jnp.sum(jnp.where(vlane == SLAB * tile + vsub, values, 0.0), axis=1, keepdims=True)

    for n in range(X):
        lab = slab_values(n * Z + z, virs).astype(I32)
        for i3 in range(PAIRS):
            brow[n, i3] = block_rows(lab, occ_irrep[PAIRS * x + i3])
    va_lab = slab_values(t, virs).astype(I32)
    va_en = slab_values(t, vir_energy[...])
    for i in range(OCC):
        n, i3 = i // PAIRS, i % PAIRS
        brow[X + n, i3] = block_rows(va_lab, occ_irrep[i])
        lab = jnp.broadcast_to(jnp.bitwise_xor(va_lab, occ_irrep[i]).astype(F32), (24, 128))
        en = jnp.broadcast_to(occ_energy[i] - va_en, (24, 128))
        rows_out[0, n, MAIN * i3 : MAIN * (i3 + 1), :] = lab[:MAIN]
        rows_out[0, n, MAIN * PAIRS + REM * i3 : MAIN * PAIRS + REM * (i3 + 1), :] = lab[MAIN:SLAB]
        rows_out[1, n, MAIN * i3 : MAIN * (i3 + 1), :] = en[:MAIN]
        rows_out[1, n, MAIN * PAIRS + REM * i3 : MAIN * PAIRS + REM * (i3 + 1), :] = en[MAIN:SLAB]
    for n in range(X):
        rows_out[0, n, ROWS - REM : ROWS, :] = jnp.full((REM, 128), -1.0, F32)
        rows_out[1, n, ROWS - REM : ROWS, :] = jnp.zeros((REM, 128), F32)

    pad = jnp.zeros((8, 1024 - X * FOLD), F32)
    shift = (1024 - WIDTH * r) % 1024
    lane8 = lane_iota(8)
    half = lane8 & 63

    def columns(values):
        whole = jnp.concatenate([jnp.broadcast_to(values, (8, X * FOLD)), pad], axis=1)
        mine = jnp.where(lane8 < WIDTH, pltpu.roll(whole, shift, 1)[:, :128], 0.0)
        return mine + pltpu.roll(mine, 64, 1)

    vb_lab = columns(virs).astype(I32)
    vb_en = columns(vir_energy[...])
    sub16 = lax.broadcasted_iota(I32, (MAIN, 128), 0)
    vb_lab16 = jnp.concatenate([vb_lab, vb_lab], axis=0)
    for g in range(GROUPS):
        for h in range(2):
            first = PAIRS * g + 2 * h
            second = min(first + 1, PAIRS * g + 2)
            cols = slice(256 * g + 128 * h, 256 * g + 128 * h + 128)
            lab = jnp.bitwise_xor(vb_lab, jnp.where(lane8 < 64, occ_irrep[first], occ_irrep[second]))
            lab = jnp.where(half < WIDTH, lab, -2)
            cols_out[0, :, cols] = jnp.where((lane8 < 64) | (h == 0), lab, -2).astype(F32)
            cols_out[1, :, cols] = jnp.where(lane8 < 64, occ_energy[first], occ_energy[second])
            cols_out[2, :, cols] = vb_en
            lab = jnp.concatenate([lab, lab], axis=0)
            if h == 1:
                occ = [occ_irrep[PAIRS * g + j] for j in range(PAIRS)]
                occ = jnp.where(sub16 < REM, occ[0], jnp.where(sub16 < 2 * REM, occ[1], occ[2]))
                rem = jnp.where((lane_iota(MAIN) & 63) < WIDTH, jnp.bitwise_xor(vb_lab16, occ), -2)
                lab = jnp.where(lane_iota(MAIN) < 64, lab, rem)
            bcol[g, :, 128 * h : 128 * h + 128] = lab


    loads[PAIRS].wait()
    zero4 = jnp.zeros((64 - WIDTH, WINDOW), F32)
    for g in range(GROUPS):
        ff_out[256 * g + 192 : 256 * (g + 1), :] = jnp.zeros((64, WINDOW), BF16)
    for k in range(OCC):
        base = 256 * (k // PAIRS) + 64 * (k % PAIRS)
        total = fac_v[k, :, 0:WINDOW].astype(F32)
        for n in range(1, NAUX // WINDOW):
            total = total + fac_v[k, :, WINDOW * n : WINDOW * (n + 1)].astype(F32)
        last = NAUX // WINDOW * WINDOW
        tail = fac_v[k, :, last:NAUX].astype(F32)
        total = total + jnp.concatenate([tail, jnp.zeros((WIDTH, WINDOW - NAUX + last), F32)], axis=1)
        ff_out[base : base + 64, :] = jnp.concatenate([total, zero4], axis=0).astype(BF16)

    vlane8 = lax.broadcasted_iota(I32, (8, X * FOLD), 1)
    vsub8 = lax.broadcasted_iota(I32, (8, X * FOLD), 0)
    first_lab = jnp.sum(
        jnp.where(vlane8 == WIDTH * r + vsub8, virs, 0.0), axis=1, keepdims=True
    ).astype(I32)
    seen = jnp.zeros((8, NAUX), I32)
    for k in range(OCC):
        bit = jnp.left_shift(jnp.int32(1), jnp.bitwise_xor(first_lab, occ_irrep[k]))
        seen = jnp.bitwise_or(seen, jnp.where(fac_v[k, 0:16, :].astype(F32)[0:8] != 0.0, bit, 0))
    for n in (4, 2, 1):
        seen = jnp.bitwise_or(seen, pltpu.roll(seen, n, 0))
    seen = seen[0:1]
    bad = jnp.zeros((1, 1), F32)
    covered = jnp.zeros((1, 1), F32)
    for h in range(8):
        aux_size = jnp.sum(jnp.where(seen == (1 << h), 1.0, 0.0), axis=1, keepdims=True)
        vir_size = jnp.sum(jnp.where(vir_irrep[...] == h, 1.0, 0.0), axis=1, keepdims=True)
        covered = covered + aux_size
        bad = bad + jnp.where(aux_size > WINDOW, 1.0, 0.0) + jnp.where(vir_size > FOLD, 1.0, 0.0)
    bad = bad + jnp.where(covered != NAUX, 1.0, 0.0)
    flag_s[...] = jnp.broadcast_to(jnp.where(bad > 0.0, 1.0, 0.0), (8, 128))

    peers = gbuf.at[x, pl.ds(0, Z - 1)]
    pltpu.make_async_copy(peers, peers, zrecv).wait()
    blocks = [gbuf[x, n] for n in range(Z)]
    cols = [bcol[g] for g in range(GROUPS)]
    for n in range(X):
        assemble(ms.at[pl.ds(ROWS * n, ROWS)], blocks, [brow[n, i3] for i3 in range(PAIRS)], cols)
    sub = lax.broadcasted_iota(I32, (ROWS, WINDOW), 0)
    sums = jnp.dot(ms[...], ff_out[...], preferred_element_type=F32)
    for n in range(X):
        res = sums[ROWS * n : ROWS * (n + 1)]
        res = jnp.where(sub < ROWS - REM, res, flag_s[0:1, 0:1]).astype(BF16)
        part[0, n] = res[: ROWS // 2]
        part[1, n] = res[ROWS // 2 :]

    swap = pltpu.make_async_remote_copy(
        src_ref=part.at[1 - core], dst_ref=cbuf, send_sem=csend, recv_sem=crecv, device_id=sibling
    )
    swap.start()
    swap.wait_recv()
    for n in range(X):
        total = (part[core, n].astype(F32) + cbuf[n].astype(F32)).astype(BF16)
        send[n, 0] = total[:MAIN]
        send[n, 1] = total[MAIN:]

    for n in range(X):
        for h in range(2):
            to = reducer(n, h)

            @pl.when((n != x) | (to != r))
            def _():
                pltpu.make_async_remote_copy(
                    src_ref=send.at[n, h], dst_ref=rsbuf.at[y], send_sem=rsend, recv_sem=rrecv,
                    device_id=(n * Z + z, to),
                ).start()

    for d in (1, 3, 2):
        pltpu.make_async_remote_copy(
            src_ref=gbuf.at[x], dst_ref=gbuf.at[x], send_sem=xsend, recv_sem=xrecv.at[x],
            device_id=(((x + d) % X) * Z + z, r),
        ).start()
    assemble(m_out.at[x], blocks, [brow[X + x, i3] for i3 in range(PAIRS)], cols)

    own = origin == x

    @pl.when(own)
    def _():
        rsbuf[y] = send[x, mine_h]
        rest = rsbuf.at[pl.ds(0, R // 2 - 1)]
        pltpu.make_async_copy(rest, rest, rrecv).wait()
        pltpu.make_async_copy(rest, rest, rsend).wait()

    @pl.when(jnp.logical_not(own))
    def _():
        pltpu.make_async_copy(rsbuf, rsbuf, rrecv).wait()
        pltpu.make_async_copy(rsbuf, rsbuf, rsend).wait()

    total = rsbuf[0].astype(F32)
    for n in range(1, R // 2):
        total = total + rsbuf[n].astype(F32)
    inter_s[chunk] = total.astype(BF16)

    @pl.loop(0, R // 2 - 1)
    def _(n):
        near = (R // 4) - (n + 1) // 2
        to = (y + jnp.where(n % 2 == 0, near, R // 2 - near)) % (R // 2)
        pltpu.make_async_remote_copy(
            src_ref=inter_s.at[chunk], dst_ref=inter_s.at[chunk], send_sem=gsend, recv_sem=grecv.at[y],
            device_id=(t, 2 * to + core),
        ).start()

    def hand_on(slot):
        pltpu.make_async_remote_copy(
            src_ref=inter_s.at[slot], dst_ref=inter_s.at[slot], send_sem=fsend, recv_sem=frecv,
            device_id=sibling,
        ).start()

    hand_on(chunk)

    for d in (1, 3, 2):
        xs = (x + d) % X
        pltpu.make_async_copy(gbuf.at[xs], gbuf.at[xs], xrecv.at[xs]).wait()
        assemble(
            m_out.at[xs], [gbuf[xs, n] for n in range(Z)], [brow[X + xs, i3] for i3 in range(PAIRS)], cols
        )

    @pl.loop(0, R // 2 - 1)
    def _(n):
        near = n // 2 + 1
        source = (y + jnp.where(n % 2 == 0, near, R // 2 - near)) % (R // 2)
        slot = 4 * ((source // 2 - x + X) % X) + 2 * core + source % 2
        pltpu.make_async_copy(inter_s.at[slot], inter_s.at[slot], grecv.at[source]).wait()
        hand_on(slot)

    others = inter_s.at[pl.ds(0, R // 2)]
    pltpu.make_async_copy(others, others, frecv).wait()
    inter_out[...] = inter_s[...]
    flag_out[0] = jnp.max(inter_s[3].astype(F32)[15:16, 0:128])

    sent = pk.at[pl.ds(0, Z - 1)]
    pltpu.make_async_copy(sent, sent, zsend).wait()
    sent = gbuf.at[pl.ds(0, X - 1)]
    pltpu.make_async_copy(sent, sent, xsend).wait()
    swap.wait_send()
    sent = inter_s.at[pl.ds(0, R // 2 - 1)]
    pltpu.make_async_copy(sent, sent, gsend).wait()
    pltpu.make_async_copy(others, others, fsend).wait()


def exchange(amplitudes, occ_energy, vir_energy, occ_irrep, vir_irrep, factors):
    hbm = pl.BlockSpec(memory_space=pl.ANY)
    smem = pl.BlockSpec(memory_space=pltpu.SMEM)
    shapes = [
        ((X, ROWS, COLS), BF16),
        ((R, MAIN, WINDOW), BF16),
        ((COLS, WINDOW), BF16),
        ((2, X, ROWS, 128), F32),
        ((3, 8, COLS), F32),
    ]
    dma = pltpu.SemaphoreType.DMA
    return pl.pallas_call(
        exchange_kernel,
        out_shape=[pltpu.VMEM(*s) for s in shapes] + [pltpu.SMEM((1,), F32)],
        in_specs=[hbm] * 6,
        out_specs=[pl.BlockSpec(memory_space=pltpu.VMEM)] * 5 + [smem],
        scratch_shapes=[
            pltpu.VMEM((PAIRS, WIDTH, X * FOLD), BF16),
            pltpu.VMEM((OCC, WIDTH, NAUX), BF16),
            pltpu.VMEM((1, X * FOLD), I32),
            pltpu.VMEM((1, X * FOLD), F32),
            pltpu.SMEM((OCC,), I32),
            pltpu.SMEM((OCC,), F32),
            pltpu.VMEM((FOLD, 256), F32),
            pltpu.VMEM((Z, MAIN, 256), BF16),
            pltpu.VMEM((X, Z, MAIN, 256), BF16),
            pltpu.VMEM((GROUPS, MAIN, 256), I32),
            pltpu.VMEM((2 * X, PAIRS, MAIN, 256), I32),
            pltpu.VMEM((X * ROWS, COLS), BF16),
            pltpu.VMEM((2, X, ROWS // 2, WINDOW), BF16),
            pltpu.VMEM((X, ROWS // 2, WINDOW), BF16),
            pltpu.VMEM((X, 2, MAIN, WINDOW), BF16),
            pltpu.VMEM((R // 2, MAIN, WINDOW), BF16),
            pltpu.VMEM((R, MAIN, WINDOW), BF16),
            pltpu.VMEM((8, 128), F32),
            dma((PAIRS + 5,)), dma, dma, dma, dma((X,)), dma, dma, dma, dma, dma, dma((R // 2,)), dma, dma,
        ],
        compiler_params=pltpu.CompilerParams(
            collective_id=0, has_side_effects=True, vmem_limit_bytes=24 * 1024 * 1024
        ),
        name="exchange",
    )(
        amplitudes.transpose(0, 2, 1), factors, vir_irrep.reshape(1, -1), vir_energy.reshape(1, -1),
        occ_irrep, occ_energy,
    )


def finish_kernel(m_ref, inter_ref, ff_ref, rows_ref, cols_ref, out_hbm, out, res, sem):
    inter = inter_ref[...].reshape(X * ROWS, WINDOW)
    whole = lax.dot_general(inter, ff_ref[...], (((1,), (1,)), ((), ())), preferred_element_type=F32)
    for n in range(X):
        cycle = whole[ROWS * n : ROWS * (n + 1)]
        rlab = jnp.concatenate([rows_ref[0, n]] * 2, axis=1)
        ren = jnp.concatenate([rows_ref[1, n]] * 2, axis=1)
        for g in range(GROUPS):
            cols = slice(256 * g, 256 * (g + 1))
            denom = ren + cols_ref[1, 0:1, cols] - cols_ref[2, 0:1, cols]
            value = m_ref[n, :, cols].astype(F32) + cycle[:, cols] / denom
            res[:, cols] = jnp.where(rlab == cols_ref[0, 0:1, cols], value, 0.0)
        for i3 in range(PAIRS):
            i = PAIRS * n + i3
            for j in range(OCC):
                base = 256 * (j // PAIRS) + 64 * (j % PAIRS)
                out[i, j, 0:MAIN, :] = res[MAIN * i3 : MAIN * (i3 + 1), base : base + WIDTH]
                rem = MAIN * PAIRS + REM * i3
                out[i, j, MAIN:SLAB, :] = res[rem : rem + REM, base : base + WIDTH]
        done = pl.ds(PAIRS * n, PAIRS)
        pltpu.make_async_copy(out.at[done], out_hbm.at[done], sem.at[n]).start()
    for n in range(X):
        done = pl.ds(PAIRS * n, PAIRS)
        pltpu.make_async_copy(out.at[done], out_hbm.at[done], sem.at[n]).wait()


def finish(*operands):
    vmem = pl.BlockSpec(memory_space=pltpu.VMEM)
    out = pl.pallas_call(
        finish_kernel,
        out_shape=pltpu.HBM((OCC, OCC, SLAB, WIDTH), F32),
        in_specs=[vmem] * 5,
        out_specs=pl.BlockSpec(memory_space=pltpu.HBM),
        scratch_shapes=[
            pltpu.VMEM((OCC, OCC, SLAB, WIDTH), F32),
            pltpu.VMEM((ROWS, COLS), F32),
            pltpu.SemaphoreType.DMA((X,)),
        ],
        compiler_params=pltpu.CompilerParams(vmem_limit_bytes=24 * 1024 * 1024),
        name="finish",
    )(*operands)
    return out.transpose(0, 2, 1, 3)


def per_device(*arguments):
    *operands, flag = exchange(*arguments)
    return lax.cond(flag[0] == 0.0, lambda: finish(*operands), lambda: dense_path(*arguments))


def solution(mesh):
    return jax.shard_map(
        per_device,
        mesh=mesh,
        in_specs=(P("tile", None, "rep"), P(), P(), P(), P(), P(None, "rep", None)),
        out_specs=P(None, "tile", None, "rep"),
        check_vma=False,
    )
```

```python
import functools

import jax
import jax.numpy as jnp
from jax import lax
from jax.experimental import pallas as pl
from jax.experimental.pallas import tpu as pltpu
from jax.sharding import PartitionSpec as P

X, Z, R = 4, 12, 16
OCC = 12
SLAB = 20
WIDTH = 60
PAIRS = 3
GROUPS = 4
FOLD = SLAB * Z
NAUX = 2048
WINDOW = 384
COLS = GROUPS * 256
ROWS = 64
MAIN = 16
REM = SLAB - MAIN
F32, BF16, I32 = jnp.float32, jnp.bfloat16, jnp.int32


def sum_over_rep(partial_value):
    count = lax.axis_size("rep")
    blocks = partial_value.reshape(count, -1, partial_value.shape[1])
    blocks = lax.all_to_all(blocks, "rep", split_axis=0, concat_axis=0, tiled=True)
    total = jnp.sum(blocks.astype(jnp.float32), axis=0).astype(jnp.bfloat16)
    total = jnp.broadcast_to(total[None], blocks.shape)
    total = lax.all_to_all(total, "rep", split_axis=0, concat_axis=0, tiled=True)
    return total.reshape(partial_value.shape)


def dense_path(amplitudes, occ_energy, vir_energy, occ_irrep, vir_irrep, factors):
    tile_count = lax.axis_size("tile")
    occ_count = occ_energy.shape[0]
    vir_count = vir_energy.shape[0]
    first_width = vir_count // tile_count
    second_width = amplitudes.shape[2]
    relaid = lax.all_to_all(amplitudes, "tile", split_axis=1, concat_axis=0, tiled=True)
    relaid = relaid.reshape(occ_count, occ_count, first_width, second_width).transpose(0, 2, 1, 3)
    matrix = relaid.reshape(occ_count * first_width, occ_count * second_width)
    factor_rows = factors.reshape(occ_count * second_width, factors.shape[2])
    partial_value = jnp.dot(matrix, factor_rows, preferred_element_type=jnp.float32)
    inter = sum_over_rep(partial_value.astype(jnp.bfloat16))
    cycle = jnp.einsum("mq,nq->mn", inter, factor_rows, preferred_element_type=jnp.float32)
    cycle = cycle.reshape(occ_count, first_width, occ_count, second_width)
    tile_start = lax.axis_index("tile") * first_width
    rep_start = lax.axis_index("rep") * second_width
    vir_first = lax.dynamic_slice_in_dim(vir_energy, tile_start, first_width)
    vir_second = lax.dynamic_slice_in_dim(vir_energy, rep_start, second_width)
    irrep_first = lax.dynamic_slice_in_dim(vir_irrep, tile_start, first_width)
    irrep_second = lax.dynamic_slice_in_dim(vir_irrep, rep_start, second_width)
    denom = (
        occ_energy[:, None, None, None]
        - vir_first[None, :, None, None]
        + occ_energy[None, None, :, None]
        - vir_second[None, None, None, :]
    )
    symmetry = jnp.bitwise_xor(
        jnp.bitwise_xor(occ_irrep[:, None, None, None], irrep_first[None, :, None, None]),
        jnp.bitwise_xor(occ_irrep[None, None, :, None], irrep_second[None, None, None, :]),
    )
    return jnp.where(symmetry == 0, relaid.astype(jnp.float32) + cycle / denom, jnp.float32(0.0))


def lane_iota(rows):
    return lax.broadcasted_iota(I32, (rows, 128), 1)


def assemble(dst, blocks, rows, bcol):
    low = lane_iota(MAIN) < 64
    for g in range(GROUPS):
        cols = slice(256 * g, 256 * (g + 1))
        kept = [
            jnp.where(rows[i3] == bcol[g], blocks[GROUPS * i3 + g].astype(F32), 0.0) for i3 in range(PAIRS)
        ]
        for i3 in range(PAIRS):
            dst[MAIN * i3 : MAIN * (i3 + 1), cols] = kept[i3].astype(BF16)
        pieces = []
        for j in range(PAIRS):
            rem = [v[REM * j : REM * (j + 1), 128:256] for v in kept]
            pieces.append(jnp.concatenate(rem + [jnp.zeros((REM, 128), F32)], axis=0))
        left = jnp.where(low, pltpu.roll(pieces[0], 64, 1), pieces[1])
        right = jnp.where(low, pltpu.roll(pieces[2], 64, 1), 0.0)
        dst[MAIN * PAIRS : ROWS, cols] = jnp.concatenate([left, right], axis=1).astype(BF16)


def block_rows(lab, occ):
    main = jnp.broadcast_to(jnp.bitwise_xor(lab[:MAIN], occ), (MAIN, 128))
    rem = jnp.bitwise_xor(lab[MAIN:SLAB], occ)
    rem = jnp.concatenate([rem] * PAIRS + [jnp.full((MAIN - PAIRS * REM, 1), -1, I32)], axis=0)
    right = jnp.where(lane_iota(MAIN) < 64, main, jnp.broadcast_to(rem, (MAIN, 128)))
    return jnp.concatenate([main, right], axis=1)


def exchange_kernel(
    amp_hbm, fac_hbm, vir_irrep_hbm, vir_energy_hbm, occ_irrep_hbm, occ_energy_hbm,
    m_out, inter_out, ff_out, rows_out, cols_out, flag_out,
    amp_v, fac_v, vir_irrep, vir_energy, occ_irrep, occ_energy, pkf, pk, gbuf, bcol, brow, ms, part, cbuf, send, rsbuf, inter_s, flag_s,
    load_sem, zsend, zrecv, xsend, xrecv, csend, crecv, rsend, rrecv, gsend, grecv, fsend, frecv,
):
    t = lax.axis_index("tile")
    r = lax.axis_index("rep")
    x = t // Z
    z = t % Z
    y = r // 2
    core = r % 2
    sibling = (t, 2 * y + 1 - core)

    loads = [pltpu.make_async_copy(amp_hbm.at[j], amp_v.at[j], load_sem.at[j]) for j in range(PAIRS)]
    loads.append(pltpu.make_async_copy(fac_hbm, fac_v, load_sem.at[PAIRS]))
    small = [
        (vir_irrep_hbm, vir_irrep), (vir_energy_hbm, vir_energy),
        (occ_irrep_hbm, occ_irrep), (occ_energy_hbm, occ_energy),
    ]
    small = [pltpu.make_async_copy(a, b, load_sem.at[PAIRS + 1 + n]) for n, (a, b) in enumerate(small)]
    barrier = pltpu.get_barrier_semaphore()

    def z_peer(n):
        near = Z // 2 - (n + 1) // 2
        return (z + jnp.where(n % 2 == 0, near, Z - near)) % Z

    @pl.loop(0, Z - 1)
    def _(n):
        pl.semaphore_signal(barrier, inc=1, device_id=(x * Z + z_peer(n), r))

    for copy in loads[:PAIRS] + small + loads[PAIRS:]:
        copy.start()

    def reducer(d, h):
        return 2 * (2 * ((x + d) % X) + h) + core

    origin = (y // 2 - x + X) % X
    mine_h = y % 2
    chunk = 4 * origin + 2 * core + mine_h

    @pl.loop(0, X)
    def _(d):
        @pl.loop(0, R // 2)
        def _(n):
            @pl.when((d != x) | (n != y))
            def _():
                pl.semaphore_signal(barrier, inc=1, device_id=(d * Z + z, 2 * n + core))

    pl.semaphore_signal(barrier, inc=1, device_id=sibling)

    pkf[...] = jnp.zeros_like(pkf)
    row = lax.broadcasted_iota(I32, (FOLD, 1), 0)
    rem_row = row - MAIN * Z
    target = jnp.where(
        row < MAIN * Z,
        SLAB * (row >> 4) + (row & 15),
        SLAB * (rem_row >> 2) + MAIN + (rem_row & 3),
    )
    lane = lax.broadcasted_iota(I32, (1, X * FOLD), 1)
    folded_lane = lane
    for n in range(1, X):
        folded_lane = folded_lane - jnp.where(lane >= n * FOLD, FOLD, 0)
    pick = jnp.where(target == folded_lane, 1.0, 0.0).astype(BF16)
    for j in range(PAIRS):
        loads[j].wait()
        folded = lax.dot_general(pick, amp_v[j], (((1,), (1,)), ((), ())), preferred_element_type=F32)
        pkf[:, 64 * j : 64 * j + WIDTH] = folded
    for n in range(Z):
        pk[n, :, 0:128] = pkf[MAIN * n : MAIN * (n + 1), 0:128].astype(BF16)
        base = MAIN * Z + REM * n
        rem_rows = [pkf[base : base + REM, 128 * (j // 2) : 128 * (j // 2) + 128] for j in range(PAIRS)]
        rem_rows = [rem_rows[0], pltpu.roll(rem_rows[1], 64, 1), rem_rows[2]]
        rem = jnp.concatenate(rem_rows + [jnp.zeros((MAIN - PAIRS * REM, 128), F32)], axis=0)
        rem = jnp.where(lane_iota(MAIN) < 64, rem, 0.0)
        right = pkf[MAIN * n : MAIN * (n + 1), 128:256] + pltpu.roll(rem, 64, 1)
        pk[n, :, 128:256] = right.astype(BF16)

    pl.semaphore_wait(barrier, Z - 1 + X * (R // 2) - 1 + 1)

    @pl.loop(0, Z - 1)
    def _(n):
        to = z_peer(n)
        pltpu.make_async_remote_copy(
            src_ref=pk.at[to], dst_ref=gbuf.at[x, z], send_sem=zsend, recv_sem=zrecv,
            device_id=(x * Z + to, r),
        ).start()

    gbuf[x, z] = pk[z]

    for copy in small:
        copy.wait()
    vlane = lax.broadcasted_iota(I32, (24, X * FOLD), 1)
    vsub = lax.broadcasted_iota(I32, (24, X * FOLD), 0)
    virs = vir_irrep[...].astype(F32)

    def slab_values(tile, values):
        return jnp.sum(jnp.where(vlane == SLAB * tile + vsub, values, 0.0), axis=1, keepdims=True)

    for n in range(X):
        lab = slab_values(n * Z + z, virs).astype(I32)
        for i3 in range(PAIRS):
            brow[n, i3] = block_rows(lab, occ_irrep[PAIRS * x + i3])
    va_lab = slab_values(t, virs).astype(I32)
    va_en = slab_values(t, vir_energy[...])
    for i in range(OCC):
        n, i3 = i // PAIRS, i % PAIRS
        brow[X + n, i3] = block_rows(va_lab, occ_irrep[i])
        lab = jnp.broadcast_to(jnp.bitwise_xor(va_lab, occ_irrep[i]).astype(F32), (24, 128))
        en = jnp.broadcast_to(occ_energy[i] - va_en, (24, 128))
        rows_out[0, n, MAIN * i3 : MAIN * (i3 + 1), :] = lab[:MAIN]
        rows_out[0, n, MAIN * PAIRS + REM * i3 : MAIN * PAIRS + REM * (i3 + 1), :] = lab[MAIN:SLAB]
        rows_out[1, n, MAIN * i3 : MAIN * (i3 + 1), :] = en[:MAIN]
        rows_out[1, n, MAIN * PAIRS + REM * i3 : MAIN * PAIRS + REM * (i3 + 1), :] = en[MAIN:SLAB]
    for n in range(X):
        rows_out[0, n, ROWS - REM : ROWS, :] = jnp.full((REM, 128), -1.0, F32)
        rows_out[1, n, ROWS - REM : ROWS, :] = jnp.zeros((REM, 128), F32)

    pad = jnp.zeros((8, 1024 - X * FOLD), F32)
    shift = (1024 - WIDTH * r) % 1024
    lane8 = lane_iota(8)
    half = lane8 & 63

    def columns(values):
        whole = jnp.concatenate([jnp.broadcast_to(values, (8, X * FOLD)), pad], axis=1)
        mine = jnp.where(lane8 < WIDTH, pltpu.roll(whole, shift, 1)[:, :128], 0.0)
        return mine + pltpu.roll(mine, 64, 1)

    vb_lab = columns(virs).astype(I32)
    vb_en = columns(vir_energy[...])
    sub16 = lax.broadcasted_iota(I32, (MAIN, 128), 0)
    vb_lab16 = jnp.concatenate([vb_lab, vb_lab], axis=0)
    for g in range(GROUPS):
        for h in range(2):
            first = PAIRS * g + 2 * h
            second = min(first + 1, PAIRS * g + 2)
            cols = slice(256 * g + 128 * h, 256 * g + 128 * h + 128)
            lab = jnp.bitwise_xor(vb_lab, jnp.where(lane8 < 64, occ_irrep[first], occ_irrep[second]))
            lab = jnp.where(half < WIDTH, lab, -2)
            cols_out[0, :, cols] = jnp.where((lane8 < 64) | (h == 0), lab, -2).astype(F32)
            cols_out[1, :, cols] = jnp.where(lane8 < 64, occ_energy[first], occ_energy[second])
            cols_out[2, :, cols] = vb_en
            lab = jnp.concatenate([lab, lab], axis=0)
            if h == 1:
                occ = [occ_irrep[PAIRS * g + j] for j in range(PAIRS)]
                occ = jnp.where(sub16 < REM, occ[0], jnp.where(sub16 < 2 * REM, occ[1], occ[2]))
                rem = jnp.where((lane_iota(MAIN) & 63) < WIDTH, jnp.bitwise_xor(vb_lab16, occ), -2)
                lab = jnp.where(lane_iota(MAIN) < 64, lab, rem)
            bcol[g, :, 128 * h : 128 * h + 128] = lab


    loads[PAIRS].wait()
    zero4 = jnp.zeros((64 - WIDTH, WINDOW), F32)
    for g in range(GROUPS):
        ff_out[256 * g + 192 : 256 * (g + 1), :] = jnp.zeros((64, WINDOW), BF16)
    for k in range(OCC):
        base = 256 * (k // PAIRS) + 64 * (k % PAIRS)
        total = fac_v[k, :, 0:WINDOW].astype(F32)
        for n in range(1, NAUX // WINDOW):
            total = total + fac_v[k, :, WINDOW * n : WINDOW * (n + 1)].astype(F32)
        last = NAUX // WINDOW * WINDOW
        tail = fac_v[k, :, last:NAUX].astype(F32)
        total = total + jnp.concatenate([tail, jnp.zeros((WIDTH, WINDOW - NAUX + last), F32)], axis=1)
        ff_out[base : base + 64, :] = jnp.concatenate([total, zero4], axis=0).astype(BF16)

    vlane8 = lax.broadcasted_iota(I32, (8, X * FOLD), 1)
    vsub8 = lax.broadcasted_iota(I32, (8, X * FOLD), 0)
    first_lab = jnp.sum(
        jnp.where(vlane8 == WIDTH * r + vsub8, virs, 0.0), axis=1, keepdims=True
    ).astype(I32)
    seen = jnp.zeros((8, NAUX), I32)
    for k in range(OCC):
        bit = jnp.left_shift(jnp.int32(1), jnp.bitwise_xor(first_lab, occ_irrep[k]))
        seen = jnp.bitwise_or(seen, jnp.where(fac_v[k, 0:16, :].astype(F32)[0:8] != 0.0, bit, 0))
    for n in (4, 2, 1):
        seen = jnp.bitwise_or(seen, pltpu.roll(seen, n, 0))
    seen = seen[0:1]
    bad = jnp.zeros((1, 1), F32)
    covered = jnp.zeros((1, 1), F32)
    for h in range(8):
        aux_size = jnp.sum(jnp.where(seen == (1 << h), 1.0, 0.0), axis=1, keepdims=True)
        vir_size = jnp.sum(jnp.where(vir_irrep[...] == h, 1.0, 0.0), axis=1, keepdims=True)
        covered = covered + aux_size
        bad = bad + jnp.where(aux_size > WINDOW, 1.0, 0.0) + jnp.where(vir_size > FOLD, 1.0, 0.0)
    bad = bad + jnp.where(covered != NAUX, 1.0, 0.0)
    flag_s[...] = jnp.broadcast_to(jnp.where(bad > 0.0, 1.0, 0.0), (8, 128))

    peers = gbuf.at[x, pl.ds(0, Z - 1)]
    pltpu.make_async_copy(peers, peers, zrecv).wait()
    blocks = [gbuf[x, n] for n in range(Z)]
    cols = [bcol[g] for g in range(GROUPS)]
    for n in range(X):
        assemble(ms.at[pl.ds(ROWS * n, ROWS)], blocks, [brow[n, i3] for i3 in range(PAIRS)], cols)
    sub = lax.broadcasted_iota(I32, (ROWS, WINDOW), 0)
    sums = jnp.dot(ms[...], ff_out[...], preferred_element_type=F32)
    for n in range(X):
        res = sums[ROWS * n : ROWS * (n + 1)]
        res = jnp.where(sub < ROWS - REM, res, flag_s[0:1, 0:1]).astype(BF16)
        part[0, n] = res[: ROWS // 2]
        part[1, n] = res[ROWS // 2 :]

    swap = pltpu.make_async_remote_copy(
        src_ref=part.at[1 - core], dst_ref=cbuf, send_sem=csend, recv_sem=crecv, device_id=sibling
    )
    swap.start()
    swap.wait_recv()
    for n in range(X):
        total = (part[core, n].astype(F32) + cbuf[n].astype(F32)).astype(BF16)
        send[n, 0] = total[:MAIN]
        send[n, 1] = total[MAIN:]

    for d in (2, 1, 3, 0):
        n = (x + d) % X
        for h in range(2):
            to = reducer(n, h)

            @pl.when((n != x) | (to != r))
            def _():
                pltpu.make_async_remote_copy(
                    src_ref=send.at[n, h], dst_ref=rsbuf.at[y], send_sem=rsend, recv_sem=rrecv,
                    device_id=(n * Z + z, to),
                ).start()

    for d in (1, 3, 2):
        pltpu.make_async_remote_copy(
            src_ref=gbuf.at[x], dst_ref=gbuf.at[x], send_sem=xsend, recv_sem=xrecv.at[x],
            device_id=(((x + d) % X) * Z + z, r),
        ).start()
    assemble(m_out.at[x], blocks, [brow[X + x, i3] for i3 in range(PAIRS)], cols)

    own = origin == x

    @pl.when(own)
    def _():
        rsbuf[y] = send[x, mine_h]
        rest = rsbuf.at[pl.ds(0, R // 2 - 1)]
        pltpu.make_async_copy(rest, rest, rrecv).wait()
        pltpu.make_async_copy(rest, rest, rsend).wait()

    @pl.when(jnp.logical_not(own))
    def _():
        pltpu.make_async_copy(rsbuf, rsbuf, rrecv).wait()
        pltpu.make_async_copy(rsbuf, rsbuf, rsend).wait()

    total = rsbuf[0].astype(F32)
    for n in range(1, R // 2):
        total = total + rsbuf[n].astype(F32)
    inter_s[chunk] = total.astype(BF16)

    @pl.loop(0, R // 2 - 1)
    def _(n):
        near = (R // 4) - (n + 1) // 2
        to = (y + jnp.where(n % 2 == 0, near, R // 2 - near)) % (R // 2)
        pltpu.make_async_remote_copy(
            src_ref=inter_s.at[chunk], dst_ref=inter_s.at[chunk], send_sem=gsend, recv_sem=grecv.at[y],
            device_id=(t, 2 * to + core),
        ).start()

    def hand_on(slot):
        pltpu.make_async_remote_copy(
            src_ref=inter_s.at[slot], dst_ref=inter_s.at[slot], send_sem=fsend, recv_sem=frecv,
            device_id=sibling,
        ).start()

    hand_on(chunk)

    for d in (1, 3, 2):
        xs = (x + d) % X
        pltpu.make_async_copy(gbuf.at[xs], gbuf.at[xs], xrecv.at[xs]).wait()
        assemble(
            m_out.at[xs], [gbuf[xs, n] for n in range(Z)], [brow[X + xs, i3] for i3 in range(PAIRS)], cols
        )

    @pl.loop(0, R // 2 - 1)
    def _(n):
        near = n // 2 + 1
        source = (y + jnp.where(n % 2 == 0, near, R // 2 - near)) % (R // 2)
        slot = 4 * ((source // 2 - x + X) % X) + 2 * core + source % 2
        pltpu.make_async_copy(inter_s.at[slot], inter_s.at[slot], grecv.at[source]).wait()
        hand_on(slot)

    others = inter_s.at[pl.ds(0, R // 2)]
    pltpu.make_async_copy(others, others, frecv).wait()
    inter_out[...] = inter_s[...]
    flag_out[0] = jnp.max(inter_s[3].astype(F32)[15:16, 0:128])

    sent = pk.at[pl.ds(0, Z - 1)]
    pltpu.make_async_copy(sent, sent, zsend).wait()
    sent = gbuf.at[pl.ds(0, X - 1)]
    pltpu.make_async_copy(sent, sent, xsend).wait()
    swap.wait_send()
    sent = inter_s.at[pl.ds(0, R // 2 - 1)]
    pltpu.make_async_copy(sent, sent, gsend).wait()
    pltpu.make_async_copy(others, others, fsend).wait()


def exchange(amplitudes, occ_energy, vir_energy, occ_irrep, vir_irrep, factors):
    hbm = pl.BlockSpec(memory_space=pl.ANY)
    smem = pl.BlockSpec(memory_space=pltpu.SMEM)
    shapes = [
        ((X, ROWS, COLS), BF16),
        ((R, MAIN, WINDOW), BF16),
        ((COLS, WINDOW), BF16),
        ((2, X, ROWS, 128), F32),
        ((3, 8, COLS), F32),
    ]
    dma = pltpu.SemaphoreType.DMA
    return pl.pallas_call(
        exchange_kernel,
        out_shape=[pltpu.VMEM(*s) for s in shapes] + [pltpu.SMEM((1,), F32)],
        in_specs=[hbm] * 6,
        out_specs=[pl.BlockSpec(memory_space=pltpu.VMEM)] * 5 + [smem],
        scratch_shapes=[
            pltpu.VMEM((PAIRS, WIDTH, X * FOLD), BF16),
            pltpu.VMEM((OCC, WIDTH, NAUX), BF16),
            pltpu.VMEM((1, X * FOLD), I32),
            pltpu.VMEM((1, X * FOLD), F32),
            pltpu.SMEM((OCC,), I32),
            pltpu.SMEM((OCC,), F32),
            pltpu.VMEM((FOLD, 256), F32),
            pltpu.VMEM((Z, MAIN, 256), BF16),
            pltpu.VMEM((X, Z, MAIN, 256), BF16),
            pltpu.VMEM((GROUPS, MAIN, 256), I32),
            pltpu.VMEM((2 * X, PAIRS, MAIN, 256), I32),
            pltpu.VMEM((X * ROWS, COLS), BF16),
            pltpu.VMEM((2, X, ROWS // 2, WINDOW), BF16),
            pltpu.VMEM((X, ROWS // 2, WINDOW), BF16),
            pltpu.VMEM((X, 2, MAIN, WINDOW), BF16),
            pltpu.VMEM((R // 2, MAIN, WINDOW), BF16),
            pltpu.VMEM((R, MAIN, WINDOW), BF16),
            pltpu.VMEM((8, 128), F32),
            dma((PAIRS + 5,)), dma, dma, dma, dma((X,)), dma, dma, dma, dma, dma, dma((R // 2,)), dma, dma,
        ],
        compiler_params=pltpu.CompilerParams(
            collective_id=0, has_side_effects=True, vmem_limit_bytes=24 * 1024 * 1024
        ),
        name="exchange",
    )(
        amplitudes.transpose(0, 2, 1), factors, vir_irrep.reshape(1, -1), vir_energy.reshape(1, -1),
        occ_irrep, occ_energy,
    )


def finish_kernel(m_ref, inter_ref, ff_ref, rows_ref, cols_ref, out_hbm, out, res, sem):
    inter = inter_ref[...].reshape(X * ROWS, WINDOW)
    whole = lax.dot_general(inter, ff_ref[...], (((1,), (1,)), ((), ())), preferred_element_type=F32)
    for n in range(X):
        cycle = whole[ROWS * n : ROWS * (n + 1)]
        rlab = jnp.concatenate([rows_ref[0, n]] * 2, axis=1)
        ren = jnp.concatenate([rows_ref[1, n]] * 2, axis=1)
        for g in range(GROUPS):
            cols = slice(256 * g, 256 * (g + 1))
            denom = ren + cols_ref[1, 0:1, cols] - cols_ref[2, 0:1, cols]
            value = m_ref[n, :, cols].astype(F32) + cycle[:, cols] / denom
            res[:, cols] = jnp.where(rlab == cols_ref[0, 0:1, cols], value, 0.0)
        for i3 in range(PAIRS):
            i = PAIRS * n + i3
            for j in range(OCC):
                base = 256 * (j // PAIRS) + 64 * (j % PAIRS)
                out[i, j, 0:MAIN, :] = res[MAIN * i3 : MAIN * (i3 + 1), base : base + WIDTH]
                rem = MAIN * PAIRS + REM * i3
                out[i, j, MAIN:SLAB, :] = res[rem : rem + REM, base : base + WIDTH]
        done = pl.ds(PAIRS * n, PAIRS)
        pltpu.make_async_copy(out.at[done], out_hbm.at[done], sem.at[n]).start()
    for n in range(X):
        done = pl.ds(PAIRS * n, PAIRS)
        pltpu.make_async_copy(out.at[done], out_hbm.at[done], sem.at[n]).wait()


def finish(*operands):
    vmem = pl.BlockSpec(memory_space=pltpu.VMEM)
    out = pl.pallas_call(
        finish_kernel,
        out_shape=pltpu.HBM((OCC, OCC, SLAB, WIDTH), F32),
        in_specs=[vmem] * 5,
        out_specs=pl.BlockSpec(memory_space=pltpu.HBM),
        scratch_shapes=[
            pltpu.VMEM((OCC, OCC, SLAB, WIDTH), F32),
            pltpu.VMEM((ROWS, COLS), F32),
            pltpu.SemaphoreType.DMA((X,)),
        ],
        compiler_params=pltpu.CompilerParams(vmem_limit_bytes=24 * 1024 * 1024),
        name="finish",
    )(*operands)
    return out.transpose(0, 2, 1, 3)


def per_device(*arguments):
    *operands, flag = exchange(*arguments)
    return lax.cond(flag[0] == 0.0, lambda: finish(*operands), lambda: dense_path(*arguments))


def solution(mesh):
    return jax.shard_map(
        per_device,
        mesh=mesh,
        in_specs=(P("tile", None, "rep"), P(), P(), P(), P(), P(None, "rep", None)),
        out_specs=P(None, "tile", None, "rep"),
        check_vma=False,
    )
```
